32 devices in a mesh: grid: 8 (over z, y), lev: 4 (over x, core).
Axes of the slice: x: 2, y: 2, z: 4, core: 2. Of those that a mesh axis runs over, the one named last changes fastest.
Arguments:
- prior_fields: float32 [128, 8, 4096], P('grid', 'lev'), may hold values from -6 to 6
- channel_weights: float32 [8, 4], P('lev'), may hold values from 0.1 to 1
- obs_owner: int32 [4], replicated, may hold values from 0 to 7
- obs_offset: int32 [4, 4, 64], replicated, may hold values from 0 to 511
- obs_value: float32 [4, 4, 64], P(None, 'lev'), may hold values from -30 to 30
- obs_error: float32 [4, 4, 64], P(None, 'lev'), may hold values from 0.5 to 2
- ancestors: int32 [4, 4, 8, 128], P(None, 'lev', 'grid'), may hold values from 0 to 127
Outputs:
- posterior_fields: float32 [128, 8, 4096], P('grid', 'lev')
The draws below stay inside these ranges and needn't reach their ends.
All inputs are finite; a program needn't handle non-finite values.
Results may differ from the reference program's by a relative error of at most 0.0003.
Values sent between devices are 32-bit elements; how exact they have to be, the bound alone decides.
No kernel may reach another device: no remote copies, remote signals or barrier semaphores. Data moves between devices by JAX's collectives and lax.ppermute only.
A program may use at most 128 MiB of HBM per device.

```python
import math
import jax
import jax.numpy as jnp
from jax import lax

M = 128
CELLS_DEV = 512
OBS = 64
NB = 4
BLOCKS = 8
GROUPS = 4
LEVELS = 8
CELLS = 4096
REGIONS = 8
N_GRID = 8


def draw_obs_value(key, part):
    base = jax.random.normal(key, (NB, GROUPS, OBS), jnp.float32)
    return jnp.clip(1.5 * base, -30.0, 30.0)


def with_ends(values, stream_key, smallest, largest):
    extent = values.shape
    place = [jax.random.randint(jax.random.fold_in(stream_key, axis), (), 0, extent[axis]) for axis in range(len(extent))]
    values = values.at[tuple(place)].set(smallest)
    longest = extent.index(max(extent))
    place[longest] = (place[longest] + 1) % extent[longest]
    return values.at[tuple(place)].set(largest)


def block_levels(stream_key, dims, shards, smallest, high):
    gain = 1.0
    for position, blocks in shards:
        draws = jax.random.uniform(jax.random.fold_in(jax.random.fold_in(stream_key, 6), position), (blocks,), jnp.float32, smallest / len(shards), high / len(shards))
        gain = gain * jnp.repeat(jnp.exp(draws), dims[position] // blocks).reshape((-1,) + (1,) * (len(dims) - 1 - position))
    return gain


def noise(key, extent, deviation, most, cuts=(), held_as=jnp.bfloat16):
    result = deviation * jax.random.normal(key, extent, jnp.float32)
    if cuts:
        result = result * block_levels(key, extent, cuts, -0.22, 0.18)
    return jnp.clip(result, -most, most).astype(held_as)


def setup_inputs(seed: int = 0) -> dict:
    streams_of = jax.random.split(jax.random.key(seed), 8)
    prior_fields = noise(streams_of[0], (M, LEVELS, CELLS), 1.0, 6.0, ((0, 8), (1, 4)), jnp.float32)
    channel_weights = jnp.clip(0.1 + 0.9 * jax.random.uniform(streams_of[1], (LEVELS, GROUPS), jnp.float32) ** block_levels(streams_of[1], (LEVELS, GROUPS), ((0, 4),), -0.2, 0.2), 0.1, 1.0)
    obs_owner = with_ends(jax.random.randint(streams_of[2], (NB,), 0, BLOCKS), jax.random.fold_in(streams_of[2], 1), 0, BLOCKS - 1).astype(jnp.int32)
    obs_offset = with_ends(jax.random.randint(streams_of[3], (NB, GROUPS, OBS), 0, CELLS_DEV), jax.random.fold_in(streams_of[3], 1), 0, CELLS_DEV - 1).astype(jnp.int32)
    obs_value = draw_obs_value(jax.random.fold_in(streams_of[7], 71), 0)
    obs_error = jnp.clip(jnp.exp(math.log(2.0) - 1.3862944 * jax.random.uniform(streams_of[5], (NB, GROUPS, OBS), jnp.float32) ** block_levels(streams_of[5], (NB, GROUPS, OBS), ((1, 4),), -0.2, 0.2)), 0.5, 2.0)
    ancestors = with_ends(jax.random.randint(streams_of[6], (NB, GROUPS, REGIONS, M), 0, M), jax.random.fold_in(streams_of[6], 1), 0, M - 1).astype(jnp.int32)
    return dict(prior_fields=prior_fields, channel_weights=channel_weights, obs_owner=obs_owner, obs_offset=obs_offset, obs_value=obs_value, obs_error=obs_error, ancestors=ancestors)


HIGH = lax.Precision.HIGHEST


def blend_matrices(prior_obs, observed, obs_dev, centres, positions, scale, parents):
    count = observed.shape[0]
    members = prior_obs.shape[1]
    innovation = ((observed[:, None] - prior_obs) / obs_dev[:, None]) ** 2
    distance = (centres[:, None] - positions[None, :]) / scale
    taper = jnp.exp(-0.5 * distance * distance)
    log_weight = (-0.5 / count) * jnp.dot(taper, innovation, precision=HIGH)
    top_value = jnp.max(log_weight, axis=1, keepdims=True)
    expo_weight = jnp.exp(log_weight - top_value)
    weight = expo_weight / jnp.sum(expo_weight, axis=1, keepdims=True)
    alpha = 0.8 * (1.0 - jnp.exp(-jnp.sum(taper, axis=1) / count))
    onehot = (parents[:, :, None] == jnp.arange(members, dtype=jnp.int32)[None, None, :]).astype(jnp.float32)
    identity = jnp.eye(members, dtype=jnp.float32)
    remain = 1.0 - alpha
    return alpha[:, None, None] * onehot + remain[:, None, None] * identity[None] + (weight - 1.0 / members)[:, None, :]


def reference(prior_fields, channel_weights, obs_owner, obs_offset, obs_value, obs_error, ancestors):
    members, levels, cells = prior_fields.shape
    groups = channel_weights.shape[1]
    group_depth = levels // groups
    regions = ancestors.shape[2]
    region_cells = cells // regions
    block_cells = cells // N_GRID
    scale = regions / 2.0
    centres = jnp.arange(regions, dtype=jnp.int32).astype(jnp.float32) + 0.5
    fields = prior_fields
    for batch in range(NB):
        obs_cells = (obs_owner[batch] * block_cells + obs_offset[batch]).astype(jnp.int32)
        picked = fields[:, :, obs_cells.reshape(-1)].reshape(members, levels, groups, OBS)
        priors = jnp.einsum("mlgk,lg->gkm", picked, channel_weights, precision=HIGH)
        pieces = []
        for group in range(groups):
            positions = obs_cells[group].astype(jnp.float32) / region_cells
            blend = blend_matrices(priors[group], obs_value[batch, group], obs_error[batch, group], centres, positions, scale, ancestors[batch, group])
            slab = fields[:, group * group_depth:(group + 1) * group_depth, :].reshape(members, group_depth, regions, region_cells)
            mixed = jnp.einsum("rjm,mlrc->jlrc", blend, slab, precision=HIGH)
            pieces.append(mixed.reshape(members, group_depth, cells))
        fields = jnp.concatenate(pieces, axis=1)
    return fields
```

```python
import jax
import jax.numpy as jnp
from jax import lax
from jax.sharding import PartitionSpec as P

NB = 4
HIGH = lax.Precision.HIGHEST


def dot(a, b):
    return jnp.dot(a, b, precision=HIGH, preferred_element_type=jnp.float32)


def share(value, axis):
    n = lax.axis_size(axis)
    return lax.all_to_all(jnp.broadcast_to(value[None], (n,) + value.shape), axis, 0, 0, tiled=True)


def taper_rows(regions, positions, scale):
    distance = (regions + 0.5 - positions) / scale
    return jnp.exp(-0.5 * distance * distance)


def body(prior_fields, channel_weights, obs_owner, obs_offset, obs_value, obs_error, ancestors):
    n = lax.axis_size("grid")
    slab, depth, cells = prior_fields.shape
    members = slab * n
    block_cells = cells // n
    groups = channel_weights.shape[1]
    count = obs_offset.shape[2]
    scale = n / 2.0
    group = lax.axis_index("lev")
    block = lax.axis_index("grid")

    cols = (obs_owner[:, None, None] * block_cells + obs_offset).reshape(-1)
    picked = prior_fields[:, :, cols].reshape(slab, depth, NB, groups, count)
    partial = jnp.einsum("mlbgk,lg->mbgk", picked, channel_weights, precision=HIGH)
    partial = share(partial.reshape(slab, NB * groups * count), "grid").reshape(members, -1)
    parents = share(ancestors[:, 0, 0], "grid")

    send = jnp.transpose(prior_fields.reshape(slab, depth, n, block_cells), (2, 0, 1, 3))
    fields = lax.all_to_all(send, "grid", 0, 0, tiled=True).reshape(members, depth * block_cells)

    own_off = lax.dynamic_index_in_dim(obs_offset, group, 1, keepdims=False)
    regions = jnp.concatenate([obs_owner, block[None]]).astype(jnp.float32)[:, None]
    tapers, alphas = [], []
    for b in range(NB):
        pos = (obs_owner[b] * block_cells + own_off[b]).astype(jnp.float32) / block_cells
        tapers.append(taper_rows(regions, pos[None], scale))
        alphas.append(0.8 * (1.0 - jnp.exp(-jnp.sum(tapers[b], axis=1) / count)))

    member = jnp.arange(members, dtype=jnp.int32)
    eye = jnp.eye(members, dtype=jnp.float32)

    def mover(b, slot, region):
        a = alphas[b][slot]
        row = lax.dynamic_index_in_dim(parents, region, 0, keepdims=False)[b]
        return a * (member[:, None] == row[None, :]).astype(jnp.float32) + (1.0 - a) * eye

    pt = partial.T.reshape(NB, groups * count, members)
    chain = {}
    for b in range(NB):
        chain[b, 0] = pt[b]
        for e in range(b):
            chain[b, e + 1] = dot(chain[b, e], mover(e, b, obs_owner[b]))
    q = jnp.stack([chain[b, b].reshape(groups, count, members) for b in range(NB)], 1)
    q = lax.all_to_all(q, "lev", 0, 0, tiled=True).sum(0)

    own = [mover(b, NB, block) for b in range(NB)]
    total = dot(dot(dot(own[0], own[1]), own[2]), own[3])
    moved = lax.dot_general(total, fields, (((0,), (0,)), ((), ())), precision=HIGH)
    moved = lax.all_to_all(moved.reshape(n, slab, depth, block_cells), "grid", 0, 0, tiled=True)

    shift = jnp.zeros((count,), jnp.float32)
    tilts = []
    for b in range(NB):
        if b > 0:
            s = sum(jnp.sum(chain[b, e] * tilts[e][b][None], axis=1) for e in range(b))
            s = lax.all_to_all(s.reshape(groups, 1, count), "lev", 0, 0, tiled=True)
            shift = s[:, 0].sum(0)
        innovation = ((obs_value[b, 0][:, None] - (q[b] + shift[:, None])) / obs_error[b, 0][:, None]) ** 2
        log_weight = -0.5 / count * dot(tapers[b], innovation)
        expo = jnp.exp(log_weight - jnp.max(log_weight, axis=1, keepdims=True))
        tilts.append(expo / jnp.sum(expo, axis=1, keepdims=True) - 1.0 / members)
    v = jnp.zeros((members,), jnp.float32)
    for b in reversed(range(NB)):
        v = dot(own[b], v) if b < NB - 1 else v
        v = v + tilts[b][NB]
    u = share(dot(v, fields).reshape(depth, block_cells), "grid")
    out = moved + u[:, None]
    return jnp.transpose(out, (1, 2, 0, 3)).reshape(slab, depth, cells)


def solution(mesh):
    in_specs = (
        P("grid", "lev", None),
        P("lev", None),
        P(),
        P(),
        P(None, "lev", None),
        P(None, "lev", None),
        P(None, "lev", "grid", None),
    )
    out_specs = P("grid", "lev", None)
    return jax.shard_map(body, mesh=mesh, in_specs=in_specs, out_specs=out_specs, check_vma=False)
```

```python
import jax
import jax.numpy as jnp
from jax import lax
from jax.sharding import PartitionSpec as P

NB = 4
HIGH = lax.Precision.HIGHEST


def dot(a, b):
    return jnp.dot(a, b, precision=HIGH, preferred_element_type=jnp.float32)


def share(value, axis):
    n = lax.axis_size(axis)
    return lax.all_to_all(jnp.broadcast_to(value[None], (n,) + value.shape), axis, 0, 0, tiled=True)


def trade(value, axis):
    n = lax.axis_size(axis)
    me = lax.axis_index(axis)
    got = [lax.dynamic_index_in_dim(value, me, 0, keepdims=False)]
    for step in range(1, n):
        piece = lax.dynamic_index_in_dim(value, lax.rem(me + step, n), 0, keepdims=False)
        got.append(lax.ppermute(piece, axis, [(j, (j + step) % n) for j in range(n)]))
    return got


def taper_rows(regions, positions, scale):
    distance = (regions + 0.5 - positions) / scale
    return jnp.exp(-0.5 * distance * distance)


def body(prior_fields, channel_weights, obs_owner, obs_offset, obs_value, obs_error, ancestors):
    n = lax.axis_size("grid")
    slab, depth, cells = prior_fields.shape
    members = slab * n
    block_cells = cells // n
    groups = channel_weights.shape[1]
    count = obs_offset.shape[2]
    scale = n / 2.0
    group = lax.axis_index("lev")
    block = lax.axis_index("grid")

    cols = (obs_owner[:, None, None] * block_cells + obs_offset).reshape(-1)
    picked = prior_fields[:, :, cols].reshape(slab, depth, NB, groups, count)
    partial = jnp.einsum("mlbgk,lg->mbgk", picked, channel_weights, precision=HIGH)
    partial = share(partial.reshape(slab, NB * groups * count), "grid").reshape(members, -1)
    parents = share(ancestors[:, 0, 0], "grid")

    send = jnp.transpose(prior_fields.reshape(slab, depth, n, block_cells), (2, 0, 1, 3))
    fields = lax.all_to_all(send, "grid", 0, 0, tiled=True).reshape(members, depth * block_cells)

    own_off = lax.dynamic_index_in_dim(obs_offset, group, 1, keepdims=False)
    regions = jnp.concatenate([obs_owner, block[None]]).astype(jnp.float32)[:, None]
    tapers, alphas = [], []
    for b in range(NB):
        pos = (obs_owner[b] * block_cells + own_off[b]).astype(jnp.float32) / block_cells
        tapers.append(taper_rows(regions, pos[None], scale))
        alphas.append(0.8 * (1.0 - jnp.exp(-jnp.sum(tapers[b], axis=1) / count)))

    member = jnp.arange(members, dtype=jnp.int32)
    eye = jnp.eye(members, dtype=jnp.float32)

    def mover(b, slot, region):
        a = alphas[b][slot]
        row = lax.dynamic_index_in_dim(parents, region, 0, keepdims=False)[b]
        return a * (member[:, None] == row[None, :]).astype(jnp.float32) + (1.0 - a) * eye

    pt = partial.T.reshape(NB, groups * count, members)
    chain = {}
    for b in range(NB):
        chain[b, 0] = pt[b]
        for e in range(b):
            chain[b, e + 1] = dot(chain[b, e], mover(e, b, obs_owner[b]))
    q = jnp.stack([chain[b, b].reshape(groups, count, members) for b in range(NB)], 1)
    q = sum(trade(q, "lev"))

    own = [mover(b, NB, block) for b in range(NB)]
    total = dot(dot(dot(own[0], own[1]), own[2]), own[3])
    moved = lax.dot_general(total, fields, (((0,), (0,)), ((), ())), precision=HIGH)
    moved = lax.all_to_all(moved.reshape(n, slab, depth, block_cells), "grid", 0, 0, tiled=True)

    shift = jnp.zeros((count,), jnp.float32)
    tilts = []
    for b in range(NB):
        if b > 0:
            s = sum(jnp.sum(chain[b, e] * tilts[e][b][None], axis=1) for e in range(b))
            shift = sum(trade(s.reshape(groups, count), "lev"))
        innovation = ((obs_value[b, 0][:, None] - (q[b] + shift[:, None])) / obs_error[b, 0][:, None]) ** 2
        log_weight = -0.5 / count * dot(tapers[b], innovation)
        expo = jnp.exp(log_weight - jnp.max(log_weight, axis=1, keepdims=True))
        tilts.append(expo / jnp.sum(expo, axis=1, keepdims=True) - 1.0 / members)
    v = jnp.zeros((members,), jnp.float32)
    for b in reversed(range(NB)):
        v = dot(own[b], v) if b < NB - 1 else v
        v = v + tilts[b][NB]
    u = dot(v, fields).reshape(depth, block_cells)
    ring = [u]
    for step in range(1, n):
        ring.append(lax.ppermute(u, "grid", [(j, (j + step) % n) for j in range(n)]))
    u = jnp.stack(ring)[lax.rem(block - jnp.arange(n) + n, n)]
    out = moved + u[:, None]
    return jnp.transpose(out, (1, 2, 0, 3)).reshape(slab, depth, cells)


def solution(mesh):
    in_specs = (
        P("grid", "lev", None),
        P("lev", None),
        P(),
        P(),
        P(None, "lev", None),
        P(None, "lev", None),
        P(None, "lev", "grid", None),
    )
    out_specs = P("grid", "lev", None)
    return jax.shard_map(body, mesh=mesh, in_specs=in_specs, out_specs=out_specs, check_vma=False)
```

```python
import functools

import jax
import jax.numpy as jnp
from jax import lax
from jax.experimental import pallas as pl
from jax.experimental.pallas import tpu as pltpu
from jax.sharding import PartitionSpec as P

NB = 4
HIGH = lax.Precision.HIGHEST
LANES = 128
SPARE = 16
F32 = jnp.float32
VMEM = pl.BlockSpec(memory_space=pltpu.VMEM)
SMEM = pl.BlockSpec(memory_space=pltpu.SMEM)
LIMIT = 48 * 1024 * 1024


def call(kernel, out_shapes, in_specs, scratch=(), flops=0, moved=0):
    many = isinstance(out_shapes, (list, tuple))
    return pl.pallas_call(
        kernel,
        out_shape=out_shapes,
        in_specs=in_specs,
        out_specs=[VMEM] * len(out_shapes) if many else VMEM,
        scratch_shapes=list(scratch),
        compiler_params=pltpu.CompilerParams(vmem_limit_bytes=LIMIT),
        cost_estimate=pl.CostEstimate(flops=flops, bytes_accessed=moved, transcendentals=0),
    )


def high_dot(a, b, dims=((1,), (0,))):
    return lax.dot_general(a, b, (dims, ((), ())), precision=HIGH, preferred_element_type=F32)


def pick_kernel(shape, owner, weights, offsets, extras, prior, out):
    n, slab, depth, block_cells, groups, count = shape
    width = groups * count
    group_of = lax.broadcasted_iota(jnp.int32, (1, width), 1) // count
    cell = lax.broadcasted_iota(jnp.int32, (block_cells, width), 0)
    for b in range(NB):
        start = pl.multiple_of(owner[b] * block_cells, LANES)
        pieces = []
        for level in range(depth):
            value = prior[:, level, pl.ds(start, block_cells)]
            first = value.astype(jnp.bfloat16)
            rest = value - first.astype(F32)
            second = rest.astype(jnp.bfloat16)
            third = (rest - second.astype(F32)).astype(jnp.bfloat16)
            pieces += [first.astype(F32), second.astype(F32), third.astype(F32)]
        onehot = (cell == offsets[b : b + 1, :]).astype(jnp.bfloat16)
        stacked = jnp.concatenate(pieces, axis=0).astype(jnp.bfloat16)
        found = jnp.dot(stacked, onehot, preferred_element_type=F32)
        total = jnp.zeros((slab, width), F32)
        for level in range(depth):
            base = 3 * level * slab
            exact = found[base : base + slab] + (
                found[base + slab : base + 2 * slab] + found[base + 2 * slab : base + 3 * slab]
            )
            row = jnp.zeros((1, width), F32)
            for g in range(groups):
                row = jnp.where(group_of == g, weights[level, g], row)
            total = total + exact * row
        for d in range(n):
            out[d, :, b * width : (b + 1) * width] = total
    for d in range(n):
        out[d, :, NB * width :] = extras[...]


def retile_kernel(shape, prior, out):
    n, slab, depth, block_cells = shape
    for r in range(n):
        for level in range(depth):
            out[r, level] = prior[:, level, r * block_cells : (r + 1) * block_cells]


PAIRS = [(e, b) for b in range(1, NB) for e in range(b)]


def turn_kernel(shape, owner, gathered, out):
    n, slab, width = shape
    members = n * slab
    for i in range(width // LANES):
        block = gathered[:, :, i * LANES : (i + 1) * LANES].reshape(members, LANES)
        out[i * LANES : (i + 1) * LANES, :] = block.T

    def slot(region, s):
        lane = width + (s // slab) * LANES
        row = s % slab
        return gathered[region, row : row + 1, lane : lane + LANES]

    for i, (e, b) in enumerate(PAIRS):
        out[width + i : width + i + 1, :] = slot(owner[b], e)
    for i in range(4):
        out[width + 8 + i : width + 9 + i, :] = slot(0, NB + i)
    out[width + 6 : width + 8, :] = jnp.zeros((2, LANES), F32)
    out[width + 12 : width + 16, :] = jnp.zeros((4, LANES), F32)


def region_column(owner, block):
    row = lax.broadcasted_iota(jnp.int32, (8, 1), 0)
    value = jnp.full((8, 1), block, jnp.int32)
    for b in range(1, NB):
        value = jnp.where(row == b - 1, owner[b], value)
    return value.astype(F32)


def tapers(owner, offs, region, b, block_cells, scale):
    cells = owner[b] * block_cells + offs
    position = cells.astype(F32) / block_cells
    distance = (region + 0.5 - position) / scale
    return jnp.exp(-0.5 * distance * distance)


def alpha_of(taper, count):
    return 0.8 * (1.0 - jnp.exp(-jnp.sum(taper, axis=1, keepdims=True) / count))


def onehot_rows(parents, members):
    member = lax.broadcasted_iota(jnp.int32, (members, members), 0)
    return (member == parents).astype(F32)


def mix_kernel(shape, owner, offsets, ancestors, fields, out):
    n, slab, depth, block_cells, count, scale = shape
    members = n * slab
    block, group = lax.axis_index("grid"), lax.axis_index("lev")
    region = jnp.full((8, 1), block, jnp.int32).astype(F32)
    row = lax.broadcasted_iota(jnp.int32, (members, members), 0)
    column = lax.broadcasted_iota(jnp.int32, (members, members), 1)
    eye = (row == column).astype(F32)
    total = None
    for b in range(NB):
        taper = tapers(owner, offsets[b, pl.ds(group, 1), :], region, b, block_cells, scale)
        alpha = alpha_of(taper, count)[0:1, 0:1]
        step = alpha * onehot_rows(ancestors[b : b + 1, :], members) + (1.0 - alpha) * eye
        total = step if total is None else high_dot(total, step)
    back = total.T
    for level in range(depth):
        value = fields[:, level].reshape(members, block_cells)
        out[:, level] = high_dot(back, value).reshape(n, slab, block_cells)


def chain_kernel(
    shape, owner, offsets, ancestors, own, near, far, cross, fields, out, taper_at, alpha_at, weight_at, column_at
):
    n, slab, depth, block_cells, groups, count, scale = shape
    members = n * slab
    width = groups * count
    base = NB * width
    block, group = lax.axis_index("grid"), lax.axis_index("lev")
    sources = [own, near, far, cross]
    index = [lax.bitwise_xor(group, p) for p in range(4)]
    region = region_column(owner, block)
    for b in range(NB):
        for g in range(groups):
            taper = tapers(owner, offsets[b, g : g + 1, :], region, b, block_cells, scale)
            taper_at[b, g] = taper
            alpha_at[b, g] = jnp.broadcast_to(alpha_of(taper, count), (8, LANES))
    parents = []
    for p, source in enumerate(sources):
        column_at[index[p]] = source[base + 8 : base + 16, :].T
        parents.append(source[base : base + 8, :].astype(jnp.int32))
    for b in range(NB):
        for c in range(groups):
            total = jnp.zeros((count, members), F32)
            tilted = jnp.zeros((count, members), F32)
            for p, source in enumerate(sources):
                start = b * width + c * count
                value = source[start : start + count, :]
                for e in range(b):
                    tilted = tilted + value * weight_at[e, index[p]][b - 1 : b, :]
                    alpha = alpha_at[e, index[p]][b - 1 : b, :]
                    line = PAIRS.index((e, b))
                    where = jnp.broadcast_to(parents[p][line : line + 1, :], (count, members))
                    moved = jnp.take_along_axis(value, where, axis=1, mode="promise_in_bounds")
                    value = alpha * moved + (1.0 - alpha) * value
                total = total + value
            if b > 0:
                total = total + jnp.sum(tilted, axis=1, keepdims=True)
            low = (b % 2) * count
            observed = column_at[c, low : low + count, b // 2 : b // 2 + 1]
            error = column_at[c, low : low + count, 2 + b // 2 : 3 + b // 2]
            scaled = (observed - total) / error
            log_weight = (-0.5 / count) * high_dot(taper_at[b, c], scaled * scaled)
            expo = jnp.exp(log_weight - jnp.max(log_weight, axis=1, keepdims=True))
            weight_at[b, c] = expo / jnp.sum(expo, axis=1, keepdims=True) - 1.0 / members
    pulled = weight_at[NB - 1, group]
    for b in reversed(range(NB - 1)):
        alpha = alpha_at[b, group]
        spread = high_dot(pulled, onehot_rows(ancestors[b : b + 1, :], members), ((1,), (1,)))
        pulled = weight_at[b, group] + alpha * spread + (1.0 - alpha) * pulled
    for level in range(depth):
        value = fields[:, level].reshape(members, block_cells)
        shift = high_dot(pulled, value)[3:4]
        for d in range(n):
            out[d, level : level + 1, :] = shift


def final_kernel(shape, moved, shift, out):
    n, slab, depth, block_cells = shape
    for r in range(n):
        for level in range(depth):
            value = moved[r, level] + shift[r, level : level + 1, :]
            out[:, level, r * block_cells : (r + 1) * block_cells] = value


def body(prior, channel_weights, obs_owner, obs_offset, obs_value, obs_error, ancestors):
    n, lev = lax.axis_size("grid"), lax.axis_size("lev")
    slab, depth, cells = prior.shape
    members = slab * n
    block_cells = cells // n
    groups = channel_weights.shape[1]
    count = obs_offset.shape[2]
    width = NB * groups * count
    scale = n / 2.0
    shape = jax.ShapeDtypeStruct
    parents = ancestors[:, 0, 0]

    slots = jnp.concatenate(
        [parents.astype(F32), obs_value.reshape(-1, LANES), obs_error.reshape(-1, LANES)], axis=0
    )
    blocks = -(-slots.shape[0] // slab)
    slots = jnp.pad(slots, ((0, blocks * slab - slots.shape[0]), (0, 0)))
    slots = slots.reshape(blocks, slab, LANES).transpose(1, 0, 2).reshape(slab, blocks * LANES)

    send = call(
        functools.partial(pick_kernel, (n, slab, depth, block_cells, groups, count)),
        shape((n, slab, width + blocks * LANES), F32),
        [SMEM, SMEM, VMEM, VMEM, VMEM],
        flops=10**8,
        moved=10**6,
    )(obs_owner, channel_weights, obs_offset.reshape(NB, -1), slots, prior)
    gathered = lax.all_to_all(send, "grid", 0, 0, tiled=True)

    send = call(
        functools.partial(retile_kernel, (n, slab, depth, block_cells)),
        shape((n, depth, slab, block_cells), F32),
        [VMEM],
        moved=10**6,
    )(prior)
    fields = lax.all_to_all(send, "grid", 0, 0, tiled=True)

    own = call(
        functools.partial(turn_kernel, (n, slab, width)),
        shape((width + SPARE, members), F32),
        [SMEM, VMEM],
        moved=10**6,
    )(obs_owner, gathered)
    far = lax.ppermute(own, "lev", [(j, j ^ 2) for j in range(lev)])
    near = lax.ppermute(own, "lev", [(j, j ^ 1) for j in range(lev)])
    cross = lax.ppermute(far, "lev", [(j, j ^ 1) for j in range(lev)])

    send = call(
        functools.partial(mix_kernel, (n, slab, depth, block_cells, count, scale)),
        shape((n, depth, slab, block_cells), F32),
        [SMEM, VMEM, VMEM, VMEM],
        flops=10**8,
        moved=10**6,
    )(obs_owner, obs_offset, parents, fields)
    moved = lax.all_to_all(send, "grid", 0, 0, tiled=True)

    send = call(
        functools.partial(chain_kernel, (n, slab, depth, block_cells, groups, count, scale)),
        shape((n, depth, block_cells), F32),
        [SMEM] + [VMEM] * 7,
        scratch=[
            pltpu.VMEM((NB, groups, 8, count), F32),
            pltpu.VMEM((NB, groups, 8, LANES), F32),
            pltpu.VMEM((NB, groups, 8, LANES), F32),
            pltpu.VMEM((groups, LANES, 8), F32),
        ],
        flops=10**9,
        moved=10**7,
    )(obs_owner, obs_offset, parents, own, near, far, cross, fields)
    shift = lax.all_to_all(send, "grid", 0, 0, tiled=True)

    return call(
        functools.partial(final_kernel, (n, slab, depth, block_cells)),
        shape((slab, depth, cells), F32),
        [VMEM, VMEM],
        moved=10**6,
    )(moved, shift)


def solution(mesh):
    in_specs = (
        P("grid", "lev", None),
        P("lev", None),
        P(),
        P(),
        P(None, "lev", None),
        P(None, "lev", None),
        P(None, "lev", "grid", None),
    )
    out_specs = P("grid", "lev", None)
    return jax.shard_map(body, mesh=mesh, in_specs=in_specs, out_specs=out_specs, check_vma=False)
```

```python
import functools

import jax
import jax.numpy as jnp
from jax import lax
from jax.experimental import pallas as pl
from jax.experimental.pallas import tpu as pltpu
from jax.sharding import PartitionSpec as P

NB = 4
HIGH = lax.Precision.HIGHEST
LANES = 128
F32 = jnp.float32
VMEM = pl.BlockSpec(memory_space=pltpu.VMEM)
SMEM = pl.BlockSpec(memory_space=pltpu.SMEM)
LIMIT = 48 * 1024 * 1024

PAIRS = [(e, b) for b in range(1, NB) for e in range(b)]
PARENT, ALPHA, LATER, VALUE, OWN, SPARE = 0, 6, 12, 18, 22, 32


def call(kernel, out_shapes, in_specs, scratch=(), flops=0, moved=0):
    many = isinstance(out_shapes, (list, tuple))
    return pl.pallas_call(
        kernel,
        out_shape=out_shapes,
        in_specs=in_specs,
        out_specs=[VMEM] * len(out_shapes) if many else VMEM,
        scratch_shapes=list(scratch),
        compiler_params=pltpu.CompilerParams(vmem_limit_bytes=LIMIT),
        cost_estimate=pl.CostEstimate(flops=flops, bytes_accessed=moved, transcendentals=0),
    )


def high_dot(a, b):
    return lax.dot_general(a, b, (((1,), (0,)), ((), ())), precision=HIGH, preferred_element_type=F32)


def lane_take(value, row):
    where = jnp.broadcast_to(row, value.shape)
    return jnp.take_along_axis(value, where, axis=1, mode="promise_in_bounds")


def pick_kernel(shape, owner, weights, offsets, ancestors, prior, out):
    slab, depth, block_cells, groups, count = shape
    width = groups * count
    per = LANES // count
    for b in range(NB):
        start = pl.multiple_of(owner[b] * block_cells, LANES)
        levels = [prior[:, level, pl.ds(start, block_cells)] for level in range(depth)]
        for c in range(width // LANES):
            cell = jnp.concatenate([offsets[b, g : g + 1, :] for g in range(c * per, (c + 1) * per)], axis=1)
            low, high = lax.rem(cell, LANES), lax.div(cell, LANES)
            total = jnp.zeros((slab, LANES), F32)
            for level in range(depth):
                found = jnp.zeros((slab, LANES), F32)
                for h in range(block_cells // LANES):
                    part = lane_take(levels[level][:, h * LANES : (h + 1) * LANES], low)
                    found = jnp.where(high == h, part, found)
                row = jnp.concatenate(
                    [
                        jnp.broadcast_to(weights[level : level + 1, g : g + 1], (1, count))
                        for g in range(c * per, (c + 1) * per)
                    ],
                    axis=1,
                )
                total = total + found * row
            lane = b * width + c * LANES
            out[:, lane : lane + LANES] = total
    lane = NB * width
    out[:, lane:] = jnp.zeros((slab, out.shape[1] - lane), F32)
    for b in range(NB):
        row, block = b % slab, lane + (b // slab) * LANES
        out[row : row + 1, block : block + LANES] = ancestors[b].astype(F32)


def retile_kernel(shape, prior, out):
    n, slab, depth, block_cells = shape
    for r in range(n):
        for level in range(depth):
            out[r, level] = prior[:, level, r * block_cells : (r + 1) * block_cells]


def prep_kernel(shape, owner, offsets, values, errors, ancestors, rows, steps):
    block_cells, count, scale, members = shape
    block, group = lax.axis_index("grid"), lax.axis_index("lev")
    index = lax.broadcasted_iota(jnp.int32, (8, 1), 0)
    region = jnp.full((8, 1), block, jnp.int32)
    for b in range(1, NB):
        region = jnp.where(index == b - 1, owner[b], region)
    centre = region.astype(F32) + 0.5
    rows[...] = jnp.zeros((SPARE, LANES), F32)
    row = lax.broadcasted_iota(jnp.int32, (members, members), 0)
    column = lax.broadcasted_iota(jnp.int32, (members, members), 1)
    turned = (row == column).astype(F32)
    for b in range(NB):
        cells = owner[b] * block_cells + offsets[b, pl.ds(group, 1), :]
        distance = (centre - cells.astype(F32) / block_cells) / scale
        taper = jnp.exp(-0.5 * distance * distance)
        alpha = 0.8 * (1.0 - jnp.exp(-jnp.sum(taper, axis=1, keepdims=True) / count))
        error = errors[b]
        part = (-0.5 / count) * (taper / (error * error))
        for later in range(b + 1, NB):
            i = PAIRS.index((b, later))
            rows[ALPHA + i : ALPHA + i + 1, :] = jnp.broadcast_to(alpha[later - 1 : later], (1, LANES))
            rows[LATER + i : LATER + i + 1, :count] = part[later - 1 : later]
        rows[VALUE + b : VALUE + b + 1, :count] = values[b]
        rows[OWN + b : OWN + b + 1, :count] = part[NB - 1 : NB]
        steps[b] = turned.T
        own = alpha[NB - 1 : NB]
        turned = own * lane_take(turned, ancestors[b]) + (1.0 - own) * turned
    steps[NB] = turned.T


def turn_kernel(shape, owner, rows, *refs):
    n, slab, width = shape
    pieces, out, held = refs[:-2], refs[-2], refs[-1]
    members = n * slab
    if len(pieces) == 1:
        held[...] = pieces[0][...]
    else:
        block = lax.axis_index("grid")
        for i, piece in enumerate(pieces):
            held[lax.bitwise_xor(block, i)] = piece[...]
    for i in range(width // LANES):
        lanes = slice(i * LANES, (i + 1) * LANES)
        out[lanes, :] = held[:, :, lanes].reshape(members, LANES).T
    out[width:, :] = rows[...]
    for i, (e, b) in enumerate(PAIRS):
        lane = width + (e // slab) * LANES
        line = e % slab
        out[width + PARENT + i : width + PARENT + i + 1, :] = held[owner[b], line : line + 1, lane : lane + LANES]


def mix_kernel(shape, steps, fields, out):
    n, slab, depth, block_cells = shape
    for level in range(depth):
        value = fields[:, level].reshape(n * slab, block_cells)
        out[:, level] = high_dot(steps[NB], value).reshape(n, slab, block_cells)


def chain_kernel(shape, own, near, far, cross, steps, fields, out):
    n, slab, depth, block_cells, groups, count = shape
    members = n * slab
    width = groups * count
    base = NB * width
    group = lax.axis_index("lev")
    sources = [own, near, far, cross]
    columns = [source[base : base + SPARE, :].T for source in sources]
    parents, alphas = [], []
    for source in sources:
        parents.append(source[base + PARENT : base + PARENT + 8, :].astype(jnp.int32))
        alphas.append(source[base + ALPHA : base + ALPHA + 6, :])
    tilts = {}
    pulled = []
    for b in range(NB):
        kinds = [(q, later) for q in range(groups) for later in range(b + 1, NB)] + [(0, None)]
        height = -(-len(kinds) // 8) * 8
        index = lax.broadcasted_iota(jnp.int32, (height, members), 0)
        logs = jnp.zeros((height, members), F32)
        for q in range(groups if b < NB - 1 else 1):
            start = pl.multiple_of(b * width + lax.bitwise_xor(group, q) * count, count)
            total = jnp.zeros((count, members), F32)
            tilted = jnp.zeros((count, members), F32)
            for p, source in enumerate(sources):
                value = source[pl.ds(start, count), :]
                for e in range(b):
                    i = PAIRS.index((e, b))
                    tilted = tilted + value * tilts[e, p, b]
                    alpha = alphas[p][i : i + 1]
                    moved = lane_take(value, parents[p][i : i + 1])
                    value = alpha * moved + (1.0 - alpha) * value
                total = total + value
            if b > 0:
                total = total + jnp.sum(tilted, axis=1, keepdims=True)
            miss = columns[q][:count, VALUE + b : VALUE + b + 1] - total
            square = miss * miss
            for row, (owner_group, later) in enumerate(kinds):
                if owner_group != q:
                    continue
                at = OWN + b if later is None else LATER + PAIRS.index((b, later))
                log = jnp.sum(columns[q][:count, at : at + 1] * square, axis=0, keepdims=True)
                logs = jnp.where(index == row, log, logs)
        expo = jnp.exp(logs - jnp.max(logs, axis=1, keepdims=True))
        tilt = expo / jnp.sum(expo, axis=1, keepdims=True) - 1.0 / members
        for row, (q, later) in enumerate(kinds):
            if later is None:
                pulled.append(tilt[row : row + 1])
            else:
                tilts[b, q, later] = tilt[row : row + 1]
    pull = jnp.zeros((8, members), F32)
    for b in range(NB):
        pull = pull + high_dot(jnp.broadcast_to(pulled[b], (8, members)), steps[b])
    for level in range(depth):
        value = fields[:, level].reshape(members, block_cells)
        shift = high_dot(pull, value)[0:1]
        for d in range(n):
            out[d, level : level + 1, :] = shift


def final_kernel(shape, moved, shift, out):
    n, slab, depth, block_cells = shape
    for r in range(n):
        for level in range(depth):
            value = moved[r, level] + shift[r, level : level + 1, :]
            out[:, level, r * block_cells : (r + 1) * block_cells] = value


def gather_pieces(piece, n):
    if n != 8:
        return [lax.all_to_all(jnp.broadcast_to(piece[None], (n,) + piece.shape), "grid", 0, 0, tiled=True)]
    pieces = [piece]
    for far in (2, 4, 6):
        pieces.append(lax.ppermute(piece, "grid", [(j, j ^ far) for j in range(n)]))
    result = []
    for part in pieces:
        result += [part, lax.ppermute(part, "grid", [(j, j ^ 1) for j in range(n)])]
    return result


def body(prior, channel_weights, obs_owner, obs_offset, obs_value, obs_error, ancestors):
    n, lev = lax.axis_size("grid"), lax.axis_size("lev")
    slab, depth, cells = prior.shape
    members = slab * n
    block_cells = cells // n
    groups = channel_weights.shape[1]
    count = obs_offset.shape[2]
    width = NB * groups * count
    scale = n / 2.0
    shape = jax.ShapeDtypeStruct
    parents = ancestors[:, 0]
    wide = width + -(-NB // slab) * LANES

    piece = call(
        functools.partial(pick_kernel, (slab, depth, block_cells, groups, count)),
        shape((slab, wide), F32),
        [SMEM, VMEM, VMEM, VMEM, VMEM],
        moved=10**6,
    )(obs_owner, channel_weights, obs_offset, parents, prior)
    pieces = gather_pieces(piece, n)

    send = call(
        functools.partial(retile_kernel, (n, slab, depth, block_cells)),
        shape((n, depth, slab, block_cells), F32),
        [VMEM],
        moved=10**6,
    )(prior)
    fields = lax.all_to_all(send, "grid", 0, 0, tiled=True)

    rows, steps = call(
        functools.partial(prep_kernel, (block_cells, count, scale, members)),
        [shape((SPARE, LANES), F32), shape((NB + 1, members, members), F32)],
        [SMEM, VMEM, VMEM, VMEM, VMEM],
        moved=10**6,
    )(obs_owner, obs_offset, obs_value, obs_error, parents)

    own = call(
        functools.partial(turn_kernel, (n, slab, width)),
        shape((width + SPARE, members), F32),
        [SMEM] + [VMEM] * (1 + len(pieces)),
        scratch=[pltpu.VMEM((n, slab, wide), F32)],
        moved=10**6,
    )(obs_owner, rows, *pieces)
    far = lax.ppermute(own, "lev", [(j, j ^ 2) for j in range(lev)])
    near = lax.ppermute(own, "lev", [(j, j ^ 1) for j in range(lev)])
    cross = lax.ppermute(far, "lev", [(j, j ^ 1) for j in range(lev)])

    send = call(
        functools.partial(mix_kernel, (n, slab, depth, block_cells)),
        shape((n, depth, slab, block_cells), F32),
        [VMEM, VMEM],
        flops=10**8,
        moved=10**6,
    )(steps, fields)
    moved = lax.all_to_all(send, "grid", 0, 0, tiled=True)

    send = call(
        functools.partial(chain_kernel, (n, slab, depth, block_cells, groups, count)),
        shape((n, depth, block_cells), F32),
        [VMEM] * 6,
        flops=10**9,
        moved=10**7,
    )(own, near, far, cross, steps, fields)
    shift = lax.all_to_all(send, "grid", 0, 0, tiled=True)

    return call(
        functools.partial(final_kernel, (n, slab, depth, block_cells)),
        shape((slab, depth, cells), F32),
        [VMEM, VMEM],
        moved=10**6,
    )(moved, shift)


def solution(mesh):
    in_specs = (
        P("grid", "lev", None),
        P("lev", None),
        P(),
        P(),
        P(None, "lev", None),
        P(None, "lev", None),
        P(None, "lev", "grid", None),
    )
    out_specs = P("grid", "lev", None)
    return jax.shard_map(body, mesh=mesh, in_specs=in_specs, out_specs=out_specs, check_vma=False)
```

```python
import functools

import jax
import jax.numpy as jnp
from jax import lax
from jax.experimental import pallas as pl
from jax.experimental.pallas import tpu as pltpu
from jax.sharding import PartitionSpec as P

NB = 4
HIGH = lax.Precision.HIGHEST
LANES = 128
F32 = jnp.float32
VMEM = pl.BlockSpec(memory_space=pltpu.VMEM)
SMEM = pl.BlockSpec(memory_space=pltpu.SMEM)
PLACE = pl.BlockSpec(memory_space=pl.ANY)
LIMIT = 48 * 1024 * 1024

PAIRS = [(e, b) for b in range(1, NB) for e in range(b)]
PARENT, ALPHA, LATER, VALUE, OWN, SPARE = 0, 6, 12, 18, 22, 32


def call(kernel, out_shapes, in_specs, scratch=(), flops=0, moved=0, limit=LIMIT):
    many = isinstance(out_shapes, (list, tuple))
    return pl.pallas_call(
        kernel,
        out_shape=out_shapes,
        in_specs=in_specs,
        out_specs=[VMEM] * len(out_shapes) if many else VMEM,
        scratch_shapes=list(scratch),
        compiler_params=pltpu.CompilerParams(vmem_limit_bytes=limit),
        cost_estimate=pl.CostEstimate(flops=flops, bytes_accessed=moved, transcendentals=0),
    )


def high_dot(a, b):
    return lax.dot_general(a, b, (((1,), (0,)), ((), ())), precision=HIGH, preferred_element_type=F32)


def lane_take(value, row):
    where = jnp.broadcast_to(row, value.shape)
    return jnp.take_along_axis(value, where, axis=1, mode="promise_in_bounds")


def pick_kernel(shape, owner, *refs):
    slab, depth, block_cells, groups, count = shape
    out, arrivals = refs[4], refs[9]
    copies = [pltpu.make_async_copy(refs[i], refs[5 + i], arrivals.at[i]) for i in range(4)]
    for copy in copies:
        copy.start()
    for copy in copies:
        copy.wait()
    weights, offsets, ancestors, prior = refs[5:9]
    width = groups * count
    per = LANES // count
    for b in range(NB):
        start = pl.multiple_of(owner[b] * block_cells, LANES)
        levels = [prior[:, level, pl.ds(start, block_cells)] for level in range(depth)]
        for c in range(width // LANES):
            cell = jnp.concatenate([offsets[b, g : g + 1, :] for g in range(c * per, (c + 1) * per)], axis=1)
            low, high = lax.rem(cell, LANES), lax.div(cell, LANES)
            total = jnp.zeros((slab, LANES), F32)
            for level in range(depth):
                found = jnp.zeros((slab, LANES), F32)
                for h in range(block_cells // LANES):
                    part = lane_take(levels[level][:, h * LANES : (h + 1) * LANES], low)
                    found = jnp.where(high == h, part, found)
                row = jnp.concatenate(
                    [
                        jnp.broadcast_to(weights[level : level + 1, g : g + 1], (1, count))
                        for g in range(c * per, (c + 1) * per)
                    ],
                    axis=1,
                )
                total = total + found * row
            lane = b * width + c * LANES
            out[:, lane : lane + LANES] = total
    lane = NB * width
    out[:, lane:] = jnp.zeros((slab, out.shape[1] - lane), F32)
    for b in range(NB):
        row, block = b % slab, lane + (b // slab) * LANES
        out[row : row + 1, block : block + LANES] = ancestors[b].astype(F32)


def retile_kernel(shape, prior, out):
    n, slab, depth, block_cells = shape
    for r in range(n):
        for level in range(depth):
            out[r, level] = prior[:, level, r * block_cells : (r + 1) * block_cells]


def prep_kernel(shape, owner, offsets, values, errors, ancestors, rows, steps):
    block_cells, count, scale, members = shape
    block, group = lax.axis_index("grid"), lax.axis_index("lev")
    index = lax.broadcasted_iota(jnp.int32, (8, 1), 0)
    region = jnp.full((8, 1), block, jnp.int32)
    for b in range(1, NB):
        region = jnp.where(index == b - 1, owner[b], region)
    centre = region.astype(F32) + 0.5
    rows[...] = jnp.zeros((SPARE, LANES), F32)
    row = lax.broadcasted_iota(jnp.int32, (members, members), 0)
    column = lax.broadcasted_iota(jnp.int32, (members, members), 1)
    turned = (row == column).astype(F32)
    for b in range(NB):
        cells = owner[b] * block_cells + offsets[b, pl.ds(group, 1), :]
        distance = (centre - cells.astype(F32) / block_cells) / scale
        taper = jnp.exp(-0.5 * distance * distance)
        alpha = 0.8 * (1.0 - jnp.exp(-jnp.sum(taper, axis=1, keepdims=True) / count))
        error = errors[b]
        part = (-0.5 / count) * (taper / (error * error))
        for later in range(b + 1, NB):
            i = PAIRS.index((b, later))
            rows[ALPHA + i : ALPHA + i + 1, :] = jnp.broadcast_to(alpha[later - 1 : later], (1, LANES))
            rows[LATER + i : LATER + i + 1, :count] = part[later - 1 : later]
        rows[VALUE + b : VALUE + b + 1, :count] = values[b]
        rows[OWN + b : OWN + b + 1, :count] = part[NB - 1 : NB]
        steps[b] = turned.T
        own = alpha[NB - 1 : NB]
        turned = own * lane_take(turned, ancestors[b]) + (1.0 - own) * turned
    steps[NB] = turned.T


def turn_kernel(shape, owner, rows, *refs):
    n, slab, width = shape
    pieces, out, held = refs[:-2], refs[-2], refs[-1]
    members = n * slab
    if len(pieces) == 1:
        held[...] = pieces[0][...]
    else:
        block = lax.axis_index("grid")
        for i, piece in enumerate(pieces):
            held[lax.bitwise_xor(block, i)] = piece[...]
    for i in range(width // LANES):
        lanes = slice(i * LANES, (i + 1) * LANES)
        out[lanes, :] = held[:, :, lanes].reshape(members, LANES).T
    out[width:, :] = rows[...]
    for i, (e, b) in enumerate(PAIRS):
        lane = width + (e // slab) * LANES
        line = e % slab
        out[width + PARENT + i : width + PARENT + i + 1, :] = held[owner[b], line : line + 1, lane : lane + LANES]


def mix_kernel(shape, steps, fields, out):
    n, slab, depth, block_cells = shape
    for level in range(depth):
        value = fields[:, level].reshape(n * slab, block_cells)
        out[:, level] = high_dot(steps[NB], value).reshape(n, slab, block_cells)


def chain_kernel(shape, own, near, far, cross, steps, fields, out):
    n, slab, depth, block_cells, groups, count = shape
    members = n * slab
    width = groups * count
    base = NB * width
    group = lax.axis_index("lev")
    sources = [own, near, far, cross]
    columns = [source[base : base + SPARE, :].T for source in sources]
    parents, alphas = [], []
    for source in sources:
        parents.append(source[base + PARENT : base + PARENT + 8, :].astype(jnp.int32))
        alphas.append(source[base + ALPHA : base + ALPHA + 6, :])
    tilts = {}
    pulled = []
    for b in range(NB):
        kinds = [(q, later) for q in range(groups) for later in range(b + 1, NB)] + [(0, None)]
        height = -(-len(kinds) // 8) * 8
        index = lax.broadcasted_iota(jnp.int32, (height, members), 0)
        logs = jnp.zeros((height, members), F32)
        for q in range(groups if b < NB - 1 else 1):
            start = pl.multiple_of(b * width + lax.bitwise_xor(group, q) * count, count)
            total = jnp.zeros((count, members), F32)
            tilted = jnp.zeros((count, members), F32)
            for p, source in enumerate(sources):
                value = source[pl.ds(start, count), :]
                for e in range(b):
                    i = PAIRS.index((e, b))
                    tilted = tilted + value * tilts[e, p, b]
                    alpha = alphas[p][i : i + 1]
                    moved = lane_take(value, parents[p][i : i + 1])
                    value = alpha * moved + (1.0 - alpha) * value
                total = total + value
            if b > 0:
                total = total + jnp.sum(tilted, axis=1, keepdims=True)
            miss = columns[q][:count, VALUE + b : VALUE + b + 1] - total
            square = miss * miss
            for row, (owner_group, later) in enumerate(kinds):
                if owner_group != q:
                    continue
                at = OWN + b if later is None else LATER + PAIRS.index((b, later))
                log = jnp.sum(columns[q][:count, at : at + 1] * square, axis=0, keepdims=True)
                logs = jnp.where(index == row, log, logs)
        expo = jnp.exp(logs - jnp.max(logs, axis=1, keepdims=True))
        tilt = expo / jnp.sum(expo, axis=1, keepdims=True) - 1.0 / members
        for row, (q, later) in enumerate(kinds):
            if later is None:
                pulled.append(tilt[row : row + 1])
            else:
                tilts[b, q, later] = tilt[row : row + 1]
    pull = jnp.zeros((8, members), F32)
    for b in range(NB):
        pull = pull + high_dot(jnp.broadcast_to(pulled[b], (8, members)), steps[b])
    for level in range(depth):
        value = fields[:, level].reshape(members, block_cells)
        shift = high_dot(pull, value)[0:1]
        for d in range(n):
            out[d, level : level + 1, :] = shift


def final_kernel(shape, moved, shift, out):
    n, slab, depth, block_cells = shape
    for r in range(n):
        for level in range(depth):
            value = moved[r, level] + shift[r, level : level + 1, :]
            out[:, level, r * block_cells : (r + 1) * block_cells] = value


def gather_pieces(piece, n):
    if n != 8:
        return [lax.all_to_all(jnp.broadcast_to(piece[None], (n,) + piece.shape), "grid", 0, 0, tiled=True)]
    pieces = [piece]
    for far in (2, 4, 6):
        pieces.append(lax.ppermute(piece, "grid", [(j, j ^ far) for j in range(n)]))
    result = []
    for part in pieces:
        result += [part, lax.ppermute(part, "grid", [(j, j ^ 1) for j in range(n)])]
    return result


def body(prior, channel_weights, obs_owner, obs_offset, obs_value, obs_error, ancestors):
    n, lev = lax.axis_size("grid"), lax.axis_size("lev")
    slab, depth, cells = prior.shape
    members = slab * n
    block_cells = cells // n
    groups = channel_weights.shape[1]
    count = obs_offset.shape[2]
    width = NB * groups * count
    scale = n / 2.0
    shape = jax.ShapeDtypeStruct
    parents = ancestors[:, 0]
    wide = width + -(-NB // slab) * LANES

    piece = call(
        functools.partial(pick_kernel, (slab, depth, block_cells, groups, count)),
        shape((slab, wide), F32),
        [SMEM] + [PLACE] * 4,
        scratch=[
            pltpu.VMEM(channel_weights.shape, F32),
            pltpu.VMEM(obs_offset.shape, jnp.int32),
            pltpu.VMEM(parents.shape, jnp.int32),
            pltpu.VMEM(prior.shape, F32),
            pltpu.SemaphoreType.DMA((4,)),
        ],
        moved=10**6,
        limit=None,
    )(obs_owner, channel_weights, obs_offset, parents, prior)
    pieces = gather_pieces(piece, n)

    send = call(
        functools.partial(retile_kernel, (n, slab, depth, block_cells)),
        shape((n, depth, slab, block_cells), F32),
        [VMEM],
        moved=10**6,
    )(prior)
    fields = lax.all_to_all(send, "grid", 0, 0, tiled=True)

    rows, steps = call(
        functools.partial(prep_kernel, (block_cells, count, scale, members)),
        [shape((SPARE, LANES), F32), shape((NB + 1, members, members), F32)],
        [SMEM, VMEM, VMEM, VMEM, VMEM],
        moved=10**6,
    )(obs_owner, obs_offset, obs_value, obs_error, parents)

    own = call(
        functools.partial(turn_kernel, (n, slab, width)),
        shape((width + SPARE, members), F32),
        [SMEM] + [VMEM] * (1 + len(pieces)),
        scratch=[pltpu.VMEM((n, slab, wide), F32)],
        moved=10**6,
    )(obs_owner, rows, *pieces)
    ready, fields = lax.optimization_barrier((own, fields))
    far = lax.ppermute(ready, "lev", [(j, j ^ 2) for j in range(lev)])
    near = lax.ppermute(own, "lev", [(j, j ^ 1) for j in range(lev)])
    cross = lax.ppermute(far, "lev", [(j, j ^ 1) for j in range(lev)])

    send = call(
        functools.partial(mix_kernel, (n, slab, depth, block_cells)),
        shape((n, depth, slab, block_cells), F32),
        [VMEM, VMEM],
        flops=10**8,
        moved=10**6,
    )(steps, fields)
    moved = lax.all_to_all(send, "grid", 0, 0, tiled=True)

    send = call(
        functools.partial(chain_kernel, (n, slab, depth, block_cells, groups, count)),
        shape((n, depth, block_cells), F32),
        [VMEM] * 6,
        flops=10**9,
        moved=10**7,
    )(own, near, far, cross, steps, fields)
    send, moved = lax.optimization_barrier((send, moved))
    shift = lax.all_to_all(send, "grid", 0, 0, tiled=True)

    return call(
        functools.partial(final_kernel, (n, slab, depth, block_cells)),
        shape((slab, depth, cells), F32),
        [VMEM, VMEM],
        moved=10**6,
    )(moved, shift)


def solution(mesh):
    in_specs = (
        P("grid", "lev", None),
        P("lev", None),
        P(),
        P(),
        P(None, "lev", None),
        P(None, "lev", None),
        P(None, "lev", "grid", None),
    )
    out_specs = P("grid", "lev", None)
    return jax.shard_map(body, mesh=mesh, in_specs=in_specs, out_specs=out_specs, check_vma=False)
```

```python
import functools

import jax
import jax.numpy as jnp
from jax import lax
from jax.experimental import pallas as pl
from jax.experimental.pallas import tpu as pltpu
from jax.sharding import PartitionSpec as P

NB = 4
HIGH = lax.Precision.HIGHEST
LANES = 128
F32 = jnp.float32
VMEM = pl.BlockSpec(memory_space=pltpu.VMEM)
SMEM = pl.BlockSpec(memory_space=pltpu.SMEM)
PLACE = pl.BlockSpec(memory_space=pl.ANY)
LIMIT = 48 * 1024 * 1024

PAIRS = [(e, b) for b in range(1, NB) for e in range(b)]
PARENT, ALPHA, LATER, VALUE, OWN, SPARE = 0, 6, 12, 18, 22, 32


def call(kernel, out_shapes, in_specs, scratch=(), flops=0, moved=0, limit=LIMIT):
    many = isinstance(out_shapes, (list, tuple))
    return pl.pallas_call(
        kernel,
        out_shape=out_shapes,
        in_specs=in_specs,
        out_specs=[VMEM] * len(out_shapes) if many else VMEM,
        scratch_shapes=list(scratch),
        compiler_params=pltpu.CompilerParams(vmem_limit_bytes=limit),
        cost_estimate=pl.CostEstimate(flops=flops, bytes_accessed=moved, transcendentals=0),
    )


def high_dot(a, b):
    return lax.dot_general(a, b, (((1,), (0,)), ((), ())), precision=HIGH, preferred_element_type=F32)


def lane_take(value, row):
    where = jnp.broadcast_to(row, value.shape)
    return jnp.take_along_axis(value, where, axis=1, mode="promise_in_bounds")


def pick_kernel(shape, *refs):
    slab, depth, block_cells, groups, count = shape
    out, arrivals = refs[5], refs[11]
    copies = [pltpu.make_async_copy(refs[i], refs[6 + i], arrivals.at[i]) for i in range(5)]
    for copy in copies:
        copy.start()
    for copy in copies:
        copy.wait()
    owner, weights, offsets, ancestors, prior = refs[6:11]
    width = groups * count
    per = LANES // count
    for b in range(NB):
        start = pl.multiple_of(owner[b] * block_cells, LANES)
        levels = [prior[:, level, pl.ds(start, block_cells)] for level in range(depth)]
        for c in range(width // LANES):
            cell = jnp.concatenate([offsets[b, g : g + 1, :] for g in range(c * per, (c + 1) * per)], axis=1)
            low, high = lax.rem(cell, LANES), lax.div(cell, LANES)
            total = jnp.zeros((slab, LANES), F32)
            for level in range(depth):
                found = jnp.zeros((slab, LANES), F32)
                for h in range(block_cells // LANES):
                    part = lane_take(levels[level][:, h * LANES : (h + 1) * LANES], low)
                    found = jnp.where(high == h, part, found)
                row = jnp.concatenate(
                    [
                        jnp.broadcast_to(weights[level : level + 1, g : g + 1], (1, count))
                        for g in range(c * per, (c + 1) * per)
                    ],
                    axis=1,
                )
                total = total + found * row
            lane = b * width + c * LANES
            out[:, lane : lane + LANES] = total
    lane = NB * width
    out[:, lane:] = jnp.zeros((slab, out.shape[1] - lane), F32)
    for b in range(NB):
        row, block = b % slab, lane + (b // slab) * LANES
        out[row : row + 1, block : block + LANES] = ancestors[b].astype(F32)


def retile_kernel(shape, prior, after, out):
    n, slab, depth, block_cells = shape
    for r in range(n):
        for level in range(depth):
            out[r, level] = prior[:, level, r * block_cells : (r + 1) * block_cells]


def prep_kernel(shape, owner, offsets, values, errors, ancestors, rows, steps):
    block_cells, count, scale, members = shape
    block, group = lax.axis_index("grid"), lax.axis_index("lev")
    index = lax.broadcasted_iota(jnp.int32, (8, 1), 0)
    region = jnp.full((8, 1), block, jnp.int32)
    for b in range(1, NB):
        region = jnp.where(index == b - 1, owner[b], region)
    centre = region.astype(F32) + 0.5
    rows[...] = jnp.zeros((SPARE, LANES), F32)
    row = lax.broadcasted_iota(jnp.int32, (members, members), 0)
    column = lax.broadcasted_iota(jnp.int32, (members, members), 1)
    turned = (row == column).astype(F32)
    for b in range(NB):
        cells = owner[b] * block_cells + offsets[b, pl.ds(group, 1), :]
        distance = (centre - cells.astype(F32) / block_cells) / scale
        taper = jnp.exp(-0.5 * distance * distance)
        alpha = 0.8 * (1.0 - jnp.exp(-jnp.sum(taper, axis=1, keepdims=True) / count))
        error = errors[b]
        part = (-0.5 / count) * (taper / (error * error))
        for later in range(b + 1, NB):
            i = PAIRS.index((b, later))
            rows[ALPHA + i : ALPHA + i + 1, :] = jnp.broadcast_to(alpha[later - 1 : later], (1, LANES))
            rows[LATER + i : LATER + i + 1, :count] = part[later - 1 : later]
        rows[VALUE + b : VALUE + b + 1, :count] = values[b]
        rows[OWN + b : OWN + b + 1, :count] = part[NB - 1 : NB]
        steps[b] = turned.T
        own = alpha[NB - 1 : NB]
        turned = own * lane_take(turned, ancestors[b]) + (1.0 - own) * turned
    steps[NB] = turned.T


def turn_kernel(shape, owner, rows, *refs):
    n, slab, width = shape
    pieces, out, held = refs[:-2], refs[-2], refs[-1]
    members = n * slab
    if len(pieces) == 1:
        held[...] = pieces[0][...]
    else:
        block = lax.axis_index("grid")
        for i, piece in enumerate(pieces):
            held[lax.bitwise_xor(block, i)] = piece[...]
    for i in range(width // LANES):
        lanes = slice(i * LANES, (i + 1) * LANES)
        out[lanes, :] = held[:, :, lanes].reshape(members, LANES).T
    out[width:, :] = rows[...]
    for i, (e, b) in enumerate(PAIRS):
        lane = width + (e // slab) * LANES
        line = e % slab
        out[width + PARENT + i : width + PARENT + i + 1, :] = held[owner[b], line : line + 1, lane : lane + LANES]


def mix_kernel(shape, steps, fields, out):
    n, slab, depth, block_cells = shape
    for level in range(depth):
        value = fields[:, level].reshape(n * slab, block_cells)
        out[:, level] = high_dot(steps[NB], value).reshape(n, slab, block_cells)


def chain_kernel(shape, own, near, far, cross, steps, fields, out):
    n, slab, depth, block_cells, groups, count = shape
    members = n * slab
    width = groups * count
    base = NB * width
    group = lax.axis_index("lev")
    sources = [own, near, far, cross]
    columns = [source[base : base + SPARE, :].T for source in sources]
    parents, alphas = [], []
    for source in sources:
        parents.append(source[base + PARENT : base + PARENT + 8, :].astype(jnp.int32))
        alphas.append(source[base + ALPHA : base + ALPHA + 6, :])
    tilts = {}
    pulled = []
    for b in range(NB):
        kinds = [(q, later) for q in range(groups) for later in range(b + 1, NB)] + [(0, None)]
        height = -(-len(kinds) // 8) * 8
        index = lax.broadcasted_iota(jnp.int32, (height, members), 0)
        logs = jnp.zeros((height, members), F32)
        for q in range(groups if b < NB - 1 else 1):
            start = pl.multiple_of(b * width + lax.bitwise_xor(group, q) * count, count)
            total = jnp.zeros((count, members), F32)
            tilted = jnp.zeros((count, members), F32)
            for p, source in enumerate(sources):
                value = source[pl.ds(start, count), :]
                for e in range(b):
                    i = PAIRS.index((e, b))
                    tilted = tilted + value * tilts[e, p, b]
                    alpha = alphas[p][i : i + 1]
                    moved = lane_take(value, parents[p][i : i + 1])
                    value = alpha * moved + (1.0 - alpha) * value
                total = total + value
            if b > 0:
                total = total + jnp.sum(tilted, axis=1, keepdims=True)
            miss = columns[q][:count, VALUE + b : VALUE + b + 1] - total
            square = miss * miss
            for row, (owner_group, later) in enumerate(kinds):
                if owner_group != q:
                    continue
                at = OWN + b if later is None else LATER + PAIRS.index((b, later))
                log = jnp.sum(columns[q][:count, at : at + 1] * square, axis=0, keepdims=True)
                logs = jnp.where(index == row, log, logs)
        expo = jnp.exp(logs - jnp.max(logs, axis=1, keepdims=True))
        tilt = expo / jnp.sum(expo, axis=1, keepdims=True) - 1.0 / members
        for row, (q, later) in enumerate(kinds):
            if later is None:
                pulled.append(tilt[row : row + 1])
            else:
                tilts[b, q, later] = tilt[row : row + 1]
    pull = jnp.zeros((8, members), F32)
    for b in range(NB):
        pull = pull + high_dot(jnp.broadcast_to(pulled[b], (8, members)), steps[b])
    for level in range(depth):
        value = fields[:, level].reshape(members, block_cells)
        shift = high_dot(pull, value)[0:1]
        for d in range(n):
            out[d, level : level + 1, :] = shift


def final_kernel(shape, moved, shift, out):
    n, slab, depth, block_cells = shape
    for r in range(n):
        for level in range(depth):
            value = moved[r, level] + shift[r, level : level + 1, :]
            out[:, level, r * block_cells : (r + 1) * block_cells] = value


def gather_pieces(piece, n):
    if n != 8:
        return [lax.all_to_all(jnp.broadcast_to(piece[None], (n,) + piece.shape), "grid", 0, 0, tiled=True)]
    pieces = [piece]
    for far in (2, 4, 6):
        pieces.append(lax.ppermute(piece, "grid", [(j, j ^ far) for j in range(n)]))
    result = []
    for part in pieces:
        result += [part, lax.ppermute(part, "grid", [(j, j ^ 1) for j in range(n)])]
    return result


def body(prior, channel_weights, obs_owner, obs_offset, obs_value, obs_error, ancestors):
    n, lev = lax.axis_size("grid"), lax.axis_size("lev")
    slab, depth, cells = prior.shape
    members = slab * n
    block_cells = cells // n
    groups = channel_weights.shape[1]
    count = obs_offset.shape[2]
    width = NB * groups * count
    scale = n / 2.0
    shape = jax.ShapeDtypeStruct
    parents = ancestors[:, 0]
    wide = width + -(-NB // slab) * LANES

    piece = call(
        functools.partial(pick_kernel, (slab, depth, block_cells, groups, count)),
        shape((slab, wide), F32),
        [PLACE] * 5,
        scratch=[
            pltpu.SMEM(obs_owner.shape, jnp.int32),
            pltpu.VMEM(channel_weights.shape, F32),
            pltpu.VMEM(obs_offset.shape, jnp.int32),
            pltpu.VMEM(parents.shape, jnp.int32),
            pltpu.VMEM(prior.shape, F32),
            pltpu.SemaphoreType.DMA((5,)),
        ],
        moved=10**6,
        limit=None,
    )(obs_owner, channel_weights, obs_offset, parents, prior)
    pieces = gather_pieces(piece, n)

    send = call(
        functools.partial(retile_kernel, (n, slab, depth, block_cells)),
        shape((n, depth, slab, block_cells), F32),
        [VMEM, PLACE],
        moved=10**6,
    )(prior, pieces[min(2, len(pieces) - 1)])
    fields = lax.all_to_all(send, "grid", 0, 0, tiled=True)

    rows, steps = call(
        functools.partial(prep_kernel, (block_cells, count, scale, members)),
        [shape((SPARE, LANES), F32), shape((NB + 1, members, members), F32)],
        [SMEM, VMEM, VMEM, VMEM, VMEM],
        moved=10**6,
    )(obs_owner, obs_offset, obs_value, obs_error, parents)

    own = call(
        functools.partial(turn_kernel, (n, slab, width)),
        shape((width + SPARE, members), F32),
        [SMEM] + [VMEM] * (1 + len(pieces)),
        scratch=[pltpu.VMEM((n, slab, wide), F32)],
        moved=10**6,
    )(obs_owner, rows, *pieces)
    far = lax.ppermute(own, "lev", [(j, j ^ 2) for j in range(lev)])
    near = lax.ppermute(own, "lev", [(j, j ^ 1) for j in range(lev)])
    cross = lax.ppermute(far, "lev", [(j, j ^ 1) for j in range(lev)])

    send = call(
        functools.partial(mix_kernel, (n, slab, depth, block_cells)),
        shape((n, depth, slab, block_cells), F32),
        [VMEM, VMEM],
        flops=10**8,
        moved=10**6,
    )(steps, fields)
    moved = lax.all_to_all(send, "grid", 0, 0, tiled=True)

    send = call(
        functools.partial(chain_kernel, (n, slab, depth, block_cells, groups, count)),
        shape((n, depth, block_cells), F32),
        [VMEM] * 6,
        flops=10**9,
        moved=10**7,
    )(own, near, far, cross, steps, fields)
    send, moved = lax.optimization_barrier((send, moved))
    shift = lax.all_to_all(send, "grid", 0, 0, tiled=True)

    return call(
        functools.partial(final_kernel, (n, slab, depth, block_cells)),
        shape((slab, depth, cells), F32),
        [VMEM, VMEM],
        moved=10**6,
    )(moved, shift)


def solution(mesh):
    in_specs = (
        P("grid", "lev", None),
        P("lev", None),
        P(),
        P(),
        P(None, "lev", None),
        P(None, "lev", None),
        P(None, "lev", "grid", None),
    )
    out_specs = P("grid", "lev", None)
    return jax.shard_map(body, mesh=mesh, in_specs=in_specs, out_specs=out_specs, check_vma=False)
```

```python
import functools

import jax
import jax.numpy as jnp
from jax import lax
from jax.experimental import pallas as pl
from jax.experimental.pallas import tpu as pltpu
from jax.sharding import PartitionSpec as P

NB = 4
HIGH = lax.Precision.HIGHEST
LANES = 128
F32 = jnp.float32
VMEM = pl.BlockSpec(memory_space=pltpu.VMEM)
SMEM = pl.BlockSpec(memory_space=pltpu.SMEM)
PLACE = pl.BlockSpec(memory_space=pl.ANY)
LIMIT = 48 * 1024 * 1024

PAIRS = [(e, b) for b in range(1, NB) for e in range(b)]
PARENT, ALPHA, LATER, VALUE, OWN, SPARE = 0, 6, 12, 18, 22, 32


def call(kernel, out_shapes, in_specs, scratch=(), flops=0, moved=0, limit=LIMIT):
    many = isinstance(out_shapes, (list, tuple))
    return pl.pallas_call(
        kernel,
        out_shape=out_shapes,
        in_specs=in_specs,
        out_specs=[VMEM] * len(out_shapes) if many else VMEM,
        scratch_shapes=list(scratch),
        compiler_params=pltpu.CompilerParams(vmem_limit_bytes=limit),
        cost_estimate=pl.CostEstimate(flops=flops, bytes_accessed=moved, transcendentals=0),
    )


def high_dot(a, b):
    return lax.dot_general(a, b, (((1,), (0,)), ((), ())), precision=HIGH, preferred_element_type=F32)


def lane_take(value, row):
    where = jnp.broadcast_to(row, value.shape)
    return jnp.take_along_axis(value, where, axis=1, mode="promise_in_bounds")


def pick_kernel(shape, *refs):
    slab, depth, block_cells, groups, count = shape
    out, arrivals = refs[5], refs[11]
    copies = [pltpu.make_async_copy(refs[i], refs[6 + i], arrivals.at[i]) for i in range(5)]
    for copy in copies:
        copy.start()
    for copy in copies:
        copy.wait()
    owner, weights, offsets, ancestors, prior = refs[6:11]
    width = groups * count
    per = LANES // count
    for b in range(NB):
        start = pl.multiple_of(owner[b] * block_cells, LANES)
        levels = [prior[:, level, pl.ds(start, block_cells)] for level in range(depth)]
        for c in range(width // LANES):
            cell = jnp.concatenate([offsets[b, g : g + 1, :] for g in range(c * per, (c + 1) * per)], axis=1)
            low, high = lax.rem(cell, LANES), lax.div(cell, LANES)
            total = jnp.zeros((slab, LANES), F32)
            for level in range(depth):
                found = jnp.zeros((slab, LANES), F32)
                for h in range(block_cells // LANES):
                    part = lane_take(levels[level][:, h * LANES : (h + 1) * LANES], low)
                    found = jnp.where(high == h, part, found)
                row = jnp.concatenate(
                    [
                        jnp.broadcast_to(weights[level : level + 1, g : g + 1], (1, count))
                        for g in range(c * per, (c + 1) * per)
                    ],
                    axis=1,
                )
                total = total + found * row
            lane = b * width + c * LANES
            out[:, lane : lane + LANES] = total
    lane = NB * width
    out[:, lane:] = jnp.zeros((slab, out.shape[1] - lane), F32)
    for b in range(NB):
        row, block = b % slab, lane + (b // slab) * LANES
        out[row : row + 1, block : block + LANES] = ancestors[b].astype(F32)


def retile_kernel(shape, prior, out):
    n, slab, depth, block_cells = shape
    for r in range(n):
        for level in range(depth):
            out[r, level] = prior[:, level, r * block_cells : (r + 1) * block_cells]


def prep_kernel(shape, owner, offsets, values, errors, ancestors, rows, steps):
    block_cells, count, scale, members = shape
    block, group = lax.axis_index("grid"), lax.axis_index("lev")
    index = lax.broadcasted_iota(jnp.int32, (8, 1), 0)
    region = jnp.full((8, 1), block, jnp.int32)
    for b in range(1, NB):
        region = jnp.where(index == b - 1, owner[b], region)
    centre = region.astype(F32) + 0.5
    rows[...] = jnp.zeros((SPARE, LANES), F32)
    row = lax.broadcasted_iota(jnp.int32, (members, members), 0)
    column = lax.broadcasted_iota(jnp.int32, (members, members), 1)
    turned = (row == column).astype(F32)
    for b in range(NB):
        cells = owner[b] * block_cells + offsets[b, pl.ds(group, 1), :]
        distance = (centre - cells.astype(F32) / block_cells) / scale
        taper = jnp.exp(-0.5 * distance * distance)
        alpha = 0.8 * (1.0 - jnp.exp(-jnp.sum(taper, axis=1, keepdims=True) / count))
        error = errors[b]
        part = (-0.5 / count) * (taper / (error * error))
        for later in range(b + 1, NB):
            i = PAIRS.index((b, later))
            rows[ALPHA + i : ALPHA + i + 1, :] = jnp.broadcast_to(alpha[later - 1 : later], (1, LANES))
            rows[LATER + i : LATER + i + 1, :count] = part[later - 1 : later]
        rows[VALUE + b : VALUE + b + 1, :count] = values[b]
        rows[OWN + b : OWN + b + 1, :count] = part[NB - 1 : NB]
        steps[b] = turned.T
        own = alpha[NB - 1 : NB]
        turned = own * lane_take(turned, ancestors[b]) + (1.0 - own) * turned
    steps[NB] = turned.T


def turn_kernel(shape, owner, rows, ahead, *refs):
    n, slab, width = shape
    pieces, out, held = refs[:-2], refs[-2], refs[-1]
    members = n * slab
    if len(pieces) == 1:
        held[...] = pieces[0][...]
    else:
        block = lax.axis_index("grid")
        for i, piece in enumerate(pieces):
            held[lax.bitwise_xor(block, i)] = piece[...]
    for i in range(width // LANES):
        lanes = slice(i * LANES, (i + 1) * LANES)
        out[lanes, :] = held[:, :, lanes].reshape(members, LANES).T
    out[width:, :] = rows[...]
    for i, (e, b) in enumerate(PAIRS):
        lane = width + (e // slab) * LANES
        line = e % slab
        out[width + PARENT + i : width + PARENT + i + 1, :] = held[owner[b], line : line + 1, lane : lane + LANES]


def mix_kernel(shape, steps, pull, fields, out):
    n, slab, depth, block_cells = shape
    blend = steps[NB] + pull[0:1, :]
    for level in range(depth):
        value = fields[:, level].reshape(n * slab, block_cells)
        out[:, level] = high_dot(blend, value).reshape(n, slab, block_cells)


def chain_kernel(shape, own, near, far, cross, steps, out):
    members, groups, count = shape
    width = groups * count
    base = NB * width
    group = lax.axis_index("lev")
    sources = [own, near, far, cross]
    columns = [source[base : base + SPARE, :].T for source in sources]
    parents, alphas = [], []
    for source in sources:
        parents.append(source[base + PARENT : base + PARENT + 8, :].astype(jnp.int32))
        alphas.append(source[base + ALPHA : base + ALPHA + 6, :])
    tilts = {}
    pulled = []
    for b in range(NB):
        kinds = [(q, later) for q in range(groups) for later in range(b + 1, NB)] + [(0, None)]
        height = -(-len(kinds) // 8) * 8
        index = lax.broadcasted_iota(jnp.int32, (height, members), 0)
        logs = jnp.zeros((height, members), F32)
        for q in range(groups if b < NB - 1 else 1):
            start = pl.multiple_of(b * width + lax.bitwise_xor(group, q) * count, count)
            total = jnp.zeros((count, members), F32)
            tilted = jnp.zeros((count, members), F32)
            for p, source in enumerate(sources):
                value = source[pl.ds(start, count), :]
                for e in range(b):
                    i = PAIRS.index((e, b))
                    tilted = tilted + value * tilts[e, p, b]
                    alpha = alphas[p][i : i + 1]
                    moved = lane_take(value, parents[p][i : i + 1])
                    value = alpha * moved + (1.0 - alpha) * value
                total = total + value
            if b > 0:
                total = total + jnp.sum(tilted, axis=1, keepdims=True)
            miss = columns[q][:count, VALUE + b : VALUE + b + 1] - total
            square = miss * miss
            for row, (owner_group, later) in enumerate(kinds):
                if owner_group != q:
                    continue
                at = OWN + b if later is None else LATER + PAIRS.index((b, later))
                log = jnp.sum(columns[q][:count, at : at + 1] * square, axis=0, keepdims=True)
                logs = jnp.where(index == row, log, logs)
        expo = jnp.exp(logs - jnp.max(logs, axis=1, keepdims=True))
        tilt = expo / jnp.sum(expo, axis=1, keepdims=True) - 1.0 / members
        for row, (q, later) in enumerate(kinds):
            if later is None:
                pulled.append(tilt[row : row + 1])
            else:
                tilts[b, q, later] = tilt[row : row + 1]
    pull = jnp.zeros((8, members), F32)
    for b in range(NB):
        pull = pull + high_dot(jnp.broadcast_to(pulled[b], (8, members)), steps[b])
    out[...] = pull


def final_kernel(shape, moved, out):
    n, slab, depth, block_cells = shape
    for r in range(n):
        for level in range(depth):
            out[:, level, r * block_cells : (r + 1) * block_cells] = moved[r, level]


def gather_pieces(piece, n):
    if n != 8:
        return [lax.all_to_all(jnp.broadcast_to(piece[None], (n,) + piece.shape), "grid", 0, 0, tiled=True)]
    pieces = [piece]
    for far in (2, 4, 6):
        pieces.append(lax.ppermute(piece, "grid", [(j, j ^ far) for j in range(n)]))
    result = []
    for part in pieces:
        result += [part, lax.ppermute(part, "grid", [(j, j ^ 1) for j in range(n)])]
    return result


def body(prior, channel_weights, obs_owner, obs_offset, obs_value, obs_error, ancestors):
    n, lev = lax.axis_size("grid"), lax.axis_size("lev")
    slab, depth, cells = prior.shape
    members = slab * n
    block_cells = cells // n
    groups = channel_weights.shape[1]
    count = obs_offset.shape[2]
    width = NB * groups * count
    scale = n / 2.0
    shape = jax.ShapeDtypeStruct
    parents = ancestors[:, 0]
    wide = width + -(-NB // slab) * LANES

    piece = call(
        functools.partial(pick_kernel, (slab, depth, block_cells, groups, count)),
        shape((slab, wide), F32),
        [PLACE] * 5,
        scratch=[
            pltpu.SMEM(obs_owner.shape, jnp.int32),
            pltpu.VMEM(channel_weights.shape, F32),
            pltpu.VMEM(obs_offset.shape, jnp.int32),
            pltpu.VMEM(parents.shape, jnp.int32),
            pltpu.VMEM(prior.shape, F32),
            pltpu.SemaphoreType.DMA((5,)),
        ],
        moved=10**6,
        limit=None,
    )(obs_owner, channel_weights, obs_offset, parents, prior)
    pieces = gather_pieces(piece, n)

    send = call(
        functools.partial(retile_kernel, (n, slab, depth, block_cells)),
        shape((n, depth, slab, block_cells), F32),
        [VMEM],
        moved=10**6,
    )(prior)
    fields = lax.all_to_all(send, "grid", 0, 0, tiled=True)

    rows, steps = call(
        functools.partial(prep_kernel, (block_cells, count, scale, members)),
        [shape((SPARE, LANES), F32), shape((NB + 1, members, members), F32)],
        [SMEM, VMEM, VMEM, VMEM, VMEM],
        moved=10**6,
    )(obs_owner, obs_offset, obs_value, obs_error, parents)

    own = call(
        functools.partial(turn_kernel, (n, slab, width)),
        shape((width + SPARE, members), F32),
        [SMEM, VMEM, PLACE] + [VMEM] * len(pieces),
        scratch=[pltpu.VMEM((n, slab, wide), F32)],
        moved=10**6,
    )(obs_owner, rows, send, *pieces)
    far = lax.ppermute(own, "lev", [(j, j ^ 2) for j in range(lev)])
    near = lax.ppermute(own, "lev", [(j, j ^ 1) for j in range(lev)])
    cross = lax.ppermute(far, "lev", [(j, j ^ 1) for j in range(lev)])

    pull = call(
        functools.partial(chain_kernel, (members, groups, count)),
        shape((8, members), F32),
        [VMEM] * 5,
        moved=10**5,
    )(own, near, far, cross, steps)

    send = call(
        functools.partial(mix_kernel, (n, slab, depth, block_cells)),
        shape((n, depth, slab, block_cells), F32),
        [VMEM] * 3,
        flops=10**8,
        moved=10**6,
    )(steps, pull, fields)
    moved = lax.all_to_all(send, "grid", 0, 0, tiled=True)

    return call(
        functools.partial(final_kernel, (n, slab, depth, block_cells)),
        shape((slab, depth, cells), F32),
        [VMEM],
        moved=10**6,
    )(moved)


def solution(mesh):
    in_specs = (
        P("grid", "lev", None),
        P("lev", None),
        P(),
        P(),
        P(None, "lev", None),
        P(None, "lev", None),
        P(None, "lev", "grid", None),
    )
    out_specs = P("grid", "lev", None)
    return jax.shard_map(body, mesh=mesh, in_specs=in_specs, out_specs=out_specs, check_vma=False)
```

```python
import functools

import jax
import jax.numpy as jnp
from jax import lax
from jax.experimental import pallas as pl
from jax.experimental.pallas import tpu as pltpu
from jax.sharding import PartitionSpec as P

NB = 4
HIGH = lax.Precision.HIGHEST
LANES = 128
F32 = jnp.float32
VMEM = pl.BlockSpec(memory_space=pltpu.VMEM)
SMEM = pl.BlockSpec(memory_space=pltpu.SMEM)
PLACE = pl.BlockSpec(memory_space=pl.ANY)
LIMIT = 48 * 1024 * 1024

PAIRS = [(e, b) for b in range(1, NB) for e in range(b)]
PARENT, ALPHA, LATER, VALUE, OWN, SPARE = 0, 6, 12, 18, 22, 32


def call(kernel, out_shapes, in_specs, scratch=(), flops=0, moved=0, limit=LIMIT):
    many = isinstance(out_shapes, (list, tuple))
    return pl.pallas_call(
        kernel,
        out_shape=out_shapes,
        in_specs=in_specs,
        out_specs=[VMEM] * len(out_shapes) if many else VMEM,
        scratch_shapes=list(scratch),
        compiler_params=pltpu.CompilerParams(vmem_limit_bytes=limit),
        cost_estimate=pl.CostEstimate(flops=flops, bytes_accessed=moved, transcendentals=0),
    )


def high_dot(a, b):
    return lax.dot_general(a, b, (((1,), (0,)), ((), ())), precision=HIGH, preferred_element_type=F32)


def lane_take(value, row):
    where = jnp.broadcast_to(row, value.shape)
    return jnp.take_along_axis(value, where, axis=1, mode="promise_in_bounds")


def pick_kernel(shape, *refs):
    slab, depth, block_cells, groups, count = shape
    out, arrivals = refs[5], refs[11]
    copies = [pltpu.make_async_copy(refs[i], refs[6 + i], arrivals.at[i]) for i in range(5)]
    for copy in copies:
        copy.start()
    for copy in copies:
        copy.wait()
    owner, weights, offsets, ancestors, prior = refs[6:11]
    width = groups * count
    per = LANES // count
    for b in range(NB):
        start = pl.multiple_of(owner[b] * block_cells, LANES)
        levels = [prior[:, level, pl.ds(start, block_cells)] for level in range(depth)]
        for c in range(width // LANES):
            cell = jnp.concatenate([offsets[b, g : g + 1, :] for g in range(c * per, (c + 1) * per)], axis=1)
            low, high = lax.rem(cell, LANES), lax.div(cell, LANES)
            total = jnp.zeros((slab, LANES), F32)
            for level in range(depth):
                found = jnp.zeros((slab, LANES), F32)
                for h in range(block_cells // LANES):
                    part = lane_take(levels[level][:, h * LANES : (h + 1) * LANES], low)
                    found = jnp.where(high == h, part, found)
                row = jnp.concatenate(
                    [
                        jnp.broadcast_to(weights[level : level + 1, g : g + 1], (1, count))
                        for g in range(c * per, (c + 1) * per)
                    ],
                    axis=1,
                )
                total = total + found * row
            lane = b * width + c * LANES
            out[:, lane : lane + LANES] = total
    lane = NB * width
    out[:, lane:] = jnp.zeros((slab, out.shape[1] - lane), F32)
    for b in range(NB):
        row, block = b % slab, lane + (b // slab) * LANES
        out[row : row + 1, block : block + LANES] = ancestors[b].astype(F32)


def retile_kernel(shape, prior, out):
    n, slab, depth, block_cells = shape
    for r in range(n):
        for level in range(depth):
            out[r, level] = prior[:, level, r * block_cells : (r + 1) * block_cells]


def prep_kernel(shape, owner, offsets, values, errors, ancestors, rows, steps):
    block_cells, count, scale, members = shape
    block, group = lax.axis_index("grid"), lax.axis_index("lev")
    index = lax.broadcasted_iota(jnp.int32, (8, 1), 0)
    region = jnp.full((8, 1), block, jnp.int32)
    for b in range(1, NB):
        region = jnp.where(index == b - 1, owner[b], region)
    centre = region.astype(F32) + 0.5
    rows[...] = jnp.zeros((SPARE, LANES), F32)
    row = lax.broadcasted_iota(jnp.int32, (members, members), 0)
    column = lax.broadcasted_iota(jnp.int32, (members, members), 1)
    turned = (row == column).astype(F32)
    for b in range(NB):
        cells = owner[b] * block_cells + offsets[b, pl.ds(group, 1), :]
        distance = (centre - cells.astype(F32) / block_cells) / scale
        taper = jnp.exp(-0.5 * distance * distance)
        alpha = 0.8 * (1.0 - jnp.exp(-jnp.sum(taper, axis=1, keepdims=True) / count))
        error = errors[b]
        part = (-0.5 / count) * (taper / (error * error))
        for later in range(b + 1, NB):
            i = PAIRS.index((b, later))
            rows[ALPHA + i : ALPHA + i + 1, :] = jnp.broadcast_to(alpha[later - 1 : later], (1, LANES))
            rows[LATER + i : LATER + i + 1, :count] = part[later - 1 : later]
        rows[VALUE + b : VALUE + b + 1, :count] = values[b]
        rows[OWN + b : OWN + b + 1, :count] = part[NB - 1 : NB]
        steps[b] = turned.T
        own = alpha[NB - 1 : NB]
        turned = own * lane_take(turned, ancestors[b]) + (1.0 - own) * turned
    steps[NB] = turned.T


def turn_kernel(shape, owner, rows, ahead, *refs):
    n, slab, width = shape
    pieces, out, held = refs[:-2], refs[-2], refs[-1]
    members = n * slab
    if len(pieces) == 1:
        held[...] = pieces[0][...]
    else:
        block = lax.axis_index("grid")
        for i, piece in enumerate(pieces):
            held[lax.bitwise_xor(block, i)] = piece[...]
    for i in range(width // LANES):
        lanes = slice(i * LANES, (i + 1) * LANES)
        out[lanes, :] = held[:, :, lanes].reshape(members, LANES).T
    out[width:, :] = rows[...]
    for i, (e, b) in enumerate(PAIRS):
        lane = width + (e // slab) * LANES
        line = e % slab
        out[width + PARENT + i : width + PARENT + i + 1, :] = held[owner[b], line : line + 1, lane : lane + LANES]


def mix_kernel(shape, steps, pull, fields, *refs):
    n, slab, depth, block_cells = shape
    outs, held = refs[:-1], refs[-1]
    members = n * slab
    held[...] = (steps[NB] + pull[0:1, :]).reshape(n, slab, members)
    block = lax.axis_index("grid")
    if len(outs) == n:
        blend = jnp.concatenate([held[lax.bitwise_xor(block, i)] for i in range(n)], axis=0)
    else:
        blend = held[...].reshape(members, members)
    for level in range(depth):
        value = high_dot(blend, fields[:, level].reshape(members, block_cells)).reshape(n, slab, block_cells)
        if len(outs) == n:
            for i in range(n):
                outs[i][level] = value[i]
        else:
            outs[0][:, level] = value


def chain_kernel(shape, own, near, far, cross, steps, out):
    members, groups, count = shape
    width = groups * count
    base = NB * width
    group = lax.axis_index("lev")
    sources = [own, near, far, cross]
    columns = [source[base : base + SPARE, :].T for source in sources]
    parents, alphas = [], []
    for source in sources:
        parents.append(source[base + PARENT : base + PARENT + 8, :].astype(jnp.int32))
        alphas.append(source[base + ALPHA : base + ALPHA + 6, :])
    tilts = {}
    pulled = []
    for b in range(NB):
        kinds = [(q, later) for q in range(groups) for later in range(b + 1, NB)] + [(0, None)]
        height = -(-len(kinds) // 8) * 8
        index = lax.broadcasted_iota(jnp.int32, (height, members), 0)
        logs = jnp.zeros((height, members), F32)
        for q in range(groups if b < NB - 1 else 1):
            start = pl.multiple_of(b * width + lax.bitwise_xor(group, q) * count, count)
            total = jnp.zeros((count, members), F32)
            tilted = jnp.zeros((count, members), F32)
            for p, source in enumerate(sources):
                value = source[pl.ds(start, count), :]
                for e in range(b):
                    i = PAIRS.index((e, b))
                    tilted = tilted + value * tilts[e, p, b]
                    alpha = alphas[p][i : i + 1]
                    moved = lane_take(value, parents[p][i : i + 1])
                    value = alpha * moved + (1.0 - alpha) * value
                total = total + value
            if b > 0:
                total = total + jnp.sum(tilted, axis=1, keepdims=True)
            miss = columns[q][:count, VALUE + b : VALUE + b + 1] - total
            square = miss * miss
            for row, (owner_group, later) in enumerate(kinds):
                if owner_group != q:
                    continue
                at = OWN + b if later is None else LATER + PAIRS.index((b, later))
                log = jnp.sum(columns[q][:count, at : at + 1] * square, axis=0, keepdims=True)
                logs = jnp.where(index == row, log, logs)
        expo = jnp.exp(logs - jnp.max(logs, axis=1, keepdims=True))
        tilt = expo / jnp.sum(expo, axis=1, keepdims=True) - 1.0 / members
        for row, (q, later) in enumerate(kinds):
            if later is None:
                pulled.append(tilt[row : row + 1])
            else:
                tilts[b, q, later] = tilt[row : row + 1]
    pull = jnp.zeros((8, members), F32)
    for b in range(NB):
        pull = pull + high_dot(jnp.broadcast_to(pulled[b], (8, members)), steps[b])
    out[...] = pull


def final_kernel(shape, *refs):
    n, slab, depth, block_cells = shape
    pieces, out = refs[:-1], refs[-1]
    block = lax.axis_index("grid")
    for i in range(n):
        region = lax.bitwise_xor(block, i) if len(pieces) == n else i
        cells = pl.ds(pl.multiple_of(region * block_cells, LANES), block_cells)
        for level in range(depth):
            out[:, level, cells] = pieces[i][level] if len(pieces) == n else pieces[0][i, level]


def gather_pieces(piece, n):
    if n != 8:
        return [lax.all_to_all(jnp.broadcast_to(piece[None], (n,) + piece.shape), "grid", 0, 0, tiled=True)]
    pieces = [piece]
    for far in (2, 4, 6):
        pieces.append(lax.ppermute(piece, "grid", [(j, j ^ far) for j in range(n)]))
    result = []
    for part in pieces:
        result += [part, lax.ppermute(part, "grid", [(j, j ^ 1) for j in range(n)])]
    return result


def exchange_pieces(pieces, n):
    if len(pieces) == 1:
        return [lax.all_to_all(pieces[0], "grid", 0, 0, tiled=True)]
    return [pieces[0]] + [
        lax.ppermute(pieces[i], "grid", [(j, j ^ i) for j in range(n)]) for i in range(1, n)
    ]


def body(prior, channel_weights, obs_owner, obs_offset, obs_value, obs_error, ancestors):
    n, lev = lax.axis_size("grid"), lax.axis_size("lev")
    slab, depth, cells = prior.shape
    members = slab * n
    block_cells = cells // n
    groups = channel_weights.shape[1]
    count = obs_offset.shape[2]
    width = NB * groups * count
    scale = n / 2.0
    shape = jax.ShapeDtypeStruct
    parents = ancestors[:, 0]
    wide = width + -(-NB // slab) * LANES

    piece = call(
        functools.partial(pick_kernel, (slab, depth, block_cells, groups, count)),
        shape((slab, wide), F32),
        [PLACE] * 5,
        scratch=[
            pltpu.SMEM(obs_owner.shape, jnp.int32),
            pltpu.VMEM(channel_weights.shape, F32),
            pltpu.VMEM(obs_offset.shape, jnp.int32),
            pltpu.VMEM(parents.shape, jnp.int32),
            pltpu.VMEM(prior.shape, F32),
            pltpu.SemaphoreType.DMA((5,)),
        ],
        moved=10**6,
        limit=None,
    )(obs_owner, channel_weights, obs_offset, parents, prior)
    pieces = gather_pieces(piece, n)

    send = call(
        functools.partial(retile_kernel, (n, slab, depth, block_cells)),
        shape((n, depth, slab, block_cells), F32),
        [VMEM],
        moved=10**6,
    )(prior)
    fields = lax.all_to_all(send, "grid", 0, 0, tiled=True)

    rows, steps = call(
        functools.partial(prep_kernel, (block_cells, count, scale, members)),
        [shape((SPARE, LANES), F32), shape((NB + 1, members, members), F32)],
        [SMEM, VMEM, VMEM, VMEM, VMEM],
        moved=10**6,
    )(obs_owner, obs_offset, obs_value, obs_error, parents)

    own = call(
        functools.partial(turn_kernel, (n, slab, width)),
        shape((width + SPARE, members), F32),
        [SMEM, VMEM, PLACE] + [VMEM] * len(pieces),
        scratch=[pltpu.VMEM((n, slab, wide), F32)],
        moved=10**6,
    )(obs_owner, rows, send, *pieces)
    far = lax.ppermute(own, "lev", [(j, j ^ 2) for j in range(lev)])
    near = lax.ppermute(own, "lev", [(j, j ^ 1) for j in range(lev)])
    cross = lax.ppermute(far, "lev", [(j, j ^ 1) for j in range(lev)])

    pull = call(
        functools.partial(chain_kernel, (members, groups, count)),
        shape((8, members), F32),
        [VMEM] * 5,
        moved=10**5,
    )(own, near, far, cross, steps)

    if n == 8:
        layout = [shape((depth, slab, block_cells), F32)] * n
    else:
        layout = [shape((n, depth, slab, block_cells), F32)]
    send = call(
        functools.partial(mix_kernel, (n, slab, depth, block_cells)),
        layout,
        [VMEM] * 3,
        scratch=[pltpu.VMEM((n, slab, members), F32)],
        flops=10**8,
        moved=10**6,
    )(steps, pull, fields)
    moved = exchange_pieces(send, n)

    return call(
        functools.partial(final_kernel, (n, slab, depth, block_cells)),
        shape((slab, depth, cells), F32),
        [VMEM] * len(moved),
        moved=10**6,
    )(*moved)


def solution(mesh):
    in_specs = (
        P("grid", "lev", None),
        P("lev", None),
        P(),
        P(),
        P(None, "lev", None),
        P(None, "lev", None),
        P(None, "lev", "grid", None),
    )
    out_specs = P("grid", "lev", None)
    return jax.shard_map(body, mesh=mesh, in_specs=in_specs, out_specs=out_specs, check_vma=False)
```

```python
import functools

import jax
import jax.numpy as jnp
from jax import lax
from jax.experimental import pallas as pl
from jax.experimental.pallas import tpu as pltpu
from jax.sharding import PartitionSpec as P

NB = 4
HIGH = lax.Precision.HIGHEST
LANES = 128
F32 = jnp.float32
VMEM = pl.BlockSpec(memory_space=pltpu.VMEM)
SMEM = pl.BlockSpec(memory_space=pltpu.SMEM)
PLACE = pl.BlockSpec(memory_space=pl.ANY)
LIMIT = 48 * 1024 * 1024

ORDER = (0, 6, 4, 7, 5, 2, 3, 1)
PAIRS = [(e, b) for b in range(1, NB) for e in range(b)]
PARENT, ALPHA, LATER, VALUE, OWN, SPARE = 0, 6, 12, 18, 22, 32


def call(kernel, out_shapes, in_specs, scratch=(), flops=0, moved=0, limit=LIMIT):
    many = isinstance(out_shapes, (list, tuple))
    return pl.pallas_call(
        kernel,
        out_shape=out_shapes,
        in_specs=in_specs,
        out_specs=[VMEM] * len(out_shapes) if many else VMEM,
        scratch_shapes=list(scratch),
        compiler_params=pltpu.CompilerParams(vmem_limit_bytes=limit),
        cost_estimate=pl.CostEstimate(flops=flops, bytes_accessed=moved, transcendentals=0),
    )


def high_dot(a, b):
    return lax.dot_general(a, b, (((1,), (0,)), ((), ())), precision=HIGH, preferred_element_type=F32)


def lane_take(value, row):
    where = jnp.broadcast_to(row, value.shape)
    return jnp.take_along_axis(value, where, axis=1, mode="promise_in_bounds")


def pick_kernel(shape, *refs):
    slab, depth, block_cells, groups, count = shape
    out, arrivals = refs[5], refs[11]
    copies = [pltpu.make_async_copy(refs[i], refs[6 + i], arrivals.at[i]) for i in range(5)]
    for copy in copies:
        copy.start()
    for copy in copies:
        copy.wait()
    owner, weights, offsets, ancestors, prior = refs[6:11]
    width = groups * count
    per = LANES // count
    for b in range(NB):
        start = pl.multiple_of(owner[b] * block_cells, LANES)
        levels = [prior[:, level, pl.ds(start, block_cells)] for level in range(depth)]
        for c in range(width // LANES):
            cell = jnp.concatenate([offsets[b, g : g + 1, :] for g in range(c * per, (c + 1) * per)], axis=1)
            low, high = lax.rem(cell, LANES), lax.div(cell, LANES)
            total = jnp.zeros((slab, LANES), F32)
            for level in range(depth):
                found = jnp.zeros((slab, LANES), F32)
                for h in range(block_cells // LANES):
                    part = lane_take(levels[level][:, h * LANES : (h + 1) * LANES], low)
                    found = jnp.where(high == h, part, found)
                row = jnp.concatenate(
                    [
                        jnp.broadcast_to(weights[level : level + 1, g : g + 1], (1, count))
                        for g in range(c * per, (c + 1) * per)
                    ],
                    axis=1,
                )
                total = total + found * row
            line = (b * width // LANES + c) * slab
            out[line : line + slab, :] = total
    line = NB * width // LANES * slab
    out[line:, :] = jnp.zeros((out.shape[0] - line, LANES), F32)
    for b in range(NB):
        out[line + b : line + b + 1, :] = ancestors[b].astype(F32)


def join_kernel(own, far, out):
    out[0] = own[...]
    out[1] = far[...]


def retile_kernel(shape, prior, out):
    n, slab, depth, block_cells = shape
    for r in range(n):
        for level in range(depth):
            out[r, level] = prior[:, level, r * block_cells : (r + 1) * block_cells]


def prep_kernel(shape, owner, offsets, values, errors, ancestors, rows, steps):
    block_cells, count, scale, members = shape
    block, group = lax.axis_index("grid"), lax.axis_index("lev")
    index = lax.broadcasted_iota(jnp.int32, (8, 1), 0)
    region = jnp.full((8, 1), block, jnp.int32)
    for b in range(1, NB):
        region = jnp.where(index == b - 1, owner[b], region)
    centre = region.astype(F32) + 0.5
    rows[...] = jnp.zeros((SPARE, LANES), F32)
    row = lax.broadcasted_iota(jnp.int32, (members, members), 0)
    column = lax.broadcasted_iota(jnp.int32, (members, members), 1)
    turned = (row == column).astype(F32)
    for b in range(NB):
        cells = owner[b] * block_cells + offsets[b, pl.ds(group, 1), :]
        distance = (centre - cells.astype(F32) / block_cells) / scale
        taper = jnp.exp(-0.5 * distance * distance)
        alpha = 0.8 * (1.0 - jnp.exp(-jnp.sum(taper, axis=1, keepdims=True) / count))
        error = errors[b]
        part = (-0.5 / count) * (taper / (error * error))
        for later in range(b + 1, NB):
            i = PAIRS.index((b, later))
            rows[ALPHA + i : ALPHA + i + 1, :] = jnp.broadcast_to(alpha[later - 1 : later], (1, LANES))
            rows[LATER + i : LATER + i + 1, :count] = part[later - 1 : later]
        rows[VALUE + b : VALUE + b + 1, :count] = values[b]
        rows[OWN + b : OWN + b + 1, :count] = part[NB - 1 : NB]
        steps[b] = turned.T
        own = alpha[NB - 1 : NB]
        turned = own * lane_take(turned, ancestors[b]) + (1.0 - own) * turned
    steps[NB] = turned.T


def turn_kernel(shape, owner, rows, far_rows, ahead, *refs):
    n, slab, width = shape
    pieces, out, held = refs[:-2], refs[-2], refs[-1]
    members = n * slab
    block = lax.axis_index("grid")
    for i in range(n):
        if len(pieces) == n:
            held[lax.bitwise_xor(block, i)] = pieces[i][...]
        else:
            held[i] = pieces[0][i]
    for part, extra in enumerate((rows, far_rows)):
        for i in range(width // LANES):
            value = held[:, part, i * slab : (i + 1) * slab, :].reshape(members, LANES)
            out[part, i * LANES : (i + 1) * LANES, :] = value.T
        out[part, width:, :] = extra[...]
        line = width // LANES * slab
        for i, (e, b) in enumerate(PAIRS):
            out[part, width + PARENT + i : width + PARENT + i + 1, :] = held[owner[b], part, line + e : line + e + 1, :]


def mix_kernel(shape, steps, pull, fields, *refs):
    n, slab, depth, block_cells = shape
    outs, held = refs[:-1], refs[-1]
    members = n * slab
    held[...] = (steps[NB] + pull[0:1, :]).reshape(n, slab, members)
    block = lax.axis_index("grid")
    if len(outs) == n:
        blend = jnp.concatenate([held[lax.bitwise_xor(block, i)] for i in range(n)], axis=0)
    else:
        blend = held[...].reshape(members, members)
    for level in range(depth):
        value = high_dot(blend, fields[:, level].reshape(members, block_cells)).reshape(n, slab, block_cells)
        if len(outs) == n:
            for i in range(n):
                outs[i][level] = value[i]
        else:
            outs[0][:, level] = value


def chain_kernel(shape, own, near, steps, out):
    members, groups, count = shape
    width = groups * count
    base = NB * width
    group = lax.axis_index("lev")
    sources = [own.at[0], near.at[0], own.at[1], near.at[1]]
    columns = [source[base : base + SPARE, :].T for source in sources]
    parents, alphas = [], []
    for source in sources:
        parents.append(source[base + PARENT : base + PARENT + 8, :].astype(jnp.int32))
        alphas.append(source[base + ALPHA : base + ALPHA + 6, :])
    tilts = {}
    pulled = []
    for b in range(NB):
        kinds = [(q, later) for q in range(groups) for later in range(b + 1, NB)] + [(0, None)]
        height = -(-len(kinds) // 8) * 8
        index = lax.broadcasted_iota(jnp.int32, (height, members), 0)
        logs = jnp.zeros((height, members), F32)
        for q in range(groups if b < NB - 1 else 1):
            start = pl.multiple_of(b * width + lax.bitwise_xor(group, q) * count, count)
            total = jnp.zeros((count, members), F32)
            tilted = jnp.zeros((count, members), F32)
            for p, source in enumerate(sources):
                value = source[pl.ds(start, count), :]
                for e in range(b):
                    i = PAIRS.index((e, b))
                    tilted = tilted + value * tilts[e, p, b]
                    alpha = alphas[p][i : i + 1]
                    moved = lane_take(value, parents[p][i : i + 1])
                    value = alpha * moved + (1.0 - alpha) * value
                total = total + value
            if b > 0:
                total = total + jnp.sum(tilted, axis=1, keepdims=True)
            miss = columns[q][:count, VALUE + b : VALUE + b + 1] - total
            square = miss * miss
            for row, (owner_group, later) in enumerate(kinds):
                if owner_group != q:
                    continue
                at = OWN + b if later is None else LATER + PAIRS.index((b, later))
                log = jnp.sum(columns[q][:count, at : at + 1] * square, axis=0, keepdims=True)
                logs = jnp.where(index == row, log, logs)
        expo = jnp.exp(logs - jnp.max(logs, axis=1, keepdims=True))
        tilt = expo / jnp.sum(expo, axis=1, keepdims=True) - 1.0 / members
        for row, (q, later) in enumerate(kinds):
            if later is None:
                pulled.append(tilt[row : row + 1])
            else:
                tilts[b, q, later] = tilt[row : row + 1]
    pull = jnp.zeros((8, members), F32)
    for b in range(NB):
        pull = pull + high_dot(jnp.broadcast_to(pulled[b], (8, members)), steps[b])
    out[...] = pull


def final_kernel(shape, *refs):
    n, slab, depth, block_cells = shape
    pieces, out = refs[:-1], refs[-1]
    block = lax.axis_index("grid")
    for i in range(n):
        region = lax.bitwise_xor(block, ORDER[i]) if len(pieces) == n else i
        cells = pl.ds(pl.multiple_of(region * block_cells, LANES), block_cells)
        for level in range(depth):
            out[:, level, cells] = pieces[i][level] if len(pieces) == n else pieces[0][i, level]


def gather_pieces(piece, n):
    if n != 8:
        return [lax.all_to_all(jnp.broadcast_to(piece[None], (n,) + piece.shape), "grid", 0, 0, tiled=True)]
    pieces = [piece]
    pieces = {0: piece}
    for i in (6, 4, 2):
        pieces[i] = lax.ppermute(piece, "grid", [(j, j ^ i) for j in range(n)])
    for i in (0, 2, 4, 6):
        pieces[i + 1] = lax.ppermute(pieces[i], "grid", [(j, j ^ 1) for j in range(n)])
    return [pieces[i] for i in range(n)]


def exchange_pieces(pieces, n):
    if len(pieces) == 1:
        return [lax.all_to_all(pieces[0], "grid", 0, 0, tiled=True)]
    return [pieces[0]] + [
        lax.ppermute(pieces[i], "grid", [(j, j ^ i) for j in range(n)]) for i in ORDER[1:]
    ]


def body(prior, channel_weights, obs_owner, obs_offset, obs_value, obs_error, ancestors):
    n, lev = lax.axis_size("grid"), lax.axis_size("lev")
    slab, depth, cells = prior.shape
    members = slab * n
    block_cells = cells // n
    groups = channel_weights.shape[1]
    count = obs_offset.shape[2]
    width = NB * groups * count
    scale = n / 2.0
    shape = jax.ShapeDtypeStruct
    parents = ancestors[:, 0]
    tall = width // LANES * slab + 8

    piece = call(
        functools.partial(pick_kernel, (slab, depth, block_cells, groups, count)),
        shape((tall, LANES), F32),
        [PLACE] * 5,
        scratch=[
            pltpu.SMEM(obs_owner.shape, jnp.int32),
            pltpu.VMEM(channel_weights.shape, F32),
            pltpu.VMEM(obs_offset.shape, jnp.int32),
            pltpu.VMEM(parents.shape, jnp.int32),
            pltpu.VMEM(prior.shape, F32),
            pltpu.SemaphoreType.DMA((5,)),
        ],
        moved=10**6,
        limit=None,
    )(obs_owner, channel_weights, obs_offset, parents, prior)
    far = lax.ppermute(piece, "lev", [(j, j ^ 2) for j in range(lev)])
    both = call(join_kernel, shape((2, tall, LANES), F32), [VMEM] * 2, moved=10**5)(piece, far)
    pieces = gather_pieces(both, n)

    send = call(
        functools.partial(retile_kernel, (n, slab, depth, block_cells)),
        shape((n, depth, slab, block_cells), F32),
        [VMEM],
        moved=10**6,
    )(prior)
    fields = lax.all_to_all(send, "grid", 0, 0, tiled=True)

    rows, steps = call(
        functools.partial(prep_kernel, (block_cells, count, scale, members)),
        [shape((SPARE, LANES), F32), shape((NB + 1, members, members), F32)],
        [SMEM, VMEM, VMEM, VMEM, VMEM],
        moved=10**6,
    )(obs_owner, obs_offset, obs_value, obs_error, parents)

    far_rows = lax.ppermute(rows, "lev", [(j, j ^ 2) for j in range(lev)])

    own = call(
        functools.partial(turn_kernel, (n, slab, width)),
        shape((2, width + SPARE, members), F32),
        [SMEM, VMEM, VMEM, PLACE] + [VMEM] * len(pieces),
        scratch=[pltpu.VMEM((n, 2, tall, LANES), F32)],
        moved=10**6,
    )(obs_owner, rows, far_rows, send, *pieces)
    near = lax.ppermute(own, "lev", [(j, j ^ 1) for j in range(lev)])

    pull = call(
        functools.partial(chain_kernel, (members, groups, count)),
        shape((8, members), F32),
        [VMEM] * 3,
        moved=10**5,
    )(own, near, steps)

    if n == 8:
        layout = [shape((depth, slab, block_cells), F32)] * n
    else:
        layout = [shape((n, depth, slab, block_cells), F32)]
    send = call(
        functools.partial(mix_kernel, (n, slab, depth, block_cells)),
        layout,
        [VMEM] * 3,
        scratch=[pltpu.VMEM((n, slab, members), F32)],
        flops=10**8,
        moved=10**6,
    )(steps, pull, fields)
    moved = exchange_pieces(send, n)

    return call(
        functools.partial(final_kernel, (n, slab, depth, block_cells)),
        shape((slab, depth, cells), F32),
        [VMEM] * len(moved),
        moved=10**6,
    )(*moved)


def solution(mesh):
    in_specs = (
        P("grid", "lev", None),
        P("lev", None),
        P(),
        P(),
        P(None, "lev", None),
        P(None, "lev", None),
        P(None, "lev", "grid", None),
    )
    out_specs = P("grid", "lev", None)
    return jax.shard_map(body, mesh=mesh, in_specs=in_specs, out_specs=out_specs, check_vma=False)
```

```python
import functools

import jax
import jax.numpy as jnp
from jax import lax
from jax.experimental import pallas as pl
from jax.experimental.pallas import tpu as pltpu
from jax.sharding import PartitionSpec as P

NB = 4
HIGH = lax.Precision.HIGHEST
LANES = 128
F32 = jnp.float32
VMEM = pl.BlockSpec(memory_space=pltpu.VMEM)
SMEM = pl.BlockSpec(memory_space=pltpu.SMEM)
PLACE = pl.BlockSpec(memory_space=pl.ANY)
LIMIT = 48 * 1024 * 1024

PAIRS = [(e, b) for b in range(1, NB) for e in range(b)]
PARENT, ALPHA, LATER, VALUE, OWN, SPARE = 0, 6, 12, 18, 22, 32


def call(kernel, out_shapes, in_specs, scratch=(), flops=0, moved=0, limit=LIMIT):
    many = isinstance(out_shapes, (list, tuple))
    return pl.pallas_call(
        kernel,
        out_shape=out_shapes,
        in_specs=in_specs,
        out_specs=[VMEM] * len(out_shapes) if many else VMEM,
        scratch_shapes=list(scratch),
        compiler_params=pltpu.CompilerParams(vmem_limit_bytes=limit),
        cost_estimate=pl.CostEstimate(flops=flops, bytes_accessed=moved, transcendentals=0),
    )


def high_dot(a, b):
    return lax.dot_general(a, b, (((1,), (0,)), ((), ())), precision=HIGH, preferred_element_type=F32)


def lane_take(value, row):
    where = jnp.broadcast_to(row, value.shape)
    return jnp.take_along_axis(value, where, axis=1, mode="promise_in_bounds")


def pick_kernel(shape, *refs):
    slab, depth, block_cells, groups, count = shape
    out, arrivals = refs[5], refs[11]
    copies = [pltpu.make_async_copy(refs[i], refs[6 + i], arrivals.at[i]) for i in range(5)]
    for copy in copies:
        copy.start()
    for copy in copies:
        copy.wait()
    owner, weights, offsets, ancestors, prior = refs[6:11]
    width = groups * count
    per = LANES // count
    for b in range(NB):
        start = pl.multiple_of(owner[b] * block_cells, LANES)
        levels = [prior[:, level, pl.ds(start, block_cells)] for level in range(depth)]
        for c in range(width // LANES):
            cell = jnp.concatenate([offsets[b, g : g + 1, :] for g in range(c * per, (c + 1) * per)], axis=1)
            low, high = lax.rem(cell, LANES), lax.div(cell, LANES)
            total = jnp.zeros((slab, LANES), F32)
            for level in range(depth):
                found = jnp.zeros((slab, LANES), F32)
                for h in range(block_cells // LANES):
                    part = lane_take(levels[level][:, h * LANES : (h + 1) * LANES], low)
                    found = jnp.where(high == h, part, found)
                row = jnp.concatenate(
                    [
                        jnp.broadcast_to(weights[level : level + 1, g : g + 1], (1, count))
                        for g in range(c * per, (c + 1) * per)
                    ],
                    axis=1,
                )
                total = total + found * row
            line = (b * width // LANES + c) * slab
            out[line : line + slab, :] = total
    line = NB * width // LANES * slab
    out[line:, :] = jnp.zeros((out.shape[0] - line, LANES), F32)
    for b in range(NB):
        out[line + b : line + b + 1, :] = ancestors[b].astype(F32)


def retile_kernel(shape, prior, out):
    n, slab, depth, block_cells = shape
    for i in range(n):
        for level in range(depth):
            out[i, level] = prior[:, level, i * block_cells : (i + 1) * block_cells]


def prep_kernel(shape, owner, offsets, values, errors, ancestors, rows, steps):
    block_cells, count, scale, members = shape
    block, group = lax.axis_index("grid"), lax.axis_index("lev")
    index = lax.broadcasted_iota(jnp.int32, (8, 1), 0)
    region = jnp.full((8, 1), block, jnp.int32)
    for b in range(1, NB):
        region = jnp.where(index == b - 1, owner[b], region)
    centre = region.astype(F32) + 0.5
    rows[...] = jnp.zeros((SPARE, LANES), F32)
    row = lax.broadcasted_iota(jnp.int32, (members, members), 0)
    column = lax.broadcasted_iota(jnp.int32, (members, members), 1)
    turned = (row == column).astype(F32)
    for b in range(NB):
        cells = owner[b] * block_cells + offsets[b, pl.ds(group, 1), :]
        distance = (centre - cells.astype(F32) / block_cells) / scale
        taper = jnp.exp(-0.5 * distance * distance)
        alpha = 0.8 * (1.0 - jnp.exp(-jnp.sum(taper, axis=1, keepdims=True) / count))
        error = errors[b]
        part = (-0.5 / count) * (taper / (error * error))
        for later in range(b + 1, NB):
            i = PAIRS.index((b, later))
            rows[ALPHA + i : ALPHA + i + 1, :] = jnp.broadcast_to(alpha[later - 1 : later], (1, LANES))
            rows[LATER + i : LATER + i + 1, :count] = part[later - 1 : later]
        rows[VALUE + b : VALUE + b + 1, :count] = values[b]
        rows[OWN + b : OWN + b + 1, :count] = part[NB - 1 : NB]
        steps[b] = turned.T
        own = alpha[NB - 1 : NB]
        turned = own * lane_take(turned, ancestors[b]) + (1.0 - own) * turned
    steps[NB] = turned.T


def turn_kernel(shape, owner, rows, *refs):
    n, slab, width, count = shape
    pieces, out, slim, held = refs[:-3], refs[-3], refs[-2], refs[-1]
    members = n * slab
    block, group = lax.axis_index("grid"), lax.axis_index("lev")
    if len(pieces) == 1:
        held[...] = pieces[0][...]
    else:
        for i, piece in enumerate(pieces):
            held[lax.bitwise_xor(block, i)] = piece[...]
    common = width // NB * (NB - 1)
    for i in range(width // LANES):
        value = held[:, i * slab : (i + 1) * slab, :].reshape(members, LANES).T
        out[i * LANES : (i + 1) * LANES, :] = value
        if (i + 1) * LANES <= common:
            slim[i * LANES : (i + 1) * LANES, :] = value
    for i in range(2):
        start = pl.multiple_of(common + lax.bitwise_xor(group, 2 + i) * count, count)
        slim[common + i * count : common + (i + 1) * count, :] = out[pl.ds(start, count), :]
    low = common + 2 * count
    out[width:, :] = rows[...]
    slim[low:, :] = rows[...]
    line = width // LANES * slab
    for i, (e, b) in enumerate(PAIRS):
        value = held[owner[b], line + e : line + e + 1, :]
        out[width + PARENT + i : width + PARENT + i + 1, :] = value
        slim[low + PARENT + i : low + PARENT + i + 1, :] = value


def mix_kernel(shape, steps, fields, out):
    n, slab, depth, block_cells = shape
    for level in range(depth):
        value = fields[:, level].reshape(n * slab, block_cells)
        out[:, level] = high_dot(steps[NB], value).reshape(n, slab, block_cells)


def chain_kernel(shape, own, near, far, cross, steps, fields, out):
    members, groups, count, depth, block_cells = shape
    width = groups * count
    group = lax.axis_index("lev")
    sources = [own, near, far, cross]
    bases = [NB * width, NB * width, (NB - 1) * width + 2 * count, (NB - 1) * width + 2 * count]
    columns = [source[base : base + SPARE, :].T for source, base in zip(sources, bases)]
    parents, alphas = [], []
    for source, base in zip(sources, bases):
        parents.append(source[base + PARENT : base + PARENT + 8, :].astype(jnp.int32))
        alphas.append(source[base + ALPHA : base + ALPHA + 6, :])
    tilts = {}
    pulled = []
    for b in range(NB):
        kinds = [(q, later) for q in range(groups) for later in range(b + 1, NB)] + [(0, None)]
        height = -(-len(kinds) // 8) * 8
        index = lax.broadcasted_iota(jnp.int32, (height, members), 0)
        logs = jnp.zeros((height, members), F32)
        for q in range(groups if b < NB - 1 else 1):
            start = pl.multiple_of(b * width + lax.bitwise_xor(group, q) * count, count)
            total = jnp.zeros((count, members), F32)
            tilted = jnp.zeros((count, members), F32)
            for p, source in enumerate(sources):
                if b == NB - 1 and p > 1:
                    value = source[b * width + (p - 2) * count : b * width + (p - 1) * count, :]
                else:
                    value = source[pl.ds(start, count), :]
                for e in range(b):
                    i = PAIRS.index((e, b))
                    tilted = tilted + value * tilts[e, p, b]
                    alpha = alphas[p][i : i + 1]
                    moved = lane_take(value, parents[p][i : i + 1])
                    value = alpha * moved + (1.0 - alpha) * value
                total = total + value
            if b > 0:
                total = total + jnp.sum(tilted, axis=1, keepdims=True)
            miss = columns[q][:count, VALUE + b : VALUE + b + 1] - total
            square = miss * miss
            for row, (owner_group, later) in enumerate(kinds):
                if owner_group != q:
                    continue
                at = OWN + b if later is None else LATER + PAIRS.index((b, later))
                log = jnp.sum(columns[q][:count, at : at + 1] * square, axis=0, keepdims=True)
                logs = jnp.where(index == row, log, logs)
        expo = jnp.exp(logs - jnp.max(logs, axis=1, keepdims=True))
        tilt = expo / jnp.sum(expo, axis=1, keepdims=True) - 1.0 / members
        for row, (q, later) in enumerate(kinds):
            if later is None:
                pulled.append(tilt[row : row + 1])
            else:
                tilts[b, q, later] = tilt[row : row + 1]
    pull = jnp.zeros((8, members), F32)
    for b in range(NB):
        pull = pull + high_dot(jnp.broadcast_to(pulled[b], (8, members)), steps[b])
    for level in range(depth):
        value = fields[:, level].reshape(members, block_cells)
        out[level : level + 1, :] = high_dot(pull, value)[0:1]


def final_kernel(shape, moved, *refs):
    n, slab, depth, block_cells = shape
    shifts, out = refs[:-1], refs[-1]
    block = lax.axis_index("grid")
    for i in range(n):
        region = i if len(shifts) == 1 else lax.bitwise_xor(block, i)
        cells = pl.ds(pl.multiple_of(region * block_cells, LANES), block_cells)
        for level in range(depth):
            if len(shifts) == 1:
                shift = shifts[0][i, level : level + 1, :]
            else:
                shift = shifts[i][level : level + 1, :]
            out[:, level, cells] = moved[region, level] + shift


def hop(value, distance, n):
    return lax.ppermute(value, "grid", [(j, j ^ distance) for j in range(n)])


def gather_pieces(piece, n):
    if n != 8:
        return [lax.all_to_all(jnp.broadcast_to(piece[None], (n,) + piece.shape), "grid", 0, 0, tiled=True)]
    pieces = {0: piece}
    for i in (6, 4, 2):
        pieces[i] = hop(piece, i, n)
    for i in (0, 2, 4, 6):
        pieces[i + 1] = hop(pieces[i], 1, n)
    return [pieces[i] for i in range(n)]


def body(prior, channel_weights, obs_owner, obs_offset, obs_value, obs_error, ancestors):
    n, lev = lax.axis_size("grid"), lax.axis_size("lev")
    slab, depth, cells = prior.shape
    members = slab * n
    block_cells = cells // n
    groups = channel_weights.shape[1]
    count = obs_offset.shape[2]
    width = NB * groups * count
    scale = n / 2.0
    shape = jax.ShapeDtypeStruct
    parents = ancestors[:, 0]
    tall = width // LANES * slab + 8

    piece = call(
        functools.partial(pick_kernel, (slab, depth, block_cells, groups, count)),
        shape((tall, LANES), F32),
        [PLACE] * 5,
        scratch=[
            pltpu.SMEM(obs_owner.shape, jnp.int32),
            pltpu.VMEM(channel_weights.shape, F32),
            pltpu.VMEM(obs_offset.shape, jnp.int32),
            pltpu.VMEM(parents.shape, jnp.int32),
            pltpu.VMEM(prior.shape, F32),
            pltpu.SemaphoreType.DMA((5,)),
        ],
        moved=10**6,
        limit=None,
    )(obs_owner, channel_weights, obs_offset, parents, prior)
    pieces = gather_pieces(piece, n)
    send = call(
        functools.partial(retile_kernel, (n, slab, depth, block_cells)),
        shape((n, depth, slab, block_cells), F32),
        [VMEM],
        moved=10**6,
    )(prior)
    send, *_ = lax.optimization_barrier((send, *pieces[2::2]))
    fields = lax.all_to_all(send, "grid", 0, 0, tiled=True)

    rows, steps = call(
        functools.partial(prep_kernel, (block_cells, count, scale, members)),
        [shape((SPARE, LANES), F32), shape((NB + 1, members, members), F32)],
        [SMEM, VMEM, VMEM, VMEM, VMEM],
        moved=10**6,
    )(obs_owner, obs_offset, obs_value, obs_error, parents)

    slim_height = (NB - 1) * groups * count + 2 * count + SPARE
    own, slim = call(
        functools.partial(turn_kernel, (n, slab, width, count)),
        [shape((width + SPARE, members), F32), shape((slim_height, members), F32)],
        [SMEM, VMEM] + [VMEM] * len(pieces),
        scratch=[pltpu.VMEM((n, tall, LANES), F32)],
        moved=10**6,
    )(obs_owner, rows, *pieces)
    far = lax.ppermute(slim, "lev", [(j, j ^ 2) for j in range(lev)])
    near = lax.ppermute(own, "lev", [(j, j ^ 1) for j in range(lev)])
    cross = lax.ppermute(far, "lev", [(j, j ^ 1) for j in range(lev)])

    send = call(
        functools.partial(mix_kernel, (n, slab, depth, block_cells)),
        shape((n, depth, slab, block_cells), F32),
        [VMEM] * 2,
        flops=10**8,
        moved=10**6,
    )(steps, fields)
    moved = lax.all_to_all(send, "grid", 0, 0, tiled=True)

    shift = call(
        functools.partial(chain_kernel, (members, groups, count, depth, block_cells)),
        shape((depth, block_cells), F32),
        [VMEM] * 6,
        moved=10**5,
    )(own, near, far, cross, steps, fields)
    shifts = gather_pieces(shift, n)

    return call(
        functools.partial(final_kernel, (n, slab, depth, block_cells)),
        shape((slab, depth, cells), F32),
        [VMEM] * (1 + len(shifts)),
        moved=10**6,
    )(moved, *shifts)


def solution(mesh):
    in_specs = (
        P("grid", "lev", None),
        P("lev", None),
        P(),
        P(),
        P(None, "lev", None),
        P(None, "lev", None),
        P(None, "lev", "grid", None),
    )
    out_specs = P("grid", "lev", None)
    return jax.shard_map(body, mesh=mesh, in_specs=in_specs, out_specs=out_specs, check_vma=False)
```

```python
import functools

import jax
import jax.numpy as jnp
from jax import lax
from jax.experimental import pallas as pl
from jax.experimental.pallas import tpu as pltpu
from jax.sharding import PartitionSpec as P

NB = 4
HIGH = lax.Precision.HIGHEST
LANES = 128
F32 = jnp.float32
VMEM = pl.BlockSpec(memory_space=pltpu.VMEM)
SMEM = pl.BlockSpec(memory_space=pltpu.SMEM)
PLACE = pl.BlockSpec(memory_space=pl.ANY)
LIMIT = 48 * 1024 * 1024

PARTS = ((0,), (6, 7), (4,), (5,), (2, 3), (1,))
ORDER = (0, 6, 4, 5, 2, 1, 3, 7)
PAIRS = [(e, b) for b in range(1, NB) for e in range(b)]
PARENT, ALPHA, LATER, VALUE, OWN, SPARE = 0, 6, 12, 18, 22, 32


def call(kernel, out_shapes, in_specs, scratch=(), flops=0, moved=0, limit=LIMIT):
    many = isinstance(out_shapes, (list, tuple))
    return pl.pallas_call(
        kernel,
        out_shape=out_shapes,
        in_specs=in_specs,
        out_specs=[VMEM] * len(out_shapes) if many else VMEM,
        scratch_shapes=list(scratch),
        compiler_params=pltpu.CompilerParams(vmem_limit_bytes=limit),
        cost_estimate=pl.CostEstimate(flops=flops, bytes_accessed=moved, transcendentals=0),
    )


def high_dot(a, b):
    return lax.dot_general(a, b, (((1,), (0,)), ((), ())), precision=HIGH, preferred_element_type=F32)


def lane_take(value, row):
    where = jnp.broadcast_to(row, value.shape)
    return jnp.take_along_axis(value, where, axis=1, mode="promise_in_bounds")


def pick_kernel(shape, *refs):
    slab, depth, block_cells, groups, count = shape
    out, arrivals = refs[5], refs[11]
    copies = [pltpu.make_async_copy(refs[i], refs[6 + i], arrivals.at[i]) for i in range(5)]
    for copy in copies:
        copy.start()
    for copy in copies:
        copy.wait()
    owner, weights, offsets, ancestors, prior = refs[6:11]
    width = groups * count
    per = LANES // count
    for b in range(NB):
        start = pl.multiple_of(owner[b] * block_cells, LANES)
        levels = [prior[:, level, pl.ds(start, block_cells)] for level in range(depth)]
        for c in range(width // LANES):
            cell = jnp.concatenate([offsets[b, g : g + 1, :] for g in range(c * per, (c + 1) * per)], axis=1)
            low, high = lax.rem(cell, LANES), lax.div(cell, LANES)
            total = jnp.zeros((slab, LANES), F32)
            for level in range(depth):
                found = jnp.zeros((slab, LANES), F32)
                for h in range(block_cells // LANES):
                    part = lane_take(levels[level][:, h * LANES : (h + 1) * LANES], low)
                    found = jnp.where(high == h, part, found)
                row = jnp.concatenate(
                    [
                        jnp.broadcast_to(weights[level : level + 1, g : g + 1], (1, count))
                        for g in range(c * per, (c + 1) * per)
                    ],
                    axis=1,
                )
                total = total + found * row
            line = (b * width // LANES + c) * slab
            out[line : line + slab, :] = total
    line = NB * width // LANES * slab
    out[line:, :] = jnp.zeros((out.shape[0] - line, LANES), F32)
    for b in range(NB):
        out[line + b : line + b + 1, :] = ancestors[b].astype(F32)


def retile_kernel(shape, prior, out):
    n, slab, depth, block_cells = shape
    for i in range(n):
        for level in range(depth):
            out[i, level] = prior[:, level, i * block_cells : (i + 1) * block_cells]


def prep_kernel(shape, owner, offsets, values, errors, ancestors, rows, steps):
    block_cells, count, scale, members = shape
    block, group = lax.axis_index("grid"), lax.axis_index("lev")
    index = lax.broadcasted_iota(jnp.int32, (8, 1), 0)
    region = jnp.full((8, 1), block, jnp.int32)
    for b in range(1, NB):
        region = jnp.where(index == b - 1, owner[b], region)
    centre = region.astype(F32) + 0.5
    rows[...] = jnp.zeros((SPARE, LANES), F32)
    row = lax.broadcasted_iota(jnp.int32, (members, members), 0)
    column = lax.broadcasted_iota(jnp.int32, (members, members), 1)
    turned = (row == column).astype(F32)
    for b in range(NB):
        cells = owner[b] * block_cells + offsets[b, pl.ds(group, 1), :]
        distance = (centre - cells.astype(F32) / block_cells) / scale
        taper = jnp.exp(-0.5 * distance * distance)
        alpha = 0.8 * (1.0 - jnp.exp(-jnp.sum(taper, axis=1, keepdims=True) / count))
        error = errors[b]
        part = (-0.5 / count) * (taper / (error * error))
        for later in range(b + 1, NB):
            i = PAIRS.index((b, later))
            rows[ALPHA + i : ALPHA + i + 1, :] = jnp.broadcast_to(alpha[later - 1 : later], (1, LANES))
            rows[LATER + i : LATER + i + 1, :count] = part[later - 1 : later]
        rows[VALUE + b : VALUE + b + 1, :count] = values[b]
        rows[OWN + b : OWN + b + 1, :count] = part[NB - 1 : NB]
        steps[b] = turned.T
        own = alpha[NB - 1 : NB]
        turned = own * lane_take(turned, ancestors[b]) + (1.0 - own) * turned
    steps[NB] = turned.T


def turn_kernel(shape, owner, rows, ahead, *refs):
    n, slab, width, count = shape
    pieces, out, slim, held = refs[:-3], refs[-3], refs[-2], refs[-1]
    members = n * slab
    block, group = lax.axis_index("grid"), lax.axis_index("lev")
    if len(pieces) == 1:
        held[...] = pieces[0][...]
    else:
        for i, piece in enumerate(pieces):
            held[lax.bitwise_xor(block, i)] = piece[...]
    common = width // NB * (NB - 1)
    for i in range(width // LANES):
        value = held[:, i * slab : (i + 1) * slab, :].reshape(members, LANES).T
        out[i * LANES : (i + 1) * LANES, :] = value
        if (i + 1) * LANES <= common:
            slim[i * LANES : (i + 1) * LANES, :] = value
    for i in range(2):
        start = pl.multiple_of(common + lax.bitwise_xor(group, 2 + i) * count, count)
        slim[common + i * count : common + (i + 1) * count, :] = out[pl.ds(start, count), :]
    low = common + 2 * count
    out[width:, :] = rows[...]
    slim[low:, :] = rows[...]
    line = width // LANES * slab
    for i, (e, b) in enumerate(PAIRS):
        value = held[owner[b], line + e : line + e + 1, :]
        out[width + PARENT + i : width + PARENT + i + 1, :] = value
        slim[low + PARENT + i : low + PARENT + i + 1, :] = value


def mix_kernel(shape, steps, pull, fields, *refs):
    n, slab, depth, block_cells = shape
    outs, held = refs[:-1], refs[-1]
    members = n * slab
    held[...] = (steps[NB] + pull[0:1, :]).reshape(n, slab, members)
    block = lax.axis_index("grid")
    if len(outs) == 1:
        blend = held[...].reshape(members, members)
    else:
        blend = jnp.concatenate([held[lax.bitwise_xor(block, i)] for i in range(n)], axis=0)
    for level in range(depth):
        value = high_dot(blend, fields[:, level].reshape(members, block_cells)).reshape(n, slab, block_cells)
        if len(outs) == 1:
            outs[0][:, level] = value
        else:
            for out, part in zip(outs, PARTS):
                for i, distance in enumerate(part):
                    out[i, level] = value[distance]


def chain_kernel(shape, own, near, far, cross, steps, out):
    members, groups, count = shape
    width = groups * count
    group = lax.axis_index("lev")
    sources = [own, near, far, cross]
    bases = [NB * width, NB * width, (NB - 1) * width + 2 * count, (NB - 1) * width + 2 * count]
    columns = [source[base : base + SPARE, :].T for source, base in zip(sources, bases)]
    parents, alphas = [], []
    for source, base in zip(sources, bases):
        parents.append(source[base + PARENT : base + PARENT + 8, :].astype(jnp.int32))
        alphas.append(source[base + ALPHA : base + ALPHA + 6, :])
    tilts = {}
    pulled = []
    for b in range(NB):
        kinds = [(q, later) for q in range(groups) for later in range(b + 1, NB)] + [(0, None)]
        height = -(-len(kinds) // 8) * 8
        index = lax.broadcasted_iota(jnp.int32, (height, members), 0)
        logs = jnp.zeros((height, members), F32)
        for q in range(groups if b < NB - 1 else 1):
            start = pl.multiple_of(b * width + lax.bitwise_xor(group, q) * count, count)
            total = jnp.zeros((count, members), F32)
            tilted = jnp.zeros((count, members), F32)
            for p, source in enumerate(sources):
                if b == NB - 1 and p > 1:
                    value = source[b * width + (p - 2) * count : b * width + (p - 1) * count, :]
                else:
                    value = source[pl.ds(start, count), :]
                for e in range(b):
                    i = PAIRS.index((e, b))
                    tilted = tilted + value * tilts[e, p, b]
                    alpha = alphas[p][i : i + 1]
                    moved = lane_take(value, parents[p][i : i + 1])
                    value = alpha * moved + (1.0 - alpha) * value
                total = total + value
            if b > 0:
                total = total + jnp.sum(tilted, axis=1, keepdims=True)
            miss = columns[q][:count, VALUE + b : VALUE + b + 1] - total
            square = miss * miss
            for row, (owner_group, later) in enumerate(kinds):
                if owner_group != q:
                    continue
                at = OWN + b if later is None else LATER + PAIRS.index((b, later))
                log = jnp.sum(columns[q][:count, at : at + 1] * square, axis=0, keepdims=True)
                logs = jnp.where(index == row, log, logs)
        expo = jnp.exp(logs - jnp.max(logs, axis=1, keepdims=True))
        tilt = expo / jnp.sum(expo, axis=1, keepdims=True) - 1.0 / members
        for row, (q, later) in enumerate(kinds):
            if later is None:
                pulled.append(tilt[row : row + 1])
            else:
                tilts[b, q, later] = tilt[row : row + 1]
    pull = jnp.zeros((8, members), F32)
    for b in range(NB):
        pull = pull + high_dot(jnp.broadcast_to(pulled[b], (8, members)), steps[b])
    out[...] = pull


def final_kernel(shape, *refs):
    n, slab, depth, block_cells = shape
    pieces, out = refs[:-1], refs[-1]
    block = lax.axis_index("grid")
    for i in range(n):
        region = i if len(pieces) == 1 else lax.bitwise_xor(block, ORDER[i])
        cells = pl.ds(pl.multiple_of(region * block_cells, LANES), block_cells)
        for level in range(depth):
            out[:, level, cells] = pieces[0][i, level] if len(pieces) == 1 else pieces[i][0, level]


def hop(value, distance, n):
    return lax.ppermute(value, "grid", [(j, j ^ distance) for j in range(n)])


def gather_pieces(piece, n):
    if n != 8:
        return [lax.all_to_all(jnp.broadcast_to(piece[None], (n,) + piece.shape), "grid", 0, 0, tiled=True)]
    pieces = {0: piece}
    for i in (6, 4, 2):
        pieces[i] = hop(piece, i, n)
    for i in (0, 2, 4, 6):
        pieces[i + 1] = hop(pieces[i], 1, n)
    return [pieces[i] for i in range(n)]


def exchange_parts(parts, n):
    if len(parts) == 1:
        return [lax.all_to_all(parts[0], "grid", 0, 0, tiled=True)]
    pieces = {0: parts[0]}
    for part, distances in zip(parts[1:], PARTS[1:]):
        pieces[distances[0]] = hop(part, distances[0], n)
        if len(distances) == 2:
            pieces[distances[1]] = hop(pieces[distances[0]][1:], 1, n)
    return [pieces[i] for i in ORDER]


def body(prior, channel_weights, obs_owner, obs_offset, obs_value, obs_error, ancestors):
    n, lev = lax.axis_size("grid"), lax.axis_size("lev")
    slab, depth, cells = prior.shape
    members = slab * n
    block_cells = cells // n
    groups = channel_weights.shape[1]
    count = obs_offset.shape[2]
    width = NB * groups * count
    scale = n / 2.0
    shape = jax.ShapeDtypeStruct
    parents = ancestors[:, 0]
    tall = width // LANES * slab + 8

    piece = call(
        functools.partial(pick_kernel, (slab, depth, block_cells, groups, count)),
        shape((tall, LANES), F32),
        [PLACE] * 5,
        scratch=[
            pltpu.SMEM(obs_owner.shape, jnp.int32),
            pltpu.VMEM(channel_weights.shape, F32),
            pltpu.VMEM(obs_offset.shape, jnp.int32),
            pltpu.VMEM(parents.shape, jnp.int32),
            pltpu.VMEM(prior.shape, F32),
            pltpu.SemaphoreType.DMA((5,)),
        ],
        moved=10**6,
        limit=None,
    )(obs_owner, channel_weights, obs_offset, parents, prior)
    pieces = gather_pieces(piece, n)
    send = call(
        functools.partial(retile_kernel, (n, slab, depth, block_cells)),
        shape((n, depth, slab, block_cells), F32),
        [VMEM],
        moved=10**6,
    )(prior)
    fields = lax.all_to_all(send, "grid", 0, 0, tiled=True)

    rows, steps = call(
        functools.partial(prep_kernel, (block_cells, count, scale, members)),
        [shape((SPARE, LANES), F32), shape((NB + 1, members, members), F32)],
        [SMEM, VMEM, VMEM, VMEM, VMEM],
        moved=10**6,
    )(obs_owner, obs_offset, obs_value, obs_error, parents)

    slim_height = (NB - 1) * groups * count + 2 * count + SPARE
    own, slim = call(
        functools.partial(turn_kernel, (n, slab, width, count)),
        [shape((width + SPARE, members), F32), shape((slim_height, members), F32)],
        [SMEM, VMEM, PLACE] + [VMEM] * len(pieces),
        scratch=[pltpu.VMEM((n, tall, LANES), F32)],
        moved=10**6,
    )(obs_owner, rows, send, *pieces)
    far = lax.ppermute(slim, "lev", [(j, j ^ 2) for j in range(lev)])
    near = lax.ppermute(own, "lev", [(j, j ^ 1) for j in range(lev)])
    cross = lax.ppermute(far, "lev", [(j, j ^ 1) for j in range(lev)])

    pull = call(
        functools.partial(chain_kernel, (members, groups, count)),
        shape((8, members), F32),
        [VMEM] * 5,
        moved=10**5,
    )(own, near, far, cross, steps)

    if n == 8:
        layout = [shape((len(part), depth, slab, block_cells), F32) for part in PARTS]
    else:
        layout = [shape((n, depth, slab, block_cells), F32)]
    send = call(
        functools.partial(mix_kernel, (n, slab, depth, block_cells)),
        layout,
        [VMEM] * 3,
        scratch=[pltpu.VMEM((n, slab, members), F32)],
        flops=10**8,
        moved=10**6,
    )(steps, pull, fields)
    moved = exchange_parts(send, n)

    return call(
        functools.partial(final_kernel, (n, slab, depth, block_cells)),
        shape((slab, depth, cells), F32),
        [VMEM] * len(moved),
        moved=10**6,
    )(*moved)


def solution(mesh):
    in_specs = (
        P("grid", "lev", None),
        P("lev", None),
        P(),
        P(),
        P(None, "lev", None),
        P(None, "lev", None),
        P(None, "lev", "grid", None),
    )
    out_specs = P("grid", "lev", None)
    return jax.shard_map(body, mesh=mesh, in_specs=in_specs, out_specs=out_specs, check_vma=False)
```

```python
import functools

import jax
import jax.numpy as jnp
from jax import lax
from jax.experimental import pallas as pl
from jax.experimental.pallas import tpu as pltpu
from jax.sharding import PartitionSpec as P

NB = 4
HIGH = lax.Precision.HIGHEST
LANES = 128
F32 = jnp.float32
VMEM = pl.BlockSpec(memory_space=pltpu.VMEM)
SMEM = pl.BlockSpec(memory_space=pltpu.SMEM)
PLACE = pl.BlockSpec(memory_space=pl.ANY)
LIMIT = 48 * 1024 * 1024

PARTS = ((0,), (6, 7), (4,), (5,), (2, 3), (1,))
ORDER = (0, 6, 4, 5, 2, 1, 3, 7)
PAIRS = [(e, b) for b in range(1, NB) for e in range(b)]
PARENT, ALPHA, LATER, VALUE, OWN, SPARE = 0, 6, 12, 18, 22, 32


def call(kernel, out_shapes, in_specs, scratch=(), flops=0, moved=0, limit=LIMIT):
    many = isinstance(out_shapes, (list, tuple))
    return pl.pallas_call(
        kernel,
        out_shape=out_shapes,
        in_specs=in_specs,
        out_specs=[VMEM] * len(out_shapes) if many else VMEM,
        scratch_shapes=list(scratch),
        compiler_params=pltpu.CompilerParams(vmem_limit_bytes=limit),
        cost_estimate=pl.CostEstimate(flops=flops, bytes_accessed=moved, transcendentals=0),
    )


def high_dot(a, b):
    return lax.dot_general(a, b, (((1,), (0,)), ((), ())), precision=HIGH, preferred_element_type=F32)


def lane_take(value, row):
    where = jnp.broadcast_to(row, value.shape)
    return jnp.take_along_axis(value, where, axis=1, mode="promise_in_bounds")


def pick_kernel(shape, *refs):
    slab, depth, block_cells, groups, count = shape
    out, arrivals = refs[5], refs[11]
    copies = [pltpu.make_async_copy(refs[i], refs[6 + i], arrivals.at[i]) for i in range(5)]
    for copy in copies:
        copy.start()
    for copy in copies:
        copy.wait()
    owner, weights, offsets, ancestors, prior = refs[6:11]
    width = groups * count
    per = LANES // count
    for b in range(NB):
        start = pl.multiple_of(owner[b] * block_cells, LANES)
        levels = [prior[:, level, pl.ds(start, block_cells)] for level in range(depth)]
        for c in range(width // LANES):
            cell = jnp.concatenate([offsets[b, g : g + 1, :] for g in range(c * per, (c + 1) * per)], axis=1)
            low, high = lax.rem(cell, LANES), lax.div(cell, LANES)
            total = jnp.zeros((slab, LANES), F32)
            for level in range(depth):
                found = jnp.zeros((slab, LANES), F32)
                for h in range(block_cells // LANES):
                    part = lane_take(levels[level][:, h * LANES : (h + 1) * LANES], low)
                    found = jnp.where(high == h, part, found)
                row = jnp.concatenate(
                    [
                        jnp.broadcast_to(weights[level : level + 1, g : g + 1], (1, count))
                        for g in range(c * per, (c + 1) * per)
                    ],
                    axis=1,
                )
                total = total + found * row
            line = (b * width // LANES + c) * slab
            out[line : line + slab, :] = total
    line = NB * width // LANES * slab
    out[line:, :] = jnp.zeros((out.shape[0] - line, LANES), F32)
    for b in range(NB):
        out[line + b : line + b + 1, :] = ancestors[b].astype(F32)


def retile_kernel(shape, prior, out):
    n, slab, depth, block_cells = shape
    for i in range(n):
        for level in range(depth):
            out[i, level] = prior[:, level, i * block_cells : (i + 1) * block_cells]


def prep_kernel(shape, owner, offsets, values, errors, ancestors, rows, steps):
    block_cells, count, scale, members = shape
    block, group = lax.axis_index("grid"), lax.axis_index("lev")
    index = lax.broadcasted_iota(jnp.int32, (8, 1), 0)
    region = jnp.full((8, 1), block, jnp.int32)
    for b in range(1, NB):
        region = jnp.where(index == b - 1, owner[b], region)
    centre = region.astype(F32) + 0.5
    rows[...] = jnp.zeros((SPARE, LANES), F32)
    row = lax.broadcasted_iota(jnp.int32, (members, members), 0)
    column = lax.broadcasted_iota(jnp.int32, (members, members), 1)
    turned = (row == column).astype(F32)
    for b in range(NB):
        cells = owner[b] * block_cells + offsets[b, pl.ds(group, 1), :]
        distance = (centre - cells.astype(F32) / block_cells) / scale
        taper = jnp.exp(-0.5 * distance * distance)
        alpha = 0.8 * (1.0 - jnp.exp(-jnp.sum(taper, axis=1, keepdims=True) / count))
        error = errors[b]
        part = (-0.5 / count) * (taper / (error * error))
        for later in range(b + 1, NB):
            i = PAIRS.index((b, later))
            rows[ALPHA + i : ALPHA + i + 1, :] = jnp.broadcast_to(alpha[later - 1 : later], (1, LANES))
            rows[LATER + i : LATER + i + 1, :count] = part[later - 1 : later]
        rows[VALUE + b : VALUE + b + 1, :count] = values[b]
        rows[OWN + b : OWN + b + 1, :count] = part[NB - 1 : NB]
        steps[b] = turned.T
        own = alpha[NB - 1 : NB]
        turned = own * lane_take(turned, ancestors[b]) + (1.0 - own) * turned
    steps[NB] = turned.T


def turn_kernel(shape, owner, rows, ahead, *refs):
    n, slab, width, count = shape
    pieces, out, slim, held = refs[:-3], refs[-3], refs[-2], refs[-1]
    members = n * slab
    block, group = lax.axis_index("grid"), lax.axis_index("lev")
    if len(pieces) == 1:
        held[...] = pieces[0][...]
    else:
        for i, piece in enumerate(pieces):
            held[lax.bitwise_xor(block, i)] = piece[...]
    common = width // NB * (NB - 1)
    for i in range(width // LANES):
        value = held[:, i * slab : (i + 1) * slab, :].reshape(members, LANES).T
        out[i * LANES : (i + 1) * LANES, :] = value
        if (i + 1) * LANES <= common:
            slim[i * LANES : (i + 1) * LANES, :] = value
    for i in range(2):
        start = pl.multiple_of(common + lax.bitwise_xor(group, 2 + i) * count, count)
        slim[common + i * count : common + (i + 1) * count, :] = out[pl.ds(start, count), :]
    low = common + 2 * count
    out[width:, :] = rows[...]
    slim[low:, :] = rows[...]
    line = width // LANES * slab
    for i, (e, b) in enumerate(PAIRS):
        value = held[owner[b], line + e : line + e + 1, :]
        out[width + PARENT + i : width + PARENT + i + 1, :] = value
        slim[low + PARENT + i : low + PARENT + i + 1, :] = value


def mix_kernel(shape, steps, pull, fields, *refs):
    n, slab, depth, block_cells = shape
    outs, held = refs[:-1], refs[-1]
    members = n * slab
    held[...] = (steps[NB] + pull[0:1, :]).reshape(n, slab, members)
    block = lax.axis_index("grid")
    if len(outs) == 1:
        blend = held[...].reshape(members, members)
    else:
        blend = jnp.concatenate([held[lax.bitwise_xor(block, i)] for i in range(n)], axis=0)
    for level in range(depth):
        value = high_dot(blend, fields[:, level].reshape(members, block_cells)).reshape(n, slab, block_cells)
        if len(outs) == 1:
            outs[0][:, level] = value
        else:
            for out, part in zip(outs, PARTS):
                for i, distance in enumerate(part):
                    out[i, level] = value[distance]


def chain_kernel(shape, own, near, far, cross, steps, out):
    members, groups, count = shape
    width = groups * count
    group = lax.axis_index("lev")
    sources = [own, near, far, cross]
    bases = [NB * width, NB * width, (NB - 1) * width + 2 * count, (NB - 1) * width + 2 * count]
    columns = [source[base : base + SPARE, :].T for source, base in zip(sources, bases)]
    parents, alphas = [], []
    for source, base in zip(sources, bases):
        parents.append(source[base + PARENT : base + PARENT + 8, :].astype(jnp.int32))
        alphas.append(source[base + ALPHA : base + ALPHA + 6, :])
    tilts = {}
    pulled = []
    for b in range(NB):
        kinds = [(q, later) for q in range(groups) for later in range(b + 1, NB)] + [(0, None)]
        height = -(-len(kinds) // 8) * 8
        index = lax.broadcasted_iota(jnp.int32, (height, members), 0)
        logs = jnp.zeros((height, members), F32)
        for q in range(groups if b < NB - 1 else 1):
            start = pl.multiple_of(b * width + lax.bitwise_xor(group, q) * count, count)
            total = jnp.zeros((count, members), F32)
            tilted = jnp.zeros((count, members), F32)
            for p, source in enumerate(sources):
                if b == NB - 1 and p > 1:
                    value = source[b * width + (p - 2) * count : b * width + (p - 1) * count, :]
                else:
                    value = source[pl.ds(start, count), :]
                for e in range(b):
                    i = PAIRS.index((e, b))
                    tilted = tilted + value * tilts[e, p, b]
                    alpha = alphas[p][i : i + 1]
                    moved = lane_take(value, parents[p][i : i + 1])
                    value = alpha * moved + (1.0 - alpha) * value
                total = total + value
            if b > 0:
                total = total + jnp.sum(tilted, axis=1, keepdims=True)
            miss = columns[q][:count, VALUE + b : VALUE + b + 1] - total
            square = miss * miss
            for row, (owner_group, later) in enumerate(kinds):
                if owner_group != q:
                    continue
                at = OWN + b if later is None else LATER + PAIRS.index((b, later))
                log = jnp.sum(columns[q][:count, at : at + 1] * square, axis=0, keepdims=True)
                logs = jnp.where(index == row, log, logs)
        expo = jnp.exp(logs - jnp.max(logs, axis=1, keepdims=True))
        tilt = expo / jnp.sum(expo, axis=1, keepdims=True) - 1.0 / members
        for row, (q, later) in enumerate(kinds):
            if later is None:
                pulled.append(tilt[row : row + 1])
            else:
                tilts[b, q, later] = tilt[row : row + 1]
    pull = jnp.zeros((8, members), F32)
    for b in range(NB):
        pull = pull + high_dot(jnp.broadcast_to(pulled[b], (8, members)), steps[b])
    out[...] = pull


def final_kernel(shape, *refs):
    n, slab, depth, block_cells = shape
    pieces, out = refs[:-1], refs[-1]
    block = lax.axis_index("grid")
    for i in range(n):
        region = i if len(pieces) == 1 else lax.bitwise_xor(block, ORDER[i])
        cells = pl.ds(pl.multiple_of(region * block_cells, LANES), block_cells)
        for level in range(depth):
            out[:, level, cells] = pieces[0][i, level] if len(pieces) == 1 else pieces[i][0, level]


def hop(value, distance, n):
    return lax.ppermute(value, "grid", [(j, j ^ distance) for j in range(n)])


def gather_pieces(piece, n):
    if n != 8:
        return [lax.all_to_all(jnp.broadcast_to(piece[None], (n,) + piece.shape), "grid", 0, 0, tiled=True)]
    pieces = {0: piece}
    for i in (6, 4, 2):
        pieces[i] = hop(piece, i, n)
    for i in (0, 2, 4, 6):
        pieces[i + 1] = hop(pieces[i], 1, n)
    return [pieces[i] for i in range(n)]


def exchange_parts(parts, n):
    if len(parts) == 1:
        return [lax.all_to_all(parts[0], "grid", 0, 0, tiled=True)]
    pieces = {0: parts[0]}
    for part, distances in zip(parts[1:], PARTS[1:]):
        pieces[distances[0]] = hop(part, distances[0], n)
        if len(distances) == 2:
            pieces[distances[1]] = hop(pieces[distances[0]][1:], 1, n)
    return [pieces[i] for i in ORDER]


def body(prior, channel_weights, obs_owner, obs_offset, obs_value, obs_error, ancestors):
    n, lev = lax.axis_size("grid"), lax.axis_size("lev")
    slab, depth, cells = prior.shape
    members = slab * n
    block_cells = cells // n
    groups = channel_weights.shape[1]
    count = obs_offset.shape[2]
    width = NB * groups * count
    scale = n / 2.0
    shape = jax.ShapeDtypeStruct
    parents = ancestors[:, 0]
    tall = width // LANES * slab + 8

    piece = call(
        functools.partial(pick_kernel, (slab, depth, block_cells, groups, count)),
        shape((tall, LANES), F32),
        [PLACE] * 5,
        scratch=[
            pltpu.SMEM(obs_owner.shape, jnp.int32),
            pltpu.VMEM(channel_weights.shape, F32),
            pltpu.VMEM(obs_offset.shape, jnp.int32),
            pltpu.VMEM(parents.shape, jnp.int32),
            pltpu.VMEM(prior.shape, F32),
            pltpu.SemaphoreType.DMA((5,)),
        ],
        moved=10**6,
        limit=None,
    )(obs_owner, channel_weights, obs_offset, parents, prior)
    pieces = gather_pieces(piece, n)
    send = call(
        functools.partial(retile_kernel, (n, slab, depth, block_cells)),
        shape((n, depth, slab, block_cells), F32),
        [VMEM],
        moved=10**6,
    )(prior)
    fields = lax.all_to_all(send, "grid", 0, 0, tiled=True)

    rows, steps = call(
        functools.partial(prep_kernel, (block_cells, count, scale, members)),
        [shape((SPARE, LANES), F32), shape((NB + 1, members, members), F32)],
        [SMEM, VMEM, VMEM, VMEM, VMEM],
        moved=10**6,
    )(obs_owner, obs_offset, obs_value, obs_error, parents)

    slim_height = (NB - 1) * groups * count + 2 * count + SPARE
    own, slim = call(
        functools.partial(turn_kernel, (n, slab, width, count)),
        [shape((width + SPARE, members), F32), shape((slim_height, members), F32)],
        [SMEM, VMEM, PLACE] + [VMEM] * len(pieces),
        scratch=[pltpu.VMEM((n, tall, LANES), F32)],
        moved=10**6,
    )(obs_owner, rows, send, *pieces)
    far = lax.ppermute(slim, "lev", [(j, j ^ 2) for j in range(lev)])
    near = lax.ppermute(own, "lev", [(j, j ^ 1) for j in range(lev)])
    passed, fields = lax.optimization_barrier((far, fields))
    cross = lax.ppermute(passed, "lev", [(j, j ^ 1) for j in range(lev)])

    pull = call(
        functools.partial(chain_kernel, (members, groups, count)),
        shape((8, members), F32),
        [VMEM] * 5,
        moved=10**5,
    )(own, near, far, cross, steps)

    if n == 8:
        layout = [shape((len(part), depth, slab, block_cells), F32) for part in PARTS]
    else:
        layout = [shape((n, depth, slab, block_cells), F32)]
    send = call(
        functools.partial(mix_kernel, (n, slab, depth, block_cells)),
        layout,
        [VMEM] * 3,
        scratch=[pltpu.VMEM((n, slab, members), F32)],
        flops=10**8,
        moved=10**6,
    )(steps, pull, fields)
    moved = exchange_parts(send, n)

    return call(
        functools.partial(final_kernel, (n, slab, depth, block_cells)),
        shape((slab, depth, cells), F32),
        [VMEM] * len(moved),
        moved=10**6,
    )(*moved)


def solution(mesh):
    in_specs = (
        P("grid", "lev", None),
        P("lev", None),
        P(),
        P(),
        P(None, "lev", None),
        P(None, "lev", None),
        P(None, "lev", "grid", None),
    )
    out_specs = P("grid", "lev", None)
    return jax.shard_map(body, mesh=mesh, in_specs=in_specs, out_specs=out_specs, check_vma=False)
```

```python
import functools

import jax
import jax.numpy as jnp
from jax import lax
from jax.experimental import pallas as pl
from jax.experimental.pallas import tpu as pltpu
from jax.sharding import PartitionSpec as P

NB = 4
HIGH = lax.Precision.HIGHEST
LANES = 128
F32 = jnp.float32
VMEM = pl.BlockSpec(memory_space=pltpu.VMEM)
SMEM = pl.BlockSpec(memory_space=pltpu.SMEM)
PLACE = pl.BlockSpec(memory_space=pl.ANY)
LIMIT = 48 * 1024 * 1024

PARTS = ((0,), (6, 7), (4,), (5,), (2,), (3,), (1,))
ORDER = (0, 6, 4, 5, 2, 3, 1, 7)
PAIRS = [(e, b) for b in range(1, NB) for e in range(b)]
PARENT, ALPHA, LATER, VALUE, OWN, SPARE = 0, 6, 12, 18, 22, 32


def call(kernel, out_shapes, in_specs, scratch=(), flops=0, moved=0, limit=LIMIT):
    many = isinstance(out_shapes, (list, tuple))
    return pl.pallas_call(
        kernel,
        out_shape=out_shapes,
        in_specs=in_specs,
        out_specs=[VMEM] * len(out_shapes) if many else VMEM,
        scratch_shapes=list(scratch),
        compiler_params=pltpu.CompilerParams(vmem_limit_bytes=limit),
        cost_estimate=pl.CostEstimate(flops=flops, bytes_accessed=moved, transcendentals=0),
    )


def high_dot(a, b):
    return lax.dot_general(a, b, (((1,), (0,)), ((), ())), precision=HIGH, preferred_element_type=F32)


def lane_take(value, row):
    where = jnp.broadcast_to(row, value.shape)
    return jnp.take_along_axis(value, where, axis=1, mode="promise_in_bounds")


def pick_kernel(shape, *refs):
    slab, depth, block_cells, groups, count = shape
    out, arrivals = refs[5], refs[11]
    copies = [pltpu.make_async_copy(refs[i], refs[6 + i], arrivals.at[i]) for i in range(5)]
    for copy in copies:
        copy.start()
    for copy in copies:
        copy.wait()
    owner, weights, offsets, ancestors, prior = refs[6:11]
    width = groups * count
    per = LANES // count
    for b in range(NB):
        start = pl.multiple_of(owner[b] * block_cells, LANES)
        levels = [prior[:, level, pl.ds(start, block_cells)] for level in range(depth)]
        for c in range(width // LANES):
            cell = jnp.concatenate([offsets[b, g : g + 1, :] for g in range(c * per, (c + 1) * per)], axis=1)
            low, high = lax.rem(cell, LANES), lax.div(cell, LANES)
            total = jnp.zeros((slab, LANES), F32)
            for level in range(depth):
                found = jnp.zeros((slab, LANES), F32)
                for h in range(block_cells // LANES):
                    part = lane_take(levels[level][:, h * LANES : (h + 1) * LANES], low)
                    found = jnp.where(high == h, part, found)
                row = jnp.concatenate(
                    [
                        jnp.broadcast_to(weights[level : level + 1, g : g + 1], (1, count))
                        for g in range(c * per, (c + 1) * per)
                    ],
                    axis=1,
                )
                total = total + found * row
            line = (b * width // LANES + c) * slab
            out[line : line + slab, :] = total
    line = NB * width // LANES * slab
    out[line:, :] = jnp.zeros((out.shape[0] - line, LANES), F32)
    for b in range(NB):
        out[line + b : line + b + 1, :] = ancestors[b].astype(F32)


def retile_kernel(shape, prior, out):
    n, slab, depth, block_cells = shape
    for i in range(n):
        for level in range(depth):
            out[i, level] = prior[:, level, i * block_cells : (i + 1) * block_cells]


def prep_kernel(shape, owner, offsets, values, errors, ancestors, rows, steps):
    block_cells, count, scale, members = shape
    block, group = lax.axis_index("grid"), lax.axis_index("lev")
    index = lax.broadcasted_iota(jnp.int32, (8, 1), 0)
    region = jnp.full((8, 1), block, jnp.int32)
    for b in range(1, NB):
        region = jnp.where(index == b - 1, owner[b], region)
    centre = region.astype(F32) + 0.5
    rows[...] = jnp.zeros((SPARE, LANES), F32)
    row = lax.broadcasted_iota(jnp.int32, (members, members), 0)
    column = lax.broadcasted_iota(jnp.int32, (members, members), 1)
    turned = (row == column).astype(F32)
    for b in range(NB):
        cells = owner[b] * block_cells + offsets[b, pl.ds(group, 1), :]
        distance = (centre - cells.astype(F32) / block_cells) / scale
        taper = jnp.exp(-0.5 * distance * distance)
        alpha = 0.8 * (1.0 - jnp.exp(-jnp.sum(taper, axis=1, keepdims=True) / count))
        error = errors[b]
        part = (-0.5 / count) * (taper / (error * error))
        for later in range(b + 1, NB):
            i = PAIRS.index((b, later))
            rows[ALPHA + i : ALPHA + i + 1, :] = jnp.broadcast_to(alpha[later - 1 : later], (1, LANES))
            rows[LATER + i : LATER + i + 1, :count] = part[later - 1 : later]
        rows[VALUE + b : VALUE + b + 1, :count] = values[b]
        rows[OWN + b : OWN + b + 1, :count] = part[NB - 1 : NB]
        steps[b] = turned.T
        own = alpha[NB - 1 : NB]
        turned = own * lane_take(turned, ancestors[b]) + (1.0 - own) * turned
    steps[NB] = turned.T


def join_kernel(shape, rows, ahead, *refs):
    tall, out = shape[0], refs[-1]
    for i, piece in enumerate(refs[:-1]):
        out[i * tall : (i + 1) * tall, :] = piece[...]
    out[(len(refs) - 1) * tall :, :] = rows[...]


def turn_kernel(shape, owner, *refs):
    n, slab, width, count, tall = shape
    gathered, out, slim, held = refs[:-3], refs[-3], refs[-2], refs[-1]
    members = n * slab
    block, group = lax.axis_index("grid"), lax.axis_index("lev")
    if n == 8:
        for y, part in enumerate(gathered):
            for i in range(n // 2):
                held[lax.bitwise_xor(block, 2 * i + y)] = part[i * tall : (i + 1) * tall, :]
        rows = gathered[0][n // 2 * tall :, :]
    else:
        held[...] = gathered[0][...]
        rows = gathered[1][...]
    common = width // NB * (NB - 1)
    for i in range(width // LANES):
        value = held[:, i * slab : (i + 1) * slab, :].reshape(members, LANES).T
        out[i * LANES : (i + 1) * LANES, :] = value
        if (i + 1) * LANES <= common:
            slim[i * LANES : (i + 1) * LANES, :] = value
    start = pl.multiple_of(common + lax.bitwise_xor(group, 1) * count, count)
    slim[common : common + count, :] = out[pl.ds(start, count), :]
    low = common + count
    out[width:, :] = rows
    slim[low:, :] = rows
    line = width // LANES * slab
    for i, (e, b) in enumerate(PAIRS):
        value = held[owner[b], line + e : line + e + 1, :]
        out[width + PARENT + i : width + PARENT + i + 1, :] = value
        slim[low + PARENT + i : low + PARENT + i + 1, :] = value


def mix_kernel(shape, steps, pull, fields, *refs):
    n, slab, depth, block_cells = shape
    outs, held = refs[:-1], refs[-1]
    members = n * slab
    held[...] = (steps[NB] + pull[0:1, :]).reshape(n, slab, members)
    block = lax.axis_index("grid")
    if len(outs) == 1:
        blend = held[...].reshape(members, members)
    else:
        blend = jnp.concatenate([held[lax.bitwise_xor(block, i)] for i in range(n)], axis=0)
    for level in range(depth):
        value = high_dot(blend, fields[:, level].reshape(members, block_cells)).reshape(n, slab, block_cells)
        if len(outs) == 1:
            outs[0][:, level] = value
        else:
            for out, part in zip(outs, PARTS):
                for i, distance in enumerate(part):
                    out[i, level] = value[distance]


def chain_kernel(shape, own, near, far, cross, steps, out):
    members, groups, count = shape
    width = groups * count
    group = lax.axis_index("lev")
    sources = [own, near, far, cross]
    bases = [NB * width, (NB - 1) * width + count, NB * width, (NB - 1) * width + count]
    columns = [source[base : base + SPARE, :].T for source, base in zip(sources, bases)]
    parents, alphas = [], []
    for source, base in zip(sources, bases):
        parents.append(source[base + PARENT : base + PARENT + 8, :].astype(jnp.int32))
        alphas.append(source[base + ALPHA : base + ALPHA + 6, :])
    tilts = {}
    pulled = []
    for b in range(NB):
        kinds = [(q, later) for q in range(groups) for later in range(b + 1, NB)] + [(0, None)]
        height = -(-len(kinds) // 8) * 8
        index = lax.broadcasted_iota(jnp.int32, (height, members), 0)
        logs = jnp.zeros((height, members), F32)
        for q in range(groups if b < NB - 1 else 1):
            start = pl.multiple_of(b * width + lax.bitwise_xor(group, q) * count, count)
            total = jnp.zeros((count, members), F32)
            tilted = jnp.zeros((count, members), F32)
            for p, source in enumerate(sources):
                if b == NB - 1 and p % 2 == 1:
                    value = source[b * width : b * width + count, :]
                else:
                    value = source[pl.ds(start, count), :]
                for e in range(b):
                    i = PAIRS.index((e, b))
                    tilted = tilted + value * tilts[e, p, b]
                    alpha = alphas[p][i : i + 1]
                    moved = lane_take(value, parents[p][i : i + 1])
                    value = alpha * moved + (1.0 - alpha) * value
                total = total + value
            if b > 0:
                total = total + jnp.sum(tilted, axis=1, keepdims=True)
            miss = columns[q][:count, VALUE + b : VALUE + b + 1] - total
            square = miss * miss
            for row, (owner_group, later) in enumerate(kinds):
                if owner_group != q:
                    continue
                at = OWN + b if later is None else LATER + PAIRS.index((b, later))
                log = jnp.sum(columns[q][:count, at : at + 1] * square, axis=0, keepdims=True)
                logs = jnp.where(index == row, log, logs)
        expo = jnp.exp(logs - jnp.max(logs, axis=1, keepdims=True))
        tilt = expo / jnp.sum(expo, axis=1, keepdims=True) - 1.0 / members
        for row, (q, later) in enumerate(kinds):
            if later is None:
                pulled.append(tilt[row : row + 1])
            else:
                tilts[b, q, later] = tilt[row : row + 1]
    pull = jnp.zeros((8, members), F32)
    for b in range(NB):
        pull = pull + high_dot(jnp.broadcast_to(pulled[b], (8, members)), steps[b])
    out[...] = pull


def final_kernel(shape, *refs):
    n, slab, depth, block_cells = shape
    pieces, out = refs[:-1], refs[-1]
    block = lax.axis_index("grid")
    for i in range(n):
        region = i if len(pieces) == 1 else lax.bitwise_xor(block, ORDER[i])
        cells = pl.ds(pl.multiple_of(region * block_cells, LANES), block_cells)
        for level in range(depth):
            out[:, level, cells] = pieces[0][i, level] if len(pieces) == 1 else pieces[i][0, level]


def hop(value, distance, n):
    return lax.ppermute(value, "grid", [(j, j ^ distance) for j in range(n)])


def exchange_parts(parts, n):
    if len(parts) == 1:
        return [lax.all_to_all(parts[0], "grid", 0, 0, tiled=True)]
    pieces = {0: parts[0]}
    for part, distances in zip(parts[1:], PARTS[1:]):
        pieces[distances[0]] = hop(part, distances[0], n)
        if len(distances) == 2:
            pieces[distances[1]] = hop(pieces[distances[0]][1:], 1, n)
    return [pieces[i] for i in ORDER]


def body(prior, channel_weights, obs_owner, obs_offset, obs_value, obs_error, ancestors):
    n, lev = lax.axis_size("grid"), lax.axis_size("lev")
    slab, depth, cells = prior.shape
    members = slab * n
    block_cells = cells // n
    groups = channel_weights.shape[1]
    count = obs_offset.shape[2]
    width = NB * groups * count
    scale = n / 2.0
    shape = jax.ShapeDtypeStruct
    parents = ancestors[:, 0]
    tall = width // LANES * slab + 8

    piece = call(
        functools.partial(pick_kernel, (slab, depth, block_cells, groups, count)),
        shape((tall, LANES), F32),
        [PLACE] * 5,
        scratch=[
            pltpu.SMEM(obs_owner.shape, jnp.int32),
            pltpu.VMEM(channel_weights.shape, F32),
            pltpu.VMEM(obs_offset.shape, jnp.int32),
            pltpu.VMEM(parents.shape, jnp.int32),
            pltpu.VMEM(prior.shape, F32),
            pltpu.SemaphoreType.DMA((5,)),
        ],
        moved=10**6,
        limit=None,
    )(obs_owner, channel_weights, obs_offset, parents, prior)

    send = call(
        functools.partial(retile_kernel, (n, slab, depth, block_cells)),
        shape((n, depth, slab, block_cells), F32),
        [VMEM],
        moved=10**6,
    )(prior)
    fields = lax.all_to_all(send, "grid", 0, 0, tiled=True)

    rows, steps = call(
        functools.partial(prep_kernel, (block_cells, count, scale, members)),
        [shape((SPARE, LANES), F32), shape((NB + 1, members, members), F32)],
        [SMEM, VMEM, VMEM, VMEM, VMEM],
        moved=10**6,
    )(obs_owner, obs_offset, obs_value, obs_error, parents)

    across = [(j, j ^ 2) for j in range(lev)]
    beside = [(j, j ^ 1) for j in range(lev)]
    if n == 8:
        pieces = [piece] + [hop(piece, i, n) for i in (2, 4, 6)]
        here = call(
            functools.partial(join_kernel, (tall,)),
            shape((len(pieces) * tall + SPARE, LANES), F32),
            [VMEM, PLACE] + [VMEM] * len(pieces),
            moved=10**5,
        )(rows, send, *pieces)
        gathered = [here, hop(here, 1, n)]
    else:
        every = jnp.broadcast_to(piece[None], (n,) + piece.shape)
        gathered = [lax.all_to_all(every, "grid", 0, 0, tiled=True), rows]

    def turn(parts):
        return call(
            functools.partial(turn_kernel, (n, slab, width, count, tall)),
            [
                shape((width + SPARE, members), F32),
                shape((width // NB * (NB - 1) + count + SPARE, members), F32),
            ],
            [SMEM] + [VMEM] * len(parts),
            scratch=[pltpu.VMEM((n, tall, LANES), F32)],
            moved=10**6,
        )(obs_owner, *parts)

    arriving = [lax.ppermute(part, "lev", across) for part in gathered]
    own, slim = turn(gathered)
    near = lax.ppermute(slim, "lev", beside)
    far, slim = turn(arriving)
    cross = lax.ppermute(slim, "lev", beside)

    pull = call(
        functools.partial(chain_kernel, (members, groups, count)),
        shape((8, members), F32),
        [VMEM] * 5,
        moved=10**5,
    )(own, near, far, cross, steps)

    if n == 8:
        layout = [shape((len(part), depth, slab, block_cells), F32) for part in PARTS]
    else:
        layout = [shape((n, depth, slab, block_cells), F32)]
    send = call(
        functools.partial(mix_kernel, (n, slab, depth, block_cells)),
        layout,
        [VMEM] * 3,
        scratch=[pltpu.VMEM((n, slab, members), F32)],
        flops=10**8,
        moved=10**6,
    )(steps, pull, fields)
    moved = exchange_parts(send, n)

    return call(
        functools.partial(final_kernel, (n, slab, depth, block_cells)),
        shape((slab, depth, cells), F32),
        [VMEM] * len(moved),
        moved=10**6,
    )(*moved)


def solution(mesh):
    in_specs = (
        P("grid", "lev", None),
        P("lev", None),
        P(),
        P(),
        P(None, "lev", None),
        P(None, "lev", None),
        P(None, "lev", "grid", None),
    )
    out_specs = P("grid", "lev", None)
    return jax.shard_map(body, mesh=mesh, in_specs=in_specs, out_specs=out_specs, check_vma=False)
```

```python
import functools

import jax
import jax.numpy as jnp
from jax import lax
from jax.experimental import pallas as pl
from jax.experimental.pallas import tpu as pltpu
from jax.sharding import PartitionSpec as P

NB = 4
HIGH = lax.Precision.HIGHEST
LANES = 128
F32 = jnp.float32
VMEM = pl.BlockSpec(memory_space=pltpu.VMEM)
SMEM = pl.BlockSpec(memory_space=pltpu.SMEM)
PLACE = pl.BlockSpec(memory_space=pl.ANY)
LIMIT = 48 * 1024 * 1024

PARTS = ((0,), (6, 7), (4,), (5,), (2, 3), (1,))
ORDER = (0, 6, 4, 5, 2, 1, 3, 7)
PAIRS = [(e, b) for b in range(1, NB) for e in range(b)]
PARENT, ALPHA, LATER, VALUE, OWN, SPARE = 0, 6, 12, 18, 22, 32


def call(kernel, out_shapes, in_specs, scratch=(), flops=0, moved=0, limit=LIMIT):
    many = isinstance(out_shapes, (list, tuple))
    return pl.pallas_call(
        kernel,
        out_shape=out_shapes,
        in_specs=in_specs,
        out_specs=[VMEM] * len(out_shapes) if many else VMEM,
        scratch_shapes=list(scratch),
        compiler_params=pltpu.CompilerParams(vmem_limit_bytes=limit),
        cost_estimate=pl.CostEstimate(flops=flops, bytes_accessed=moved, transcendentals=0),
    )


def high_dot(a, b):
    return lax.dot_general(a, b, (((1,), (0,)), ((), ())), precision=HIGH, preferred_element_type=F32)


def lane_take(value, row):
    where = jnp.broadcast_to(row, value.shape)
    return jnp.take_along_axis(value, where, axis=1, mode="promise_in_bounds")


def pick_kernel(shape, *refs):
    slab, depth, block_cells, groups, count = shape
    out, arrivals = refs[5], refs[11]
    copies = [pltpu.make_async_copy(refs[i], refs[6 + i], arrivals.at[i]) for i in range(5)]
    for copy in copies:
        copy.start()
    for copy in copies:
        copy.wait()
    owner, weights, offsets, ancestors, prior = refs[6:11]
    width = groups * count
    per = LANES // count
    for b in range(NB):
        start = pl.multiple_of(owner[b] * block_cells, LANES)
        levels = [prior[:, level, pl.ds(start, block_cells)] for level in range(depth)]
        for c in range(width // LANES):
            cell = jnp.concatenate([offsets[b, g : g + 1, :] for g in range(c * per, (c + 1) * per)], axis=1)
            low, high = lax.rem(cell, LANES), lax.div(cell, LANES)
            total = jnp.zeros((slab, LANES), F32)
            for level in range(depth):
                found = jnp.zeros((slab, LANES), F32)
                for h in range(block_cells // LANES):
                    part = lane_take(levels[level][:, h * LANES : (h + 1) * LANES], low)
                    found = jnp.where(high == h, part, found)
                row = jnp.concatenate(
                    [
                        jnp.broadcast_to(weights[level : level + 1, g : g + 1], (1, count))
                        for g in range(c * per, (c + 1) * per)
                    ],
                    axis=1,
                )
                total = total + found * row
            line = (b * width // LANES + c) * slab
            out[line : line + slab, :] = total
    line = NB * width // LANES * slab
    out[line:, :] = jnp.zeros((out.shape[0] - line, LANES), F32)
    for b in range(NB):
        out[line + b : line + b + 1, :] = ancestors[b].astype(F32)


def retile_kernel(shape, prior, out):
    n, slab, depth, block_cells = shape
    for i in range(n):
        for level in range(depth):
            out[i, level] = prior[:, level, i * block_cells : (i + 1) * block_cells]


def prep_kernel(shape, owner, offsets, values, errors, ancestors, rows, steps):
    block_cells, count, scale, members = shape
    block, group = lax.axis_index("grid"), lax.axis_index("lev")
    index = lax.broadcasted_iota(jnp.int32, (8, 1), 0)
    region = jnp.full((8, 1), block, jnp.int32)
    for b in range(1, NB):
        region = jnp.where(index == b - 1, owner[b], region)
    centre = region.astype(F32) + 0.5
    rows[...] = jnp.zeros((SPARE, LANES), F32)
    row = lax.broadcasted_iota(jnp.int32, (members, members), 0)
    column = lax.broadcasted_iota(jnp.int32, (members, members), 1)
    turned = (row == column).astype(F32)
    for b in range(NB):
        cells = owner[b] * block_cells + offsets[b, pl.ds(group, 1), :]
        distance = (centre - cells.astype(F32) / block_cells) / scale
        taper = jnp.exp(-0.5 * distance * distance)
        alpha = 0.8 * (1.0 - jnp.exp(-jnp.sum(taper, axis=1, keepdims=True) / count))
        error = errors[b]
        part = (-0.5 / count) * (taper / (error * error))
        for later in range(b + 1, NB):
            i = PAIRS.index((b, later))
            rows[ALPHA + i : ALPHA + i + 1, :] = jnp.broadcast_to(alpha[later - 1 : later], (1, LANES))
            rows[LATER + i : LATER + i + 1, :count] = part[later - 1 : later]
        rows[VALUE + b : VALUE + b + 1, :count] = values[b]
        rows[OWN + b : OWN + b + 1, :count] = part[NB - 1 : NB]
        steps[b] = turned.T
        own = alpha[NB - 1 : NB]
        turned = own * lane_take(turned, ancestors[b]) + (1.0 - own) * turned
    steps[NB] = turned.T


def join_kernel(shape, rows, ahead, *refs):
    tall, out = shape[0], refs[-1]
    for i, piece in enumerate(refs[:-1]):
        out[i * tall : (i + 1) * tall, :] = piece[...]
    out[(len(refs) - 1) * tall :, :] = rows[...]


def turn_kernel(shape, owner, *refs):
    n, slab, width, count, tall = shape
    gathered, out, slim, held = refs[:-3], refs[-3], refs[-2], refs[-1]
    members = n * slab
    block, group = lax.axis_index("grid"), lax.axis_index("lev")
    if n == 8:
        for y, part in enumerate(gathered):
            for i in range(n // 2):
                held[lax.bitwise_xor(block, 2 * i + y)] = part[i * tall : (i + 1) * tall, :]
        rows = gathered[0][n // 2 * tall :, :]
    else:
        held[...] = gathered[0][...]
        rows = gathered[1][...]
    common = width // NB * (NB - 1)
    for i in range(width // LANES):
        value = held[:, i * slab : (i + 1) * slab, :].reshape(members, LANES).T
        out[i * LANES : (i + 1) * LANES, :] = value
        if (i + 1) * LANES <= common:
            slim[i * LANES : (i + 1) * LANES, :] = value
    start = pl.multiple_of(common + lax.bitwise_xor(group, 1) * count, count)
    slim[common : common + count, :] = out[pl.ds(start, count), :]
    low = common + count
    out[width:, :] = rows
    slim[low:, :] = rows
    line = width // LANES * slab
    for i, (e, b) in enumerate(PAIRS):
        value = held[owner[b], line + e : line + e + 1, :]
        out[width + PARENT + i : width + PARENT + i + 1, :] = value
        slim[low + PARENT + i : low + PARENT + i + 1, :] = value


def mix_kernel(shape, steps, pull, fields, *refs):
    n, slab, depth, block_cells = shape
    outs, held = refs[:-1], refs[-1]
    members = n * slab
    held[...] = (steps[NB] + pull[0:1, :]).reshape(n, slab, members)
    block = lax.axis_index("grid")
    if len(outs) == 1:
        blend = held[...].reshape(members, members)
    else:
        blend = jnp.concatenate([held[lax.bitwise_xor(block, i)] for i in range(n)], axis=0)
    for level in range(depth):
        value = high_dot(blend, fields[:, level].reshape(members, block_cells)).reshape(n, slab, block_cells)
        if len(outs) == 1:
            outs[0][:, level] = value
        else:
            for out, part in zip(outs, PARTS):
                for i, distance in enumerate(part):
                    out[i, level] = value[distance]


def chain_kernel(shape, own, near, far, cross, steps, out):
    members, groups, count = shape
    width = groups * count
    group = lax.axis_index("lev")
    sources = [own, near, far, cross]
    bases = [NB * width, (NB - 1) * width + count, NB * width, (NB - 1) * width + count]
    columns = [source[base : base + SPARE, :].T for source, base in zip(sources, bases)]
    parents, alphas = [], []
    for source, base in zip(sources, bases):
        parents.append(source[base + PARENT : base + PARENT + 8, :].astype(jnp.int32))
        alphas.append(source[base + ALPHA : base + ALPHA + 6, :])
    tilts = {}
    pulled = []
    for b in range(NB):
        kinds = [(q, later) for q in range(groups) for later in range(b + 1, NB)] + [(0, None)]
        height = -(-len(kinds) // 8) * 8
        index = lax.broadcasted_iota(jnp.int32, (height, members), 0)
        logs = jnp.zeros((height, members), F32)
        for q in range(groups if b < NB - 1 else 1):
            start = pl.multiple_of(b * width + lax.bitwise_xor(group, q) * count, count)
            total = jnp.zeros((count, members), F32)
            tilted = jnp.zeros((count, members), F32)
            for p, source in enumerate(sources):
                if b == NB - 1 and p % 2 == 1:
                    value = source[b * width : b * width + count, :]
                else:
                    value = source[pl.ds(start, count), :]
                for e in range(b):
                    i = PAIRS.index((e, b))
                    tilted = tilted + value * tilts[e, p, b]
                    alpha = alphas[p][i : i + 1]
                    moved = lane_take(value, parents[p][i : i + 1])
                    value = alpha * moved + (1.0 - alpha) * value
                total = total + value
            if b > 0:
                total = total + jnp.sum(tilted, axis=1, keepdims=True)
            miss = columns[q][:count, VALUE + b : VALUE + b + 1] - total
            square = miss * miss
            for row, (owner_group, later) in enumerate(kinds):
                if owner_group != q:
                    continue
                at = OWN + b if later is None else LATER + PAIRS.index((b, later))
                log = jnp.sum(columns[q][:count, at : at + 1] * square, axis=0, keepdims=True)
                logs = jnp.where(index == row, log, logs)
        expo = jnp.exp(logs - jnp.max(logs, axis=1, keepdims=True))
        tilt = expo / jnp.sum(expo, axis=1, keepdims=True) - 1.0 / members
        for row, (q, later) in enumerate(kinds):
            if later is None:
                pulled.append(tilt[row : row + 1])
            else:
                tilts[b, q, later] = tilt[row : row + 1]
    pull = jnp.zeros((8, members), F32)
    for b in range(NB):
        pull = pull + high_dot(jnp.broadcast_to(pulled[b], (8, members)), steps[b])
    out[...] = pull


def final_kernel(shape, *refs):
    n, slab, depth, block_cells = shape
    pieces, out = refs[:-1], refs[-1]
    block = lax.axis_index("grid")
    for i in range(n):
        region = i if len(pieces) == 1 else lax.bitwise_xor(block, ORDER[i])
        cells = pl.ds(pl.multiple_of(region * block_cells, LANES), block_cells)
        for level in range(depth):
            out[:, level, cells] = pieces[0][i, level] if len(pieces) == 1 else pieces[i][0, level]


def hop(value, distance, n):
    return lax.ppermute(value, "grid", [(j, j ^ distance) for j in range(n)])


def exchange_parts(parts, n):
    if len(parts) == 1:
        return [lax.all_to_all(parts[0], "grid", 0, 0, tiled=True)]
    pieces = {0: parts[0]}
    for part, distances in zip(parts[1:], PARTS[1:]):
        pieces[distances[0]] = hop(part, distances[0], n)
        if len(distances) == 2:
            pieces[distances[1]] = hop(pieces[distances[0]][1:], 1, n)
    return [pieces[i] for i in ORDER]


def body(prior, channel_weights, obs_owner, obs_offset, obs_value, obs_error, ancestors):
    n, lev = lax.axis_size("grid"), lax.axis_size("lev")
    slab, depth, cells = prior.shape
    members = slab * n
    block_cells = cells // n
    groups = channel_weights.shape[1]
    count = obs_offset.shape[2]
    width = NB * groups * count
    scale = n / 2.0
    shape = jax.ShapeDtypeStruct
    parents = ancestors[:, 0]
    tall = width // LANES * slab + 8

    piece = call(
        functools.partial(pick_kernel, (slab, depth, block_cells, groups, count)),
        shape((tall, LANES), F32),
        [PLACE] * 5,
        scratch=[
            pltpu.SMEM(obs_owner.shape, jnp.int32),
            pltpu.VMEM(channel_weights.shape, F32),
            pltpu.VMEM(obs_offset.shape, jnp.int32),
            pltpu.VMEM(parents.shape, jnp.int32),
            pltpu.VMEM(prior.shape, F32),
            pltpu.SemaphoreType.DMA((5,)),
        ],
        moved=10**6,
        limit=None,
    )(obs_owner, channel_weights, obs_offset, parents, prior)

    send = call(
        functools.partial(retile_kernel, (n, slab, depth, block_cells)),
        shape((n, depth, slab, block_cells), F32),
        [VMEM],
        moved=10**6,
    )(prior)
    fields = lax.all_to_all(send, "grid", 0, 0, tiled=True)

    rows, steps = call(
        functools.partial(prep_kernel, (block_cells, count, scale, members)),
        [shape((SPARE, LANES), F32), shape((NB + 1, members, members), F32)],
        [SMEM, VMEM, VMEM, VMEM, VMEM],
        moved=10**6,
    )(obs_owner, obs_offset, obs_value, obs_error, parents)

    across = [(j, j ^ 2) for j in range(lev)]
    beside = [(j, j ^ 1) for j in range(lev)]
    if n == 8:
        pieces = [piece] + [hop(piece, i, n) for i in (2, 4, 6)]
        here = call(
            functools.partial(join_kernel, (tall,)),
            shape((len(pieces) * tall + SPARE, LANES), F32),
            [VMEM, PLACE] + [VMEM] * len(pieces),
            moved=10**5,
        )(rows, send, *pieces)
        gathered = [here, hop(here, 1, n)]
    else:
        every = jnp.broadcast_to(piece[None], (n,) + piece.shape)
        gathered = [lax.all_to_all(every, "grid", 0, 0, tiled=True), rows]

    def turn(parts):
        return call(
            functools.partial(turn_kernel, (n, slab, width, count, tall)),
            [
                shape((width + SPARE, members), F32),
                shape((width // NB * (NB - 1) + count + SPARE, members), F32),
            ],
            [SMEM] + [VMEM] * len(parts),
            scratch=[pltpu.VMEM((n, tall, LANES), F32)],
            moved=10**6,
        )(obs_owner, *parts)

    arriving = []
    for part in gathered:
        if arriving:
            part, arriving[0] = lax.optimization_barrier((part, arriving[0]))
        arriving.append(lax.ppermute(part, "lev", across))
    own, slim = turn(gathered)
    near = lax.ppermute(slim, "lev", beside)
    far, slim = turn(arriving)
    cross = lax.ppermute(slim, "lev", beside)

    pull = call(
        functools.partial(chain_kernel, (members, groups, count)),
        shape((8, members), F32),
        [VMEM] * 5,
        moved=10**5,
    )(own, near, far, cross, steps)

    if n == 8:
        layout = [shape((len(part), depth, slab, block_cells), F32) for part in PARTS]
    else:
        layout = [shape((n, depth, slab, block_cells), F32)]
    send = call(
        functools.partial(mix_kernel, (n, slab, depth, block_cells)),
        layout,
        [VMEM] * 3,
        scratch=[pltpu.VMEM((n, slab, members), F32)],
        flops=10**8,
        moved=10**6,
    )(steps, pull, fields)
    moved = exchange_parts(send, n)

    return call(
        functools.partial(final_kernel, (n, slab, depth, block_cells)),
        shape((slab, depth, cells), F32),
        [VMEM] * len(moved),
        moved=10**6,
    )(*moved)


def solution(mesh):
    in_specs = (
        P("grid", "lev", None),
        P("lev", None),
        P(),
        P(),
        P(None, "lev", None),
        P(None, "lev", None),
        P(None, "lev", "grid", None),
    )
    out_specs = P("grid", "lev", None)
    return jax.shard_map(body, mesh=mesh, in_specs=in_specs, out_specs=out_specs, check_vma=False)
```

```python
import functools

import jax
import jax.numpy as jnp
from jax import lax
from jax.experimental import pallas as pl
from jax.experimental.pallas import tpu as pltpu
from jax.sharding import PartitionSpec as P

NB = 4
HIGH = lax.Precision.HIGHEST
LANES = 128
F32 = jnp.float32
VMEM = pl.BlockSpec(memory_space=pltpu.VMEM)
SMEM = pl.BlockSpec(memory_space=pltpu.SMEM)
PLACE = pl.BlockSpec(memory_space=pl.ANY)
LIMIT = 48 * 1024 * 1024

PARTS = ((0,), (2, 3), (6, 7), (4,), (5,), (1,))
ARRIVING = ((0,), (2,), (6,), (4,), (5,), (1, 3), (7,))
PAIRS = [(e, b) for b in range(1, NB) for e in range(b)]
PARENT, ALPHA, LATER, VALUE, OWN, SPARE = 0, 6, 12, 18, 22, 32


def call(kernel, out_shapes, in_specs, scratch=(), flops=0, moved=0, limit=LIMIT):
    many = isinstance(out_shapes, (list, tuple))
    return pl.pallas_call(
        kernel,
        out_shape=out_shapes,
        in_specs=in_specs,
        out_specs=[VMEM] * len(out_shapes) if many else VMEM,
        scratch_shapes=list(scratch),
        compiler_params=pltpu.CompilerParams(vmem_limit_bytes=limit),
        cost_estimate=pl.CostEstimate(flops=flops, bytes_accessed=moved, transcendentals=0),
    )


def high_dot(a, b):
    return lax.dot_general(a, b, (((1,), (0,)), ((), ())), precision=HIGH, preferred_element_type=F32)


def lane_take(value, row):
    where = jnp.broadcast_to(row, value.shape)
    return jnp.take_along_axis(value, where, axis=1, mode="promise_in_bounds")


def pick_kernel(shape, *refs):
    slab, depth, block_cells, groups, count = shape
    out, arrivals = refs[5], refs[11]
    copies = [pltpu.make_async_copy(refs[i], refs[6 + i], arrivals.at[i]) for i in range(5)]
    for copy in copies:
        copy.start()
    for copy in copies:
        copy.wait()
    owner, weights, offsets, ancestors, prior = refs[6:11]
    width = groups * count
    per = LANES // count
    for b in range(NB):
        start = pl.multiple_of(owner[b] * block_cells, LANES)
        levels = [prior[:, level, pl.ds(start, block_cells)] for level in range(depth)]
        for c in range(width // LANES):
            cell = jnp.concatenate([offsets[b, g : g + 1, :] for g in range(c * per, (c + 1) * per)], axis=1)
            low, high = lax.rem(cell, LANES), lax.div(cell, LANES)
            total = jnp.zeros((slab, LANES), F32)
            for level in range(depth):
                found = jnp.zeros((slab, LANES), F32)
                for h in range(block_cells // LANES):
                    part = lane_take(levels[level][:, h * LANES : (h + 1) * LANES], low)
                    found = jnp.where(high == h, part, found)
                row = jnp.concatenate(
                    [
                        jnp.broadcast_to(weights[level : level + 1, g : g + 1], (1, count))
                        for g in range(c * per, (c + 1) * per)
                    ],
                    axis=1,
                )
                total = total + found * row
            line = (b * width // LANES + c) * slab
            out[line : line + slab, :] = total
    line = NB * width // LANES * slab
    out[line:, :] = jnp.zeros((out.shape[0] - line, LANES), F32)
    for b in range(NB):
        out[line + b : line + b + 1, :] = ancestors[b].astype(F32)


def retile_kernel(shape, prior, out):
    n, slab, depth, block_cells = shape
    for i in range(n):
        for level in range(depth):
            out[i, level] = prior[:, level, i * block_cells : (i + 1) * block_cells]


def prep_kernel(shape, owner, offsets, values, errors, ancestors, rows, steps):
    block_cells, count, scale, members = shape
    block, group = lax.axis_index("grid"), lax.axis_index("lev")
    index = lax.broadcasted_iota(jnp.int32, (8, 1), 0)
    region = jnp.full((8, 1), block, jnp.int32)
    for b in range(1, NB):
        region = jnp.where(index == b - 1, owner[b], region)
    centre = region.astype(F32) + 0.5
    rows[...] = jnp.zeros((SPARE, LANES), F32)
    row = lax.broadcasted_iota(jnp.int32, (members, members), 0)
    column = lax.broadcasted_iota(jnp.int32, (members, members), 1)
    turned = (row == column).astype(F32)
    for b in range(NB):
        cells = owner[b] * block_cells + offsets[b, pl.ds(group, 1), :]
        distance = (centre - cells.astype(F32) / block_cells) / scale
        taper = jnp.exp(-0.5 * distance * distance)
        alpha = 0.8 * (1.0 - jnp.exp(-jnp.sum(taper, axis=1, keepdims=True) / count))
        error = errors[b]
        part = (-0.5 / count) * (taper / (error * error))
        for later in range(b + 1, NB):
            i = PAIRS.index((b, later))
            rows[ALPHA + i : ALPHA + i + 1, :] = jnp.broadcast_to(alpha[later - 1 : later], (1, LANES))
            rows[LATER + i : LATER + i + 1, :count] = part[later - 1 : later]
        rows[VALUE + b : VALUE + b + 1, :count] = values[b]
        rows[OWN + b : OWN + b + 1, :count] = part[NB - 1 : NB]
        steps[b] = turned.T
        own = alpha[NB - 1 : NB]
        turned = own * lane_take(turned, ancestors[b]) + (1.0 - own) * turned
    steps[NB] = turned.T


def join_kernel(shape, rows, ahead, *refs):
    tall, out = shape[0], refs[-1]
    for i, piece in enumerate(refs[:-1]):
        out[i * tall : (i + 1) * tall, :] = piece[...]
    out[(len(refs) - 1) * tall :, :] = rows[...]


def turn_kernel(shape, owner, *refs):
    n, slab, width, count, tall = shape
    gathered, out, slim, held = refs[:-3], refs[-3], refs[-2], refs[-1]
    members = n * slab
    block, group = lax.axis_index("grid"), lax.axis_index("lev")
    if n == 8:
        for y, part in enumerate(gathered):
            for i in range(n // 2):
                held[lax.bitwise_xor(block, 2 * i + y)] = part[i * tall : (i + 1) * tall, :]
        rows = gathered[0][n // 2 * tall :, :]
    else:
        held[...] = gathered[0][...]
        rows = gathered[1][...]
    common = width // NB * (NB - 1)
    for i in range(width // LANES):
        value = held[:, i * slab : (i + 1) * slab, :].reshape(members, LANES).T
        out[i * LANES : (i + 1) * LANES, :] = value
        if (i + 1) * LANES <= common:
            slim[i * LANES : (i + 1) * LANES, :] = value
    start = pl.multiple_of(common + lax.bitwise_xor(group, 1) * count, count)
    slim[common : common + count, :] = out[pl.ds(start, count), :]
    low = common + count
    out[width:, :] = rows
    slim[low:, :] = rows
    line = width // LANES * slab
    for i, (e, b) in enumerate(PAIRS):
        value = held[owner[b], line + e : line + e + 1, :]
        out[width + PARENT + i : width + PARENT + i + 1, :] = value
        slim[low + PARENT + i : low + PARENT + i + 1, :] = value


def mix_kernel(shape, steps, pull, fields, *refs):
    n, slab, depth, block_cells = shape
    outs, held = refs[:-1], refs[-1]
    members = n * slab
    held[...] = (steps[NB] + pull[0:1, :]).reshape(n, slab, members)
    block = lax.axis_index("grid")
    if len(outs) == 1:
        blend = held[...].reshape(members, members)
    else:
        blend = jnp.concatenate([held[lax.bitwise_xor(block, i)] for i in range(n)], axis=0)
    for level in range(depth):
        value = high_dot(blend, fields[:, level].reshape(members, block_cells)).reshape(n, slab, block_cells)
        if len(outs) == 1:
            outs[0][:, level] = value
        else:
            for out, part in zip(outs, PARTS):
                for i, distance in enumerate(part):
                    out[i, level] = value[distance]


def chain_kernel(shape, own, near, far, cross, steps, out):
    members, groups, count = shape
    width = groups * count
    group = lax.axis_index("lev")
    sources = [own, near, far, cross]
    bases = [NB * width, (NB - 1) * width + count, NB * width, (NB - 1) * width + count]
    columns = [source[base : base + SPARE, :].T for source, base in zip(sources, bases)]
    parents, alphas = [], []
    for source, base in zip(sources, bases):
        parents.append(source[base + PARENT : base + PARENT + 8, :].astype(jnp.int32))
        alphas.append(source[base + ALPHA : base + ALPHA + 6, :])
    tilts = {}
    pulled = []
    for b in range(NB):
        kinds = [(q, later) for q in range(groups) for later in range(b + 1, NB)] + [(0, None)]
        height = -(-len(kinds) // 8) * 8
        index = lax.broadcasted_iota(jnp.int32, (height, members), 0)
        logs = jnp.zeros((height, members), F32)
        for q in range(groups if b < NB - 1 else 1):
            start = pl.multiple_of(b * width + lax.bitwise_xor(group, q) * count, count)
            total = jnp.zeros((count, members), F32)
            tilted = jnp.zeros((count, members), F32)
            for p, source in enumerate(sources):
                if b == NB - 1 and p % 2 == 1:
                    value = source[b * width : b * width + count, :]
                else:
                    value = source[pl.ds(start, count), :]
                for e in range(b):
                    i = PAIRS.index((e, b))
                    tilted = tilted + value * tilts[e, p, b]
                    alpha = alphas[p][i : i + 1]
                    moved = lane_take(value, parents[p][i : i + 1])
                    value = alpha * moved + (1.0 - alpha) * value
                total = total + value
            if b > 0:
                total = total + jnp.sum(tilted, axis=1, keepdims=True)
            miss = columns[q][:count, VALUE + b : VALUE + b + 1] - total
            square = miss * miss
            for row, (owner_group, later) in enumerate(kinds):
                if owner_group != q:
                    continue
                at = OWN + b if later is None else LATER + PAIRS.index((b, later))
                log = jnp.sum(columns[q][:count, at : at + 1] * square, axis=0, keepdims=True)
                logs = jnp.where(index == row, log, logs)
        expo = jnp.exp(logs - jnp.max(logs, axis=1, keepdims=True))
        tilt = expo / jnp.sum(expo, axis=1, keepdims=True) - 1.0 / members
        for row, (q, later) in enumerate(kinds):
            if later is None:
                pulled.append(tilt[row : row + 1])
            else:
                tilts[b, q, later] = tilt[row : row + 1]
    pull = jnp.zeros((8, members), F32)
    for b in range(NB):
        pull = pull + high_dot(jnp.broadcast_to(pulled[b], (8, members)), steps[b])
    out[...] = pull


def final_kernel(shape, *refs):
    n, slab, depth, block_cells = shape
    arrived, out = refs[:-1], refs[-1]
    block = lax.axis_index("grid")
    if len(arrived) == 1:
        places = [(i, 0, i) for i in range(n)]
    else:
        places = [
            (lax.bitwise_xor(block, distance), i, j)
            for i, distances in enumerate(ARRIVING)
            for j, distance in enumerate(distances)
        ]
    for region, i, j in places:
        cells = pl.ds(pl.multiple_of(region * block_cells, LANES), block_cells)
        for level in range(depth):
            out[:, level, cells] = arrived[i][j, level]


def hop(value, distance, n):
    return lax.ppermute(value, "grid", [(j, j ^ distance) for j in range(n)])


def exchange_parts(parts, n):
    if len(parts) == 1:
        return [lax.all_to_all(parts[0], "grid", 0, 0, tiled=True)]
    arrived = [parts[0]]
    for part, distances in zip(parts[1:-1], PARTS[1:-1]):
        arrived.append(hop(part, distances[0], n))
    last = jnp.concatenate([parts[-1], arrived[1][1:]], axis=0)
    return arrived + [hop(last, 1, n), hop(arrived[2][1:], 1, n)]


def body(prior, channel_weights, obs_owner, obs_offset, obs_value, obs_error, ancestors):
    n, lev = lax.axis_size("grid"), lax.axis_size("lev")
    slab, depth, cells = prior.shape
    members = slab * n
    block_cells = cells // n
    groups = channel_weights.shape[1]
    count = obs_offset.shape[2]
    width = NB * groups * count
    scale = n / 2.0
    shape = jax.ShapeDtypeStruct
    parents = ancestors[:, 0]
    tall = width // LANES * slab + 8

    piece = call(
        functools.partial(pick_kernel, (slab, depth, block_cells, groups, count)),
        shape((tall, LANES), F32),
        [PLACE] * 5,
        scratch=[
            pltpu.SMEM(obs_owner.shape, jnp.int32),
            pltpu.VMEM(channel_weights.shape, F32),
            pltpu.VMEM(obs_offset.shape, jnp.int32),
            pltpu.VMEM(parents.shape, jnp.int32),
            pltpu.VMEM(prior.shape, F32),
            pltpu.SemaphoreType.DMA((5,)),
        ],
        moved=10**6,
        limit=None,
    )(obs_owner, channel_weights, obs_offset, parents, prior)

    send = call(
        functools.partial(retile_kernel, (n, slab, depth, block_cells)),
        shape((n, depth, slab, block_cells), F32),
        [VMEM],
        moved=10**6,
    )(prior)
    fields = lax.all_to_all(send, "grid", 0, 0, tiled=True)

    rows, steps = call(
        functools.partial(prep_kernel, (block_cells, count, scale, members)),
        [shape((SPARE, LANES), F32), shape((NB + 1, members, members), F32)],
        [SMEM, VMEM, VMEM, VMEM, VMEM],
        moved=10**6,
    )(obs_owner, obs_offset, obs_value, obs_error, parents)

    across = [(j, j ^ 2) for j in range(lev)]
    beside = [(j, j ^ 1) for j in range(lev)]
    if n == 8:
        pieces = [piece] + [hop(piece, i, n) for i in (2, 4, 6)]
        here = call(
            functools.partial(join_kernel, (tall,)),
            shape((len(pieces) * tall + SPARE, LANES), F32),
            [VMEM, PLACE] + [VMEM] * len(pieces),
            moved=10**5,
        )(rows, send, *pieces)
        gathered = [here, hop(here, 1, n)]
    else:
        every = jnp.broadcast_to(piece[None], (n,) + piece.shape)
        gathered = [lax.all_to_all(every, "grid", 0, 0, tiled=True), rows]

    def turn(parts):
        return call(
            functools.partial(turn_kernel, (n, slab, width, count, tall)),
            [
                shape((width + SPARE, members), F32),
                shape((width // NB * (NB - 1) + count + SPARE, members), F32),
            ],
            [SMEM] + [VMEM] * len(parts),
            scratch=[pltpu.VMEM((n, tall, LANES), F32)],
            moved=10**6,
        )(obs_owner, *parts)

    arriving = [lax.ppermute(part, "lev", across) for part in gathered]
    gathered[0], arriving[0] = lax.optimization_barrier((gathered[0], arriving[0]))
    own, slim = turn(gathered)
    near = lax.ppermute(slim, "lev", beside)
    far, slim = turn(arriving)
    cross = lax.ppermute(slim, "lev", beside)

    pull = call(
        functools.partial(chain_kernel, (members, groups, count)),
        shape((8, members), F32),
        [VMEM] * 5,
        moved=10**5,
    )(own, near, far, cross, steps)

    if n == 8:
        layout = [shape((len(part), depth, slab, block_cells), F32) for part in PARTS]
    else:
        layout = [shape((n, depth, slab, block_cells), F32)]
    send = call(
        functools.partial(mix_kernel, (n, slab, depth, block_cells)),
        layout,
        [VMEM] * 3,
        scratch=[pltpu.VMEM((n, slab, members), F32)],
        flops=10**8,
        moved=10**6,
    )(steps, pull, fields)
    moved = exchange_parts(send, n)

    return call(
        functools.partial(final_kernel, (n, slab, depth, block_cells)),
        shape((slab, depth, cells), F32),
        [VMEM] * len(moved),
        moved=10**6,
    )(*moved)


def solution(mesh):
    in_specs = (
        P("grid", "lev", None),
        P("lev", None),
        P(),
        P(),
        P(None, "lev", None),
        P(None, "lev", None),
        P(None, "lev", "grid", None),
    )
    out_specs = P("grid", "lev", None)
    return jax.shard_map(body, mesh=mesh, in_specs=in_specs, out_specs=out_specs, check_vma=False)
```

```python
import functools

import jax
import jax.numpy as jnp
from jax import lax
from jax.experimental import pallas as pl
from jax.experimental.pallas import tpu as pltpu
from jax.sharding import PartitionSpec as P

NB = 4
HIGH = lax.Precision.HIGHEST
LANES = 128
F32 = jnp.float32
VMEM = pl.BlockSpec(memory_space=pltpu.VMEM)
SMEM = pl.BlockSpec(memory_space=pltpu.SMEM)
PLACE = pl.BlockSpec(memory_space=pl.ANY)
LIMIT = 48 * 1024 * 1024

PARTS = ((0,), (6, 7), (4,), (5,), (2, 3), (1,))
ORDER = (0, 6, 4, 5, 2, 1, 3, 7)
PAIRS = [(e, b) for b in range(1, NB) for e in range(b)]
PARENT, ALPHA, LATER, VALUE, OWN, SPARE = 0, 6, 12, 18, 22, 32


def call(kernel, out_shapes, in_specs, scratch=(), flops=0, moved=0, limit=LIMIT):
    many = isinstance(out_shapes, (list, tuple))
    return pl.pallas_call(
        kernel,
        out_shape=out_shapes,
        in_specs=in_specs,
        out_specs=[VMEM] * len(out_shapes) if many else VMEM,
        scratch_shapes=list(scratch),
        compiler_params=pltpu.CompilerParams(vmem_limit_bytes=limit),
        cost_estimate=pl.CostEstimate(flops=flops, bytes_accessed=moved, transcendentals=0),
    )


def high_dot(a, b):
    return lax.dot_general(a, b, (((1,), (0,)), ((), ())), precision=HIGH, preferred_element_type=F32)


def lane_take(value, row):
    where = jnp.broadcast_to(row, value.shape)
    return jnp.take_along_axis(value, where, axis=1, mode="promise_in_bounds")


def pick_kernel(shape, *refs):
    slab, depth, block_cells, groups, count = shape
    out, arrivals = refs[5], refs[11]
    copies = [pltpu.make_async_copy(refs[i], refs[6 + i], arrivals.at[i]) for i in range(5)]
    for copy in copies:
        copy.start()
    for copy in copies:
        copy.wait()
    owner, weights, offsets, ancestors, prior = refs[6:11]
    width = groups * count
    per = LANES // count
    for b in range(NB):
        start = pl.multiple_of(owner[b] * block_cells, LANES)
        levels = [prior[:, level, pl.ds(start, block_cells)] for level in range(depth)]
        for c in range(width // LANES):
            cell = jnp.concatenate([offsets[b, g : g + 1, :] for g in range(c * per, (c + 1) * per)], axis=1)
            low, high = lax.rem(cell, LANES), lax.div(cell, LANES)
            total = jnp.zeros((slab, LANES), F32)
            for level in range(depth):
                found = jnp.zeros((slab, LANES), F32)
                for h in range(block_cells // LANES):
                    part = lane_take(levels[level][:, h * LANES : (h + 1) * LANES], low)
                    found = jnp.where(high == h, part, found)
                row = jnp.concatenate(
                    [
                        jnp.broadcast_to(weights[level : level + 1, g : g + 1], (1, count))
                        for g in range(c * per, (c + 1) * per)
                    ],
                    axis=1,
                )
                total = total + found * row
            line = (b * width // LANES + c) * slab
            out[line : line + slab, :] = total
    line = NB * width // LANES * slab
    out[line:, :] = jnp.zeros((out.shape[0] - line, LANES), F32)
    for b in range(NB):
        out[line + b : line + b + 1, :] = ancestors[b].astype(F32)


def retile_kernel(shape, prior, out):
    n, slab, depth, block_cells = shape
    for i in range(n):
        for level in range(depth):
            out[i, level] = prior[:, level, i * block_cells : (i + 1) * block_cells]


def prep_kernel(shape, owner, offsets, values, errors, ancestors, rows, steps):
    block_cells, count, scale, members = shape
    block, group = lax.axis_index("grid"), lax.axis_index("lev")
    index = lax.broadcasted_iota(jnp.int32, (8, 1), 0)
    region = jnp.full((8, 1), block, jnp.int32)
    for b in range(1, NB):
        region = jnp.where(index == b - 1, owner[b], region)
    centre = region.astype(F32) + 0.5
    rows[...] = jnp.zeros((SPARE, LANES), F32)
    row = lax.broadcasted_iota(jnp.int32, (members, members), 0)
    column = lax.broadcasted_iota(jnp.int32, (members, members), 1)
    turned = (row == column).astype(F32)
    for b in range(NB):
        cells = owner[b] * block_cells + offsets[b, pl.ds(group, 1), :]
        distance = (centre - cells.astype(F32) / block_cells) / scale
        taper = jnp.exp(-0.5 * distance * distance)
        alpha = 0.8 * (1.0 - jnp.exp(-jnp.sum(taper, axis=1, keepdims=True) / count))
        error = errors[b]
        part = (-0.5 / count) * (taper / (error * error))
        for later in range(b + 1, NB):
            i = PAIRS.index((b, later))
            rows[ALPHA + i : ALPHA + i + 1, :] = jnp.broadcast_to(alpha[later - 1 : later], (1, LANES))
            rows[LATER + i : LATER + i + 1, :count] = part[later - 1 : later]
        rows[VALUE + b : VALUE + b + 1, :count] = values[b]
        rows[OWN + b : OWN + b + 1, :count] = part[NB - 1 : NB]
        steps[b] = turned.T
        own = alpha[NB - 1 : NB]
        turned = own * lane_take(turned, ancestors[b]) + (1.0 - own) * turned
    steps[NB] = turned.T


def turn_kernel(shape, owner, rows, ahead, *refs):
    n, slab, width, count = shape
    pieces, out, slim, held = refs[:-3], refs[-3], refs[-2], refs[-1]
    members = n * slab
    block, group = lax.axis_index("grid"), lax.axis_index("lev")
    if len(pieces) == 1:
        held[...] = pieces[0][...]
    else:
        for i, piece in enumerate(pieces):
            held[lax.bitwise_xor(block, i)] = piece[...]
    common = width // NB * (NB - 1)
    for i in range(width // LANES):
        value = held[:, i * slab : (i + 1) * slab, :].reshape(members, LANES).T
        out[i * LANES : (i + 1) * LANES, :] = value
        if (i + 1) * LANES <= common:
            slim[i * LANES : (i + 1) * LANES, :] = value
    for i in range(2):
        start = pl.multiple_of(common + lax.bitwise_xor(group, 2 + i) * count, count)
        slim[common + i * count : common + (i + 1) * count, :] = out[pl.ds(start, count), :]
    low = common + 2 * count
    out[width:, :] = rows[...]
    slim[low:, :] = rows[...]
    line = width // LANES * slab
    for i, (e, b) in enumerate(PAIRS):
        value = held[owner[b], line + e : line + e + 1, :]
        out[width + PARENT + i : width + PARENT + i + 1, :] = value
        slim[low + PARENT + i : low + PARENT + i + 1, :] = value


def mix_kernel(shape, steps, pull, fields, *refs):
    n, slab, depth, block_cells = shape
    outs, held = refs[:-1], refs[-1]
    members = n * slab
    held[...] = (steps[NB] + pull[0:1, :]).reshape(n, slab, members)
    block = lax.axis_index("grid")
    if len(outs) == 1:
        blend = held[...].reshape(members, members)
    else:
        blend = jnp.concatenate([held[lax.bitwise_xor(block, i)] for i in range(n)], axis=0)
    for level in range(depth):
        value = high_dot(blend, fields[:, level].reshape(members, block_cells)).reshape(n, slab, block_cells)
        if len(outs) == 1:
            outs[0][:, level] = value
        else:
            for out, part in zip(outs, PARTS):
                for i, distance in enumerate(part):
                    out[i, level] = value[distance]


def chain_kernel(shape, own, near, far, cross, steps, out):
    members, groups, count = shape
    width = groups * count
    group = lax.axis_index("lev")
    sources = [own, near, far, cross]
    bases = [NB * width, NB * width, (NB - 1) * width + 2 * count, (NB - 1) * width + 2 * count]
    columns = [source[base : base + SPARE, :].T for source, base in zip(sources, bases)]
    parents, alphas = [], []
    for source, base in zip(sources, bases):
        parents.append(source[base + PARENT : base + PARENT + 8, :].astype(jnp.int32))
        alphas.append(source[base + ALPHA : base + ALPHA + 6, :])
    tilts = {}
    pulled = []
    for b in range(NB):
        kinds = [(q, later) for q in range(groups) for later in range(b + 1, NB)] + [(0, None)]
        height = -(-len(kinds) // 8) * 8
        index = lax.broadcasted_iota(jnp.int32, (height, members), 0)
        logs = jnp.zeros((height, members), F32)
        for q in range(groups if b < NB - 1 else 1):
            start = pl.multiple_of(b * width + lax.bitwise_xor(group, q) * count, count)
            total = jnp.zeros((count, members), F32)
            tilted = jnp.zeros((count, members), F32)
            for p, source in enumerate(sources):
                if b == NB - 1 and p > 1:
                    value = source[b * width + (p - 2) * count : b * width + (p - 1) * count, :]
                else:
                    value = source[pl.ds(start, count), :]
                for e in range(b):
                    i = PAIRS.index((e, b))
                    tilted = tilted + value * tilts[e, p, b]
                    alpha = alphas[p][i : i + 1]
                    moved = lane_take(value, parents[p][i : i + 1])
                    value = alpha * moved + (1.0 - alpha) * value
                total = total + value
            if b > 0:
                total = total + jnp.sum(tilted, axis=1, keepdims=True)
            miss = columns[q][:count, VALUE + b : VALUE + b + 1] - total
            square = miss * miss
            for row, (owner_group, later) in enumerate(kinds):
                if owner_group != q:
                    continue
                at = OWN + b if later is None else LATER + PAIRS.index((b, later))
                log = jnp.sum(columns[q][:count, at : at + 1] * square, axis=0, keepdims=True)
                logs = jnp.where(index == row, log, logs)
        expo = jnp.exp(logs - jnp.max(logs, axis=1, keepdims=True))
        tilt = expo / jnp.sum(expo, axis=1, keepdims=True) - 1.0 / members
        for row, (q, later) in enumerate(kinds):
            if later is None:
                pulled.append(tilt[row : row + 1])
            else:
                tilts[b, q, later] = tilt[row : row + 1]
    pull = jnp.zeros((8, members), F32)
    for b in range(NB):
        pull = pull + high_dot(jnp.broadcast_to(pulled[b], (8, members)), steps[b])
    out[...] = pull


def final_kernel(shape, *refs):
    n, slab, depth, block_cells = shape
    pieces, out = refs[:-1], refs[-1]
    block = lax.axis_index("grid")
    for i in range(n):
        region = i if len(pieces) == 1 else lax.bitwise_xor(block, ORDER[i])
        cells = pl.ds(pl.multiple_of(region * block_cells, LANES), block_cells)
        for level in range(depth):
            out[:, level, cells] = pieces[0][i, level] if len(pieces) == 1 else pieces[i][0, level]


def hop(value, distance, n):
    return lax.ppermute(value, "grid", [(j, j ^ distance) for j in range(n)])


def gather_pieces(piece, n):
    if n != 8:
        return [lax.all_to_all(jnp.broadcast_to(piece[None], (n,) + piece.shape), "grid", 0, 0, tiled=True)]
    pieces = {0: piece}
    for i in (4, 2, 6, 7, 1):
        pieces[i] = hop(piece, i, n)
    for i in (4, 2):
        pieces[i + 1] = hop(pieces[i], 1, n)
    return [pieces[i] for i in range(n)]


def exchange_parts(parts, n):
    if len(parts) == 1:
        return [lax.all_to_all(parts[0], "grid", 0, 0, tiled=True)]
    pieces = {0: parts[0]}
    for part, distances in zip(parts[1:], PARTS[1:]):
        pieces[distances[0]] = hop(part, distances[0], n)
        if len(distances) == 2:
            pieces[distances[1]] = hop(pieces[distances[0]][1:], 1, n)
    return [pieces[i] for i in ORDER]


def body(prior, channel_weights, obs_owner, obs_offset, obs_value, obs_error, ancestors):
    n, lev = lax.axis_size("grid"), lax.axis_size("lev")
    slab, depth, cells = prior.shape
    members = slab * n
    block_cells = cells // n
    groups = channel_weights.shape[1]
    count = obs_offset.shape[2]
    width = NB * groups * count
    scale = n / 2.0
    shape = jax.ShapeDtypeStruct
    parents = ancestors[:, 0]
    tall = width // LANES * slab + 8

    piece = call(
        functools.partial(pick_kernel, (slab, depth, block_cells, groups, count)),
        shape((tall, LANES), F32),
        [PLACE] * 5,
        scratch=[
            pltpu.SMEM(obs_owner.shape, jnp.int32),
            pltpu.VMEM(channel_weights.shape, F32),
            pltpu.VMEM(obs_offset.shape, jnp.int32),
            pltpu.VMEM(parents.shape, jnp.int32),
            pltpu.VMEM(prior.shape, F32),
            pltpu.SemaphoreType.DMA((5,)),
        ],
        moved=10**6,
        limit=None,
    )(obs_owner, channel_weights, obs_offset, parents, prior)
    pieces = gather_pieces(piece, n)
    send = call(
        functools.partial(retile_kernel, (n, slab, depth, block_cells)),
        shape((n, depth, slab, block_cells), F32),
        [VMEM],
        moved=10**6,
    )(prior)
    fields = lax.all_to_all(send, "grid", 0, 0, tiled=True)

    rows, steps = call(
        functools.partial(prep_kernel, (block_cells, count, scale, members)),
        [shape((SPARE, LANES), F32), shape((NB + 1, members, members), F32)],
        [SMEM, VMEM, VMEM, VMEM, VMEM],
        moved=10**6,
    )(obs_owner, obs_offset, obs_value, obs_error, parents)

    slim_height = (NB - 1) * groups * count + 2 * count + SPARE
    own, slim = call(
        functools.partial(turn_kernel, (n, slab, width, count)),
        [shape((width + SPARE, members), F32), shape((slim_height, members), F32)],
        [SMEM, VMEM, PLACE] + [VMEM] * len(pieces),
        scratch=[pltpu.VMEM((n, tall, LANES), F32)],
        moved=10**6,
    )(obs_owner, rows, send, *pieces)
    far = lax.ppermute(slim, "lev", [(j, j ^ 2) for j in range(lev)])
    near = lax.ppermute(own, "lev", [(j, j ^ 1) for j in range(lev)])
    cross = lax.ppermute(far, "lev", [(j, j ^ 1) for j in range(lev)])

    pull = call(
        functools.partial(chain_kernel, (members, groups, count)),
        shape((8, members), F32),
        [VMEM] * 5,
        moved=10**5,
    )(own, near, far, cross, steps)

    if n == 8:
        layout = [shape((len(part), depth, slab, block_cells), F32) for part in PARTS]
    else:
        layout = [shape((n, depth, slab, block_cells), F32)]
    send = call(
        functools.partial(mix_kernel, (n, slab, depth, block_cells)),
        layout,
        [VMEM] * 3,
        scratch=[pltpu.VMEM((n, slab, members), F32)],
        flops=10**8,
        moved=10**6,
    )(steps, pull, fields)
    moved = exchange_parts(send, n)

    return call(
        functools.partial(final_kernel, (n, slab, depth, block_cells)),
        shape((slab, depth, cells), F32),
        [VMEM] * len(moved),
        moved=10**6,
    )(*moved)


def solution(mesh):
    in_specs = (
        P("grid", "lev", None),
        P("lev", None),
        P(),
        P(),
        P(None, "lev", None),
        P(None, "lev", None),
        P(None, "lev", "grid", None),
    )
    out_specs = P("grid", "lev", None)
    return jax.shard_map(body, mesh=mesh, in_specs=in_specs, out_specs=out_specs, check_vma=False)
```

```python
import functools

import jax
import jax.numpy as jnp
from jax import lax
from jax.experimental import pallas as pl
from jax.experimental.pallas import tpu as pltpu
from jax.sharding import PartitionSpec as P

NB = 4
HIGH = lax.Precision.HIGHEST
LANES = 128
F32 = jnp.float32
VMEM = pl.BlockSpec(memory_space=pltpu.VMEM)
SMEM = pl.BlockSpec(memory_space=pltpu.SMEM)
PLACE = pl.BlockSpec(memory_space=pl.ANY)
LIMIT = 48 * 1024 * 1024

PARTS = ((0,), (6, 7), (4,), (5,), (2, 3), (1,))
ORDER = (0, 6, 4, 5, 2, 1, 3, 7)
PAIRS = [(e, b) for b in range(1, NB) for e in range(b)]
PARENT, ALPHA, LATER, VALUE, OWN, SPARE = 0, 6, 12, 18, 22, 32


def call(kernel, out_shapes, in_specs, scratch=(), flops=0, moved=0, limit=LIMIT):
    many = isinstance(out_shapes, (list, tuple))
    return pl.pallas_call(
        kernel,
        out_shape=out_shapes,
        in_specs=in_specs,
        out_specs=[VMEM] * len(out_shapes) if many else VMEM,
        scratch_shapes=list(scratch),
        compiler_params=pltpu.CompilerParams(vmem_limit_bytes=limit),
        cost_estimate=pl.CostEstimate(flops=flops, bytes_accessed=moved, transcendentals=0),
    )


def high_dot(a, b):
    return lax.dot_general(a, b, (((1,), (0,)), ((), ())), precision=HIGH, preferred_element_type=F32)


def lane_take(value, row):
    where = jnp.broadcast_to(row, value.shape)
    return jnp.take_along_axis(value, where, axis=1, mode="promise_in_bounds")


def pick_kernel(shape, *refs):
    slab, depth, block_cells, groups, count = shape
    out, arrivals = refs[5], refs[11]
    copies = [pltpu.make_async_copy(refs[i], refs[6 + i], arrivals.at[i]) for i in range(5)]
    for copy in copies:
        copy.start()
    for copy in copies:
        copy.wait()
    owner, weights, offsets, ancestors, prior = refs[6:11]
    width = groups * count
    per = LANES // count
    blocks = width // LANES
    level_of = lax.broadcasted_iota(jnp.int32, (slab, depth, LANES), 1)
    gains = []
    for c in range(blocks):
        gain = jnp.zeros((slab, depth, LANES), F32)
        for level in range(depth):
            row = jnp.concatenate(
                [
                    jnp.broadcast_to(weights[level : level + 1, g : g + 1], (1, count))
                    for g in range(c * per, (c + 1) * per)
                ],
                axis=1,
            )
            gain = jnp.where(level_of == level, row[None], gain)
        gains.append(gain.reshape(slab * depth, LANES))
    for b in range(NB):
        start = pl.multiple_of(owner[b] * block_cells, LANES)
        both = prior[:, :, pl.ds(start, block_cells)].reshape(slab * depth, block_cells)
        for c in range(blocks):
            cell = jnp.concatenate([offsets[b, g : g + 1, :] for g in range(c * per, (c + 1) * per)], axis=1)
            low, high = lax.rem(cell, LANES), lax.div(cell, LANES)
            found = jnp.zeros((slab * depth, LANES), F32)
            for h in range(block_cells // LANES):
                part = lane_take(both[:, h * LANES : (h + 1) * LANES], low)
                found = jnp.where(high == h, part, found)
            line = (b * blocks + c) * slab
            out[line : line + slab, :] = jnp.sum((found * gains[c]).reshape(slab, depth, LANES), axis=1)
    line = NB * width // LANES * slab
    out[line:, :] = jnp.zeros((out.shape[0] - line, LANES), F32)
    for b in range(NB):
        out[line + b : line + b + 1, :] = ancestors[b].astype(F32)


def retile_kernel(shape, prior, out):
    n, slab, depth, block_cells = shape
    for i in range(n):
        for level in range(depth):
            out[i, level] = prior[:, level, i * block_cells : (i + 1) * block_cells]


def prep_kernel(shape, owner, offsets, values, errors, ancestors, rows, steps):
    block_cells, count, scale, members = shape
    block, group = lax.axis_index("grid"), lax.axis_index("lev")
    index = lax.broadcasted_iota(jnp.int32, (8, 1), 0)
    region = jnp.full((8, 1), block, jnp.int32)
    for b in range(1, NB):
        region = jnp.where(index == b - 1, owner[b], region)
    centre = region.astype(F32) + 0.5
    rows[...] = jnp.zeros((SPARE, LANES), F32)
    row = lax.broadcasted_iota(jnp.int32, (members, members), 0)
    column = lax.broadcasted_iota(jnp.int32, (members, members), 1)
    turned = (row == column).astype(F32)
    for b in range(NB):
        cells = owner[b] * block_cells + offsets[b, pl.ds(group, 1), :]
        distance = (centre - cells.astype(F32) / block_cells) / scale
        taper = jnp.exp(-0.5 * distance * distance)
        alpha = 0.8 * (1.0 - jnp.exp(-jnp.sum(taper, axis=1, keepdims=True) / count))
        error = errors[b]
        part = (-0.5 / count) * (taper / (error * error))
        for later in range(b + 1, NB):
            i = PAIRS.index((b, later))
            rows[ALPHA + i : ALPHA + i + 1, :] = jnp.broadcast_to(alpha[later - 1 : later], (1, LANES))
            rows[LATER + i : LATER + i + 1, :count] = part[later - 1 : later]
        rows[VALUE + b : VALUE + b + 1, :count] = values[b]
        rows[OWN + b : OWN + b + 1, :count] = part[NB - 1 : NB]
        steps[b] = turned.T
        own = alpha[NB - 1 : NB]
        turned = own * lane_take(turned, ancestors[b]) + (1.0 - own) * turned
    steps[NB] = turned.T


def turn_kernel(shape, owner, rows, ahead, *refs):
    n, slab, width, count = shape
    pieces, out, slim, held = refs[:-3], refs[-3], refs[-2], refs[-1]
    members = n * slab
    block, group = lax.axis_index("grid"), lax.axis_index("lev")
    if len(pieces) == 1:
        held[...] = pieces[0][...]
    else:
        for i, piece in enumerate(pieces):
            held[lax.bitwise_xor(block, i)] = piece[...]
    common = width // NB * (NB - 1)
    for i in range(width // LANES):
        value = held[:, i * slab : (i + 1) * slab, :].reshape(members, LANES).T
        out[i * LANES : (i + 1) * LANES, :] = value
        if (i + 1) * LANES <= common:
            slim[i * LANES : (i + 1) * LANES, :] = value
    for i in range(2):
        start = pl.multiple_of(common + lax.bitwise_xor(group, 2 + i) * count, count)
        slim[common + i * count : common + (i + 1) * count, :] = out[pl.ds(start, count), :]
    low = common + 2 * count
    out[width:, :] = rows[...]
    slim[low:, :] = rows[...]
    line = width // LANES * slab
    for i, (e, b) in enumerate(PAIRS):
        value = held[owner[b], line + e : line + e + 1, :]
        out[width + PARENT + i : width + PARENT + i + 1, :] = value
        slim[low + PARENT + i : low + PARENT + i + 1, :] = value


def mix_kernel(shape, steps, pull, fields, *refs):
    n, slab, depth, block_cells = shape
    outs, held = refs[:-1], refs[-1]
    members = n * slab
    held[...] = (steps[NB] + pull[0:1, :]).reshape(n, slab, members)
    block = lax.axis_index("grid")
    if len(outs) == 1:
        blend = held[...].reshape(members, members)
    else:
        blend = jnp.concatenate([held[lax.bitwise_xor(block, i)] for i in range(n)], axis=0)
    for level in range(depth):
        value = high_dot(blend, fields[:, level].reshape(members, block_cells)).reshape(n, slab, block_cells)
        if len(outs) == 1:
            outs[0][:, level] = value
        else:
            for out, part in zip(outs, PARTS):
                for i, distance in enumerate(part):
                    out[i, level] = value[distance]


def chain_kernel(shape, own, near, far, cross, steps, out):
    members, groups, count = shape
    width = groups * count
    group = lax.axis_index("lev")
    sources = [own, near, far, cross]
    bases = [NB * width, NB * width, (NB - 1) * width + 2 * count, (NB - 1) * width + 2 * count]
    columns = [source[base : base + SPARE, :].T for source, base in zip(sources, bases)]
    parents, alphas = [], []
    for source, base in zip(sources, bases):
        parents.append(source[base + PARENT : base + PARENT + 8, :].astype(jnp.int32))
        alphas.append(source[base + ALPHA : base + ALPHA + 6, :])
    tilts = {}
    pulled = []
    for b in range(NB):
        kinds = [(q, later) for q in range(groups) for later in range(b + 1, NB)] + [(0, None)]
        height = -(-len(kinds) // 8) * 8
        index = lax.broadcasted_iota(jnp.int32, (height, members), 0)
        logs = jnp.zeros((height, members), F32)
        for q in range(groups if b < NB - 1 else 1):
            start = pl.multiple_of(b * width + lax.bitwise_xor(group, q) * count, count)
            total = jnp.zeros((count, members), F32)
            tilted = jnp.zeros((count, members), F32)
            for p, source in enumerate(sources):
                if b == NB - 1 and p > 1:
                    value = source[b * width + (p - 2) * count : b * width + (p - 1) * count, :]
                else:
                    value = source[pl.ds(start, count), :]
                for e in range(b):
                    i = PAIRS.index((e, b))
                    tilted = tilted + value * tilts[e, p, b]
                    alpha = alphas[p][i : i + 1]
                    moved = lane_take(value, parents[p][i : i + 1])
                    value = alpha * moved + (1.0 - alpha) * value
                total = total + value
            if b > 0:
                total = total + jnp.sum(tilted, axis=1, keepdims=True)
            miss = columns[q][:count, VALUE + b : VALUE + b + 1] - total
            square = miss * miss
            for row, (owner_group, later) in enumerate(kinds):
                if owner_group != q:
                    continue
                at = OWN + b if later is None else LATER + PAIRS.index((b, later))
                log = jnp.sum(columns[q][:count, at : at + 1] * square, axis=0, keepdims=True)
                logs = jnp.where(index == row, log, logs)
        expo = jnp.exp(logs - jnp.max(logs, axis=1, keepdims=True))
        tilt = expo / jnp.sum(expo, axis=1, keepdims=True) - 1.0 / members
        for row, (q, later) in enumerate(kinds):
            if later is None:
                pulled.append(tilt[row : row + 1])
            else:
                tilts[b, q, later] = tilt[row : row + 1]
    pull = jnp.zeros((8, members), F32)
    for b in range(NB):
        pull = pull + high_dot(jnp.broadcast_to(pulled[b], (8, members)), steps[b])
    out[...] = pull


def final_kernel(shape, *refs):
    n, slab, depth, block_cells = shape
    pieces, out = refs[:-1], refs[-1]
    block = lax.axis_index("grid")
    for i in range(n):
        region = i if len(pieces) == 1 else lax.bitwise_xor(block, ORDER[i])
        cells = pl.ds(pl.multiple_of(region * block_cells, LANES), block_cells)
        piece, at = (pieces[0], i) if len(pieces) == 1 else (pieces[i], 0)
        out[:, :, cells] = jnp.stack([piece[at, level] for level in range(depth)], axis=1)


def hop(value, distance, n):
    return lax.ppermute(value, "grid", [(j, j ^ distance) for j in range(n)])


def gather_pieces(piece, n):
    if n != 8:
        return [lax.all_to_all(jnp.broadcast_to(piece[None], (n,) + piece.shape), "grid", 0, 0, tiled=True)]
    pieces = {0: piece}
    for i in (4, 2, 6, 7, 1):
        pieces[i] = hop(piece, i, n)
    for i in (4, 2):
        pieces[i + 1] = hop(pieces[i], 1, n)
    return [pieces[i] for i in range(n)]


def exchange_parts(parts, n):
    if len(parts) == 1:
        return [lax.all_to_all(parts[0], "grid", 0, 0, tiled=True)]
    pieces = {0: parts[0]}
    for part, distances in zip(parts[1:], PARTS[1:]):
        pieces[distances[0]] = hop(part, distances[0], n)
        if len(distances) == 2:
            pieces[distances[1]] = hop(pieces[distances[0]][1:], 1, n)
    return [pieces[i] for i in ORDER]


def body(prior, channel_weights, obs_owner, obs_offset, obs_value, obs_error, ancestors):
    n, lev = lax.axis_size("grid"), lax.axis_size("lev")
    slab, depth, cells = prior.shape
    members = slab * n
    block_cells = cells // n
    groups = channel_weights.shape[1]
    count = obs_offset.shape[2]
    width = NB * groups * count
    scale = n / 2.0
    shape = jax.ShapeDtypeStruct
    parents = ancestors[:, 0]
    tall = width // LANES * slab + 8

    piece = call(
        functools.partial(pick_kernel, (slab, depth, block_cells, groups, count)),
        shape((tall, LANES), F32),
        [PLACE] * 5,
        scratch=[
            pltpu.SMEM(obs_owner.shape, jnp.int32),
            pltpu.VMEM(channel_weights.shape, F32),
            pltpu.VMEM(obs_offset.shape, jnp.int32),
            pltpu.VMEM(parents.shape, jnp.int32),
            pltpu.VMEM(prior.shape, F32),
            pltpu.SemaphoreType.DMA((5,)),
        ],
        moved=10**6,
        limit=None,
    )(obs_owner, channel_weights, obs_offset, parents, prior)
    pieces = gather_pieces(piece, n)
    send = call(
        functools.partial(retile_kernel, (n, slab, depth, block_cells)),
        shape((n, depth, slab, block_cells), F32),
        [VMEM],
        moved=10**6,
    )(prior)
    fields = lax.all_to_all(send, "grid", 0, 0, tiled=True)

    rows, steps = call(
        functools.partial(prep_kernel, (block_cells, count, scale, members)),
        [shape((SPARE, LANES), F32), shape((NB + 1, members, members), F32)],
        [SMEM, VMEM, VMEM, VMEM, VMEM],
        moved=10**6,
    )(obs_owner, obs_offset, obs_value, obs_error, parents)

    slim_height = (NB - 1) * groups * count + 2 * count + SPARE
    own, slim = call(
        functools.partial(turn_kernel, (n, slab, width, count)),
        [shape((width + SPARE, members), F32), shape((slim_height, members), F32)],
        [SMEM, VMEM, PLACE] + [VMEM] * len(pieces),
        scratch=[pltpu.VMEM((n, tall, LANES), F32)],
        moved=10**6,
    )(obs_owner, rows, send, *pieces)
    far = lax.ppermute(slim, "lev", [(j, j ^ 2) for j in range(lev)])
    near = lax.ppermute(own, "lev", [(j, j ^ 1) for j in range(lev)])
    cross = lax.ppermute(far, "lev", [(j, j ^ 1) for j in range(lev)])

    pull = call(
        functools.partial(chain_kernel, (members, groups, count)),
        shape((8, members), F32),
        [VMEM] * 5,
        moved=10**5,
    )(own, near, far, cross, steps)

    if n == 8:
        layout = [shape((len(part), depth, slab, block_cells), F32) for part in PARTS]
    else:
        layout = [shape((n, depth, slab, block_cells), F32)]
    send = call(
        functools.partial(mix_kernel, (n, slab, depth, block_cells)),
        layout,
        [VMEM] * 3,
        scratch=[pltpu.VMEM((n, slab, members), F32)],
        flops=10**8,
        moved=10**6,
    )(steps, pull, fields)
    moved = exchange_parts(send, n)

    return call(
        functools.partial(final_kernel, (n, slab, depth, block_cells)),
        shape((slab, depth, cells), F32),
        [VMEM] * len(moved),
        moved=10**6,
    )(*moved)


def solution(mesh):
    in_specs = (
        P("grid", "lev", None),
        P("lev", None),
        P(),
        P(),
        P(None, "lev", None),
        P(None, "lev", None),
        P(None, "lev", "grid", None),
    )
    out_specs = P("grid", "lev", None)
    return jax.shard_map(body, mesh=mesh, in_specs=in_specs, out_specs=out_specs, check_vma=False)
```

```python
import functools

import jax
import jax.numpy as jnp
from jax import lax
from jax.experimental import pallas as pl
from jax.experimental.pallas import tpu as pltpu
from jax.sharding import PartitionSpec as P

NB = 4
HIGH = lax.Precision.HIGHEST
LANES = 128
F32 = jnp.float32
VMEM = pl.BlockSpec(memory_space=pltpu.VMEM)
SMEM = pl.BlockSpec(memory_space=pltpu.SMEM)
PLACE = pl.BlockSpec(memory_space=pl.ANY)
LIMIT = 48 * 1024 * 1024

PARTS = ((0,), (6,), (7,), (4,), (5,), (2, 3), (1,))
ORDER = (0, 6, 7, 4, 5, 2, 1, 3)
PAIRS = [(e, b) for b in range(1, NB) for e in range(b)]
PARENT, ALPHA, LATER, VALUE, OWN, SPARE = 0, 6, 12, 18, 22, 32


def call(kernel, out_shapes, in_specs, scratch=(), flops=0, moved=0, limit=LIMIT):
    many = isinstance(out_shapes, (list, tuple))
    return pl.pallas_call(
        kernel,
        out_shape=out_shapes,
        in_specs=in_specs,
        out_specs=[VMEM] * len(out_shapes) if many else VMEM,
        scratch_shapes=list(scratch),
        compiler_params=pltpu.CompilerParams(vmem_limit_bytes=limit),
        cost_estimate=pl.CostEstimate(flops=flops, bytes_accessed=moved, transcendentals=0),
    )


def high_dot(a, b):
    return lax.dot_general(a, b, (((1,), (0,)), ((), ())), precision=HIGH, preferred_element_type=F32)


def lane_take(value, row):
    where = jnp.broadcast_to(row, value.shape)
    return jnp.take_along_axis(value, where, axis=1, mode="promise_in_bounds")


def pick_kernel(shape, *refs):
    slab, depth, block_cells, groups, count = shape
    out, arrivals = refs[5], refs[11]
    copies = [pltpu.make_async_copy(refs[i], refs[6 + i], arrivals.at[i]) for i in range(4)]
    parts = 4 if slab % 4 == 0 else 1
    for i in range(parts):
        some = pl.ds(i * (slab // parts), slab // parts)
        copies.append(pltpu.make_async_copy(refs[4].at[some], refs[10].at[some], arrivals.at[4 + i]))
    for copy in copies:
        copy.start()
    for copy in copies:
        copy.wait()
    owner, weights, offsets, ancestors, prior = refs[6:11]
    width = groups * count
    per = LANES // count
    blocks = width // LANES
    level_of = lax.broadcasted_iota(jnp.int32, (slab, depth, LANES), 1)
    gains = []
    for c in range(blocks):
        gain = jnp.zeros((slab, depth, LANES), F32)
        for level in range(depth):
            row = jnp.concatenate(
                [
                    jnp.broadcast_to(weights[level : level + 1, g : g + 1], (1, count))
                    for g in range(c * per, (c + 1) * per)
                ],
                axis=1,
            )
            gain = jnp.where(level_of == level, row[None], gain)
        gains.append(gain.reshape(slab * depth, LANES))
    for b in range(NB):
        start = pl.multiple_of(owner[b] * block_cells, LANES)
        both = prior[:, :, pl.ds(start, block_cells)].reshape(slab * depth, block_cells)
        for c in range(blocks):
            cell = jnp.concatenate([offsets[b, g : g + 1, :] for g in range(c * per, (c + 1) * per)], axis=1)
            low, high = lax.rem(cell, LANES), lax.div(cell, LANES)
            found = jnp.zeros((slab * depth, LANES), F32)
            for h in range(block_cells // LANES):
                part = lane_take(both[:, h * LANES : (h + 1) * LANES], low)
                found = jnp.where(high == h, part, found)
            line = (b * blocks + c) * slab
            out[line : line + slab, :] = jnp.sum((found * gains[c]).reshape(slab, depth, LANES), axis=1)
    line = NB * width // LANES * slab
    out[line:, :] = jnp.zeros((out.shape[0] - line, LANES), F32)
    for b in range(NB):
        out[line + b : line + b + 1, :] = ancestors[b].astype(F32)


def retile_kernel(shape, prior, out):
    n, slab, depth, block_cells = shape
    for i in range(n):
        for level in range(depth):
            out[i, level] = prior[:, level, i * block_cells : (i + 1) * block_cells]


def prep_kernel(shape, owner, offsets, values, errors, ancestors, rows, steps):
    block_cells, count, scale, members = shape
    block, group = lax.axis_index("grid"), lax.axis_index("lev")
    index = lax.broadcasted_iota(jnp.int32, (8, 1), 0)
    region = jnp.full((8, 1), block, jnp.int32)
    for b in range(1, NB):
        region = jnp.where(index == b - 1, owner[b], region)
    centre = region.astype(F32) + 0.5
    rows[...] = jnp.zeros((SPARE, LANES), F32)
    row = lax.broadcasted_iota(jnp.int32, (members, members), 0)
    column = lax.broadcasted_iota(jnp.int32, (members, members), 1)
    turned = (row == column).astype(F32)
    for b in range(NB):
        cells = owner[b] * block_cells + offsets[b, pl.ds(group, 1), :]
        distance = (centre - cells.astype(F32) / block_cells) / scale
        taper = jnp.exp(-0.5 * distance * distance)
        alpha = 0.8 * (1.0 - jnp.exp(-jnp.sum(taper, axis=1, keepdims=True) / count))
        error = errors[b]
        part = (-0.5 / count) * (taper / (error * error))
        for later in range(b + 1, NB):
            i = PAIRS.index((b, later))
            rows[ALPHA + i : ALPHA + i + 1, :] = jnp.broadcast_to(alpha[later - 1 : later], (1, LANES))
            rows[LATER + i : LATER + i + 1, :count] = part[later - 1 : later]
        rows[VALUE + b : VALUE + b + 1, :count] = values[b]
        rows[OWN + b : OWN + b + 1, :count] = part[NB - 1 : NB]
        steps[b] = turned.T
        own = alpha[NB - 1 : NB]
        turned = own * lane_take(turned, ancestors[b]) + (1.0 - own) * turned
    steps[NB] = turned.T


def turn_kernel(shape, owner, rows, ahead, *refs):
    n, slab, width, count = shape
    pieces, out, slim, held = refs[:-3], refs[-3], refs[-2], refs[-1]
    members = n * slab
    block, group = lax.axis_index("grid"), lax.axis_index("lev")
    if len(pieces) == 1:
        held[...] = pieces[0][...]
    else:
        for i, piece in enumerate(pieces):
            held[lax.bitwise_xor(block, i)] = piece[...]
    common = width // NB * (NB - 1)
    for i in range(width // LANES):
        value = held[:, i * slab : (i + 1) * slab, :].reshape(members, LANES).T
        out[i * LANES : (i + 1) * LANES, :] = value
        if (i + 1) * LANES <= common:
            slim[i * LANES : (i + 1) * LANES, :] = value
    for i in range(2):
        start = pl.multiple_of(common + lax.bitwise_xor(group, 2 + i) * count, count)
        slim[common + i * count : common + (i + 1) * count, :] = out[pl.ds(start, count), :]
    low = common + 2 * count
    out[width:, :] = rows[...]
    slim[low:, :] = rows[...]
    line = width // LANES * slab
    for i, (e, b) in enumerate(PAIRS):
        value = held[owner[b], line + e : line + e + 1, :]
        out[width + PARENT + i : width + PARENT + i + 1, :] = value
        slim[low + PARENT + i : low + PARENT + i + 1, :] = value


def mix_kernel(shape, steps, pull, fields, *refs):
    n, slab, depth, block_cells = shape
    outs, held = refs[:-1], refs[-1]
    members = n * slab
    held[...] = (steps[NB] + pull[0:1, :]).reshape(n, slab, members)
    block = lax.axis_index("grid")
    if len(outs) == 1:
        blend = held[...].reshape(members, members)
    else:
        blend = jnp.concatenate([held[lax.bitwise_xor(block, i)] for i in range(n)], axis=0)
    for level in range(depth):
        value = high_dot(blend, fields[:, level].reshape(members, block_cells)).reshape(n, slab, block_cells)
        if len(outs) == 1:
            outs[0][:, level] = value
        else:
            for out, part in zip(outs, PARTS):
                for i, distance in enumerate(part):
                    out[i, level] = value[distance]


def chain_kernel(shape, own, near, far, cross, steps, out):
    members, groups, count = shape
    width = groups * count
    group = lax.axis_index("lev")
    sources = [own, near, far, cross]
    bases = [NB * width, NB * width, (NB - 1) * width + 2 * count, (NB - 1) * width + 2 * count]
    columns = [source[base : base + SPARE, :].T for source, base in zip(sources, bases)]
    parents, alphas = [], []
    for source, base in zip(sources, bases):
        parents.append(source[base + PARENT : base + PARENT + 8, :].astype(jnp.int32))
        alphas.append(source[base + ALPHA : base + ALPHA + 6, :])
    tilts = {}
    pulled = []
    for b in range(NB):
        kinds = [(q, later) for q in range(groups) for later in range(b + 1, NB)] + [(0, None)]
        height = -(-len(kinds) // 8) * 8
        index = lax.broadcasted_iota(jnp.int32, (height, members), 0)
        logs = jnp.zeros((height, members), F32)
        for q in range(groups if b < NB - 1 else 1):
            start = pl.multiple_of(b * width + lax.bitwise_xor(group, q) * count, count)
            total = jnp.zeros((count, members), F32)
            tilted = jnp.zeros((count, members), F32)
            for p, source in enumerate(sources):
                if b == NB - 1 and p > 1:
                    value = source[b * width + (p - 2) * count : b * width + (p - 1) * count, :]
                else:
                    value = source[pl.ds(start, count), :]
                for e in range(b):
                    i = PAIRS.index((e, b))
                    tilted = tilted + value * tilts[e, p, b]
                    alpha = alphas[p][i : i + 1]
                    moved = lane_take(value, parents[p][i : i + 1])
                    value = alpha * moved + (1.0 - alpha) * value
                total = total + value
            if b > 0:
                total = total + jnp.sum(tilted, axis=1, keepdims=True)
            miss = columns[q][:count, VALUE + b : VALUE + b + 1] - total
            square = miss * miss
            for row, (owner_group, later) in enumerate(kinds):
                if owner_group != q:
                    continue
                at = OWN + b if later is None else LATER + PAIRS.index((b, later))
                log = jnp.sum(columns[q][:count, at : at + 1] * square, axis=0, keepdims=True)
                logs = jnp.where(index == row, log, logs)
        expo = jnp.exp(logs - jnp.max(logs, axis=1, keepdims=True))
        tilt = expo / jnp.sum(expo, axis=1, keepdims=True) - 1.0 / members
        for row, (q, later) in enumerate(kinds):
            if later is None:
                pulled.append(tilt[row : row + 1])
            else:
                tilts[b, q, later] = tilt[row : row + 1]
    pull = jnp.zeros((8, members), F32)
    for b in range(NB):
        pull = pull + high_dot(jnp.broadcast_to(pulled[b], (8, members)), steps[b])
    out[...] = pull


def final_kernel(shape, *refs):
    n, slab, depth, block_cells = shape
    pieces, out = refs[:-1], refs[-1]
    block = lax.axis_index("grid")
    for i in range(n):
        region = i if len(pieces) == 1 else lax.bitwise_xor(block, ORDER[i])
        cells = pl.ds(pl.multiple_of(region * block_cells, LANES), block_cells)
        for level in range(depth):
            out[:, level, cells] = pieces[0][i, level] if len(pieces) == 1 else pieces[i][0, level]


def hop(value, distance, n):
    return lax.ppermute(value, "grid", [(j, j ^ distance) for j in range(n)])


def gather_pieces(piece, n):
    if n != 8:
        return [lax.all_to_all(jnp.broadcast_to(piece[None], (n,) + piece.shape), "grid", 0, 0, tiled=True)]
    pieces = {0: piece}
    for i in (4, 2, 6, 7, 1):
        pieces[i] = hop(piece, i, n)
    for i in (4, 2):
        pieces[i + 1] = hop(pieces[i], 1, n)
    return [pieces[i] for i in range(n)]


def exchange_parts(parts, n):
    if len(parts) == 1:
        return [lax.all_to_all(parts[0], "grid", 0, 0, tiled=True)]
    pieces = {0: parts[0]}
    for part, distances in zip(parts[1:], PARTS[1:]):
        pieces[distances[0]] = hop(part, distances[0], n)
        if len(distances) == 2:
            pieces[distances[1]] = hop(pieces[distances[0]][1:], 1, n)
    return [pieces[i] for i in ORDER]


def body(prior, channel_weights, obs_owner, obs_offset, obs_value, obs_error, ancestors):
    n, lev = lax.axis_size("grid"), lax.axis_size("lev")
    slab, depth, cells = prior.shape
    members = slab * n
    block_cells = cells // n
    groups = channel_weights.shape[1]
    count = obs_offset.shape[2]
    width = NB * groups * count
    scale = n / 2.0
    shape = jax.ShapeDtypeStruct
    parents = ancestors[:, 0]
    tall = width // LANES * slab + 8

    piece = call(
        functools.partial(pick_kernel, (slab, depth, block_cells, groups, count)),
        shape((tall, LANES), F32),
        [PLACE] * 5,
        scratch=[
            pltpu.SMEM(obs_owner.shape, jnp.int32),
            pltpu.VMEM(channel_weights.shape, F32),
            pltpu.VMEM(obs_offset.shape, jnp.int32),
            pltpu.VMEM(parents.shape, jnp.int32),
            pltpu.VMEM(prior.shape, F32),
            pltpu.SemaphoreType.DMA((8,)),
        ],
        moved=10**6,
        limit=None,
    )(obs_owner, channel_weights, obs_offset, parents, prior)
    pieces = gather_pieces(piece, n)
    send = call(
        functools.partial(retile_kernel, (n, slab, depth, block_cells)),
        shape((n, depth, slab, block_cells), F32),
        [VMEM],
        moved=10**6,
    )(prior)
    fields = lax.all_to_all(send, "grid", 0, 0, tiled=True)

    rows, steps = call(
        functools.partial(prep_kernel, (block_cells, count, scale, members)),
        [shape((SPARE, LANES), F32), shape((NB + 1, members, members), F32)],
        [SMEM, VMEM, VMEM, VMEM, VMEM],
        moved=10**6,
    )(obs_owner, obs_offset, obs_value, obs_error, parents)

    slim_height = (NB - 1) * groups * count + 2 * count + SPARE
    own, slim = call(
        functools.partial(turn_kernel, (n, slab, width, count)),
        [shape((width + SPARE, members), F32), shape((slim_height, members), F32)],
        [SMEM, VMEM, PLACE] + [VMEM] * len(pieces),
        scratch=[pltpu.VMEM((n, tall, LANES), F32)],
        moved=10**6,
    )(obs_owner, rows, send, *pieces)
    far = lax.ppermute(slim, "lev", [(j, j ^ 2) for j in range(lev)])
    near = lax.ppermute(own, "lev", [(j, j ^ 1) for j in range(lev)])
    cross = lax.ppermute(far, "lev", [(j, j ^ 1) for j in range(lev)])

    pull = call(
        functools.partial(chain_kernel, (members, groups, count)),
        shape((8, members), F32),
        [VMEM] * 5,
        moved=10**5,
    )(own, near, far, cross, steps)

    if n == 8:
        layout = [shape((len(part), depth, slab, block_cells), F32) for part in PARTS]
    else:
        layout = [shape((n, depth, slab, block_cells), F32)]
    send = call(
        functools.partial(mix_kernel, (n, slab, depth, block_cells)),
        layout,
        [VMEM] * 3,
        scratch=[pltpu.VMEM((n, slab, members), F32)],
        flops=10**8,
        moved=10**6,
    )(steps, pull, fields)
    moved = exchange_parts(send, n)

    return call(
        functools.partial(final_kernel, (n, slab, depth, block_cells)),
        shape((slab, depth, cells), F32),
        [VMEM] * len(moved),
        moved=10**6,
    )(*moved)


def solution(mesh):
    in_specs = (
        P("grid", "lev", None),
        P("lev", None),
        P(),
        P(),
        P(None, "lev", None),
        P(None, "lev", None),
        P(None, "lev", "grid", None),
    )
    out_specs = P("grid", "lev", None)
    return jax.shard_map(body, mesh=mesh, in_specs=in_specs, out_specs=out_specs, check_vma=False)
```

```python
import functools

import jax
import jax.numpy as jnp
from jax import lax
from jax.experimental import pallas as pl
from jax.experimental.pallas import tpu as pltpu
from jax.sharding import PartitionSpec as P

NB = 4
HIGH = lax.Precision.HIGHEST
LANES = 128
F32 = jnp.float32
VMEM = pl.BlockSpec(memory_space=pltpu.VMEM)
SMEM = pl.BlockSpec(memory_space=pltpu.SMEM)
PLACE = pl.BlockSpec(memory_space=pl.ANY)
LIMIT = 48 * 1024 * 1024

PARTS = ((0,), (4,), (5,), (6,), (7,), (2, 3), (1,))
ORDER = (0, 4, 5, 6, 7, 2, 1, 3)
PAIRS = [(e, b) for b in range(1, NB) for e in range(b)]
PARENT, ALPHA, LATER, VALUE, OWN, SPARE = 0, 6, 12, 18, 22, 32


def call(kernel, out_shapes, in_specs, scratch=(), flops=0, moved=0, limit=LIMIT):
    many = isinstance(out_shapes, (list, tuple))
    return pl.pallas_call(
        kernel,
        out_shape=out_shapes,
        in_specs=in_specs,
        out_specs=[VMEM] * len(out_shapes) if many else VMEM,
        scratch_shapes=list(scratch),
        compiler_params=pltpu.CompilerParams(vmem_limit_bytes=limit),
        cost_estimate=pl.CostEstimate(flops=flops, bytes_accessed=moved, transcendentals=0),
    )


def high_dot(a, b):
    return lax.dot_general(a, b, (((1,), (0,)), ((), ())), precision=HIGH, preferred_element_type=F32)


def lane_take(value, row):
    where = jnp.broadcast_to(row, value.shape)
    return jnp.take_along_axis(value, where, axis=1, mode="promise_in_bounds")


def pick_kernel(shape, *refs):
    slab, depth, block_cells, groups, count = shape
    out, arrivals = refs[5], refs[11]
    copies = [pltpu.make_async_copy(refs[i], refs[6 + i], arrivals.at[i]) for i in range(5)]
    for copy in copies:
        copy.start()
    for copy in copies:
        copy.wait()
    owner, weights, offsets, ancestors, prior = refs[6:11]
    width = groups * count
    per = LANES // count
    blocks = width // LANES
    level_of = lax.broadcasted_iota(jnp.int32, (slab, depth, LANES), 1)
    gains = []
    for c in range(blocks):
        gain = jnp.zeros((slab, depth, LANES), F32)
        for level in range(depth):
            row = jnp.concatenate(
                [
                    jnp.broadcast_to(weights[level : level + 1, g : g + 1], (1, count))
                    for g in range(c * per, (c + 1) * per)
                ],
                axis=1,
            )
            gain = jnp.where(level_of == level, row[None], gain)
        gains.append(gain.reshape(slab * depth, LANES))
    for b in range(NB):
        start = pl.multiple_of(owner[b] * block_cells, LANES)
        both = prior[:, :, pl.ds(start, block_cells)].reshape(slab * depth, block_cells)
        for c in range(blocks):
            cell = jnp.concatenate([offsets[b, g : g + 1, :] for g in range(c * per, (c + 1) * per)], axis=1)
            low, high = lax.rem(cell, LANES), lax.div(cell, LANES)
            found = jnp.zeros((slab * depth, LANES), F32)
            for h in range(block_cells // LANES):
                part = lane_take(both[:, h * LANES : (h + 1) * LANES], low)
                found = jnp.where(high == h, part, found)
            line = (b * blocks + c) * slab
            out[line : line + slab, :] = jnp.sum((found * gains[c]).reshape(slab, depth, LANES), axis=1)
    line = NB * width // LANES * slab
    out[line:, :] = jnp.zeros((out.shape[0] - line, LANES), F32)
    for b in range(NB):
        out[line + b : line + b + 1, :] = ancestors[b].astype(F32)


def retile_kernel(shape, prior, out):
    n, slab, depth, block_cells = shape
    for i in range(n):
        for level in range(depth):
            out[i, level] = prior[:, level, i * block_cells : (i + 1) * block_cells]


def prep_kernel(shape, owner, offsets, values, errors, ancestors, rows, steps):
    block_cells, count, scale, members = shape
    block, group = lax.axis_index("grid"), lax.axis_index("lev")
    index = lax.broadcasted_iota(jnp.int32, (8, 1), 0)
    region = jnp.full((8, 1), block, jnp.int32)
    for b in range(1, NB):
        region = jnp.where(index == b - 1, owner[b], region)
    centre = region.astype(F32) + 0.5
    rows[...] = jnp.zeros((SPARE, LANES), F32)
    row = lax.broadcasted_iota(jnp.int32, (members, members), 0)
    column = lax.broadcasted_iota(jnp.int32, (members, members), 1)
    turned = (row == column).astype(F32)
    for b in range(NB):
        cells = owner[b] * block_cells + offsets[b, pl.ds(group, 1), :]
        distance = (centre - cells.astype(F32) / block_cells) / scale
        taper = jnp.exp(-0.5 * distance * distance)
        alpha = 0.8 * (1.0 - jnp.exp(-jnp.sum(taper, axis=1, keepdims=True) / count))
        error = errors[b]
        part = (-0.5 / count) * (taper / (error * error))
        for later in range(b + 1, NB):
            i = PAIRS.index((b, later))
            rows[ALPHA + i : ALPHA + i + 1, :] = jnp.broadcast_to(alpha[later - 1 : later], (1, LANES))
            rows[LATER + i : LATER + i + 1, :count] = part[later - 1 : later]
        rows[VALUE + b : VALUE + b + 1, :count] = values[b]
        rows[OWN + b : OWN + b + 1, :count] = part[NB - 1 : NB]
        steps[b] = turned.T
        own = alpha[NB - 1 : NB]
        turned = own * lane_take(turned, ancestors[b]) + (1.0 - own) * turned
    steps[NB] = turned.T


def turn_kernel(shape, owner, rows, ahead, *refs):
    n, slab, width, count = shape
    pieces, out, slim, held = refs[:-3], refs[-3], refs[-2], refs[-1]
    members = n * slab
    block, group = lax.axis_index("grid"), lax.axis_index("lev")
    if len(pieces) == 1:
        held[...] = pieces[0][...]
    else:
        for i, piece in enumerate(pieces):
            held[lax.bitwise_xor(block, i)] = piece[...]
    common = width // NB * (NB - 1)
    for i in range(width // LANES):
        value = held[:, i * slab : (i + 1) * slab, :].reshape(members, LANES).T
        out[i * LANES : (i + 1) * LANES, :] = value
        if (i + 1) * LANES <= common:
            slim[i * LANES : (i + 1) * LANES, :] = value
    for i in range(2):
        start = pl.multiple_of(common + lax.bitwise_xor(group, 2 + i) * count, count)
        slim[common + i * count : common + (i + 1) * count, :] = out[pl.ds(start, count), :]
    low = common + 2 * count
    out[width:, :] = rows[...]
    slim[low:, :] = rows[...]
    line = width // LANES * slab
    for i, (e, b) in enumerate(PAIRS):
        value = held[owner[b], line + e : line + e + 1, :]
        out[width + PARENT + i : width + PARENT + i + 1, :] = value
        slim[low + PARENT + i : low + PARENT + i + 1, :] = value


def mix_kernel(shape, steps, pull, fields, *refs):
    n, slab, depth, block_cells = shape
    outs, held = refs[:-1], refs[-1]
    members = n * slab
    held[...] = (steps[NB] + pull[0:1, :]).reshape(n, slab, members)
    block = lax.axis_index("grid")
    if len(outs) == 1:
        blend = held[...].reshape(members, members)
    else:
        blend = jnp.concatenate([held[lax.bitwise_xor(block, i)] for i in range(n)], axis=0)
    for level in range(depth):
        value = high_dot(blend, fields[:, level].reshape(members, block_cells)).reshape(n, slab, block_cells)
        if len(outs) == 1:
            outs[0][:, level] = value
        else:
            for out, part in zip(outs, PARTS):
                for i, distance in enumerate(part):
                    out[i, level] = value[distance]


def chain_kernel(shape, own, near, far, cross, steps, out):
    members, groups, count = shape
    width = groups * count
    group = lax.axis_index("lev")
    sources = [own, near, far, cross]
    bases = [NB * width, NB * width, (NB - 1) * width + 2 * count, (NB - 1) * width + 2 * count]
    columns = [source[base : base + SPARE, :].T for source, base in zip(sources, bases)]
    parents, alphas = [], []
    for source, base in zip(sources, bases):
        parents.append(source[base + PARENT : base + PARENT + 8, :].astype(jnp.int32))
        alphas.append(source[base + ALPHA : base + ALPHA + 6, :])
    tilts = {}
    pulled = []
    for b in range(NB):
        kinds = [(q, later) for q in range(groups) for later in range(b + 1, NB)] + [(0, None)]
        height = -(-len(kinds) // 8) * 8
        index = lax.broadcasted_iota(jnp.int32, (height, members), 0)
        logs = jnp.zeros((height, members), F32)
        for q in range(groups if b < NB - 1 else 1):
            start = pl.multiple_of(b * width + lax.bitwise_xor(group, q) * count, count)
            total = jnp.zeros((count, members), F32)
            tilted = jnp.zeros((count, members), F32)
            for p, source in enumerate(sources):
                if b == NB - 1 and p > 1:
                    value = source[b * width + (p - 2) * count : b * width + (p - 1) * count, :]
                else:
                    value = source[pl.ds(start, count), :]
                for e in range(b):
                    i = PAIRS.index((e, b))
                    tilted = tilted + value * tilts[e, p, b]
                    alpha = alphas[p][i : i + 1]
                    moved = lane_take(value, parents[p][i : i + 1])
                    value = alpha * moved + (1.0 - alpha) * value
                total = total + value
            if b > 0:
                total = total + jnp.sum(tilted, axis=1, keepdims=True)
            miss = columns[q][:count, VALUE + b : VALUE + b + 1] - total
            square = miss * miss
            for row, (owner_group, later) in enumerate(kinds):
                if owner_group != q:
                    continue
                at = OWN + b if later is None else LATER + PAIRS.index((b, later))
                log = jnp.sum(columns[q][:count, at : at + 1] * square, axis=0, keepdims=True)
                logs = jnp.where(index == row, log, logs)
        expo = jnp.exp(logs - jnp.max(logs, axis=1, keepdims=True))
        tilt = expo / jnp.sum(expo, axis=1, keepdims=True) - 1.0 / members
        for row, (q, later) in enumerate(kinds):
            if later is None:
                pulled.append(tilt[row : row + 1])
            else:
                tilts[b, q, later] = tilt[row : row + 1]
    pull = jnp.zeros((8, members), F32)
    for b in range(NB):
        pull = pull + high_dot(jnp.broadcast_to(pulled[b], (8, members)), steps[b])
    out[...] = pull


def final_kernel(shape, *refs):
    n, slab, depth, block_cells = shape
    pieces, out = refs[:-1], refs[-1]
    block = lax.axis_index("grid")
    for i in range(n):
        region = i if len(pieces) == 1 else lax.bitwise_xor(block, ORDER[i])
        cells = pl.ds(pl.multiple_of(region * block_cells, LANES), block_cells)
        for level in range(depth):
            out[:, level, cells] = pieces[0][i, level] if len(pieces) == 1 else pieces[i][0, level]


def hop(value, distance, n):
    return lax.ppermute(value, "grid", [(j, j ^ distance) for j in range(n)])


def gather_pieces(piece, n):
    if n != 8:
        return [lax.all_to_all(jnp.broadcast_to(piece[None], (n,) + piece.shape), "grid", 0, 0, tiled=True)]
    pieces = {0: piece}
    for i in (4, 2, 6, 7, 1):
        pieces[i] = hop(piece, i, n)
    for i in (4, 2):
        pieces[i + 1] = hop(pieces[i], 1, n)
    return [pieces[i] for i in range(n)]


def exchange_parts(parts, n):
    if len(parts) == 1:
        return [lax.all_to_all(parts[0], "grid", 0, 0, tiled=True)]
    pieces = {0: parts[0]}
    for part, distances in zip(parts[1:], PARTS[1:]):
        pieces[distances[0]] = hop(part, distances[0], n)
        if len(distances) == 2:
            pieces[distances[1]] = hop(pieces[distances[0]][1:], 1, n)
    return [pieces[i] for i in ORDER]


def body(prior, channel_weights, obs_owner, obs_offset, obs_value, obs_error, ancestors):
    n, lev = lax.axis_size("grid"), lax.axis_size("lev")
    slab, depth, cells = prior.shape
    members = slab * n
    block_cells = cells // n
    groups = channel_weights.shape[1]
    count = obs_offset.shape[2]
    width = NB * groups * count
    scale = n / 2.0
    shape = jax.ShapeDtypeStruct
    parents = ancestors[:, 0]
    tall = width // LANES * slab + 8

    piece = call(
        functools.partial(pick_kernel, (slab, depth, block_cells, groups, count)),
        shape((tall, LANES), F32),
        [PLACE] * 5,
        scratch=[
            pltpu.SMEM(obs_owner.shape, jnp.int32),
            pltpu.VMEM(channel_weights.shape, F32),
            pltpu.VMEM(obs_offset.shape, jnp.int32),
            pltpu.VMEM(parents.shape, jnp.int32),
            pltpu.VMEM(prior.shape, F32),
            pltpu.SemaphoreType.DMA((5,)),
        ],
        moved=10**6,
        limit=None,
    )(obs_owner, channel_weights, obs_offset, parents, prior)
    pieces = gather_pieces(piece, n)
    send = call(
        functools.partial(retile_kernel, (n, slab, depth, block_cells)),
        shape((n, depth, slab, block_cells), F32),
        [VMEM],
        moved=10**6,
    )(prior)
    fields = lax.all_to_all(send, "grid", 0, 0, tiled=True)

    rows, steps = call(
        functools.partial(prep_kernel, (block_cells, count, scale, members)),
        [shape((SPARE, LANES), F32), shape((NB + 1, members, members), F32)],
        [SMEM, VMEM, VMEM, VMEM, VMEM],
        moved=10**6,
    )(obs_owner, obs_offset, obs_value, obs_error, parents)

    slim_height = (NB - 1) * groups * count + 2 * count + SPARE
    own, slim = call(
        functools.partial(turn_kernel, (n, slab, width, count)),
        [shape((width + SPARE, members), F32), shape((slim_height, members), F32)],
        [SMEM, VMEM, PLACE] + [VMEM] * len(pieces),
        scratch=[pltpu.VMEM((n, tall, LANES), F32)],
        moved=10**6,
    )(obs_owner, rows, send, *pieces)
    far = lax.ppermute(slim, "lev", [(j, j ^ 2) for j in range(lev)])
    near = lax.ppermute(own, "lev", [(j, j ^ 1) for j in range(lev)])
    cross = lax.ppermute(far, "lev", [(j, j ^ 1) for j in range(lev)])

    pull = call(
        functools.partial(chain_kernel, (members, groups, count)),
        shape((8, members), F32),
        [VMEM] * 5,
        moved=10**5,
    )(own, near, far, cross, steps)

    if n == 8:
        layout = [shape((len(part), depth, slab, block_cells), F32) for part in PARTS]
    else:
        layout = [shape((n, depth, slab, block_cells), F32)]
    send = call(
        functools.partial(mix_kernel, (n, slab, depth, block_cells)),
        layout,
        [VMEM] * 3,
        scratch=[pltpu.VMEM((n, slab, members), F32)],
        flops=10**8,
        moved=10**6,
    )(steps, pull, fields)
    moved = exchange_parts(send, n)

    return call(
        functools.partial(final_kernel, (n, slab, depth, block_cells)),
        shape((slab, depth, cells), F32),
        [VMEM] * len(moved),
        moved=10**6,
    )(*moved)


def solution(mesh):
    in_specs = (
        P("grid", "lev", None),
        P("lev", None),
        P(),
        P(),
        P(None, "lev", None),
        P(None, "lev", None),
        P(None, "lev", "grid", None),
    )
    out_specs = P("grid", "lev", None)
    return jax.shard_map(body, mesh=mesh, in_specs=in_specs, out_specs=out_specs, check_vma=False)
```

```python
import functools

import jax
import jax.numpy as jnp
from jax import lax
from jax.experimental import pallas as pl
from jax.experimental.pallas import tpu as pltpu
from jax.sharding import PartitionSpec as P

NB = 4
HIGH = lax.Precision.HIGHEST
LANES = 128
F32 = jnp.float32
VMEM = pl.BlockSpec(memory_space=pltpu.VMEM)
SMEM = pl.BlockSpec(memory_space=pltpu.SMEM)
PLACE = pl.BlockSpec(memory_space=pl.ANY)
LIMIT = 48 * 1024 * 1024

PARTS = ((0,), (4,), (5,), (6,), (7,), (2, 3), (1,))
ORDER = (0, 4, 5, 6, 7, 2, 1, 3)
PAIRS = [(e, b) for b in range(1, NB) for e in range(b)]
PARENT, ALPHA, LATER, VALUE, OWN, SPARE = 0, 6, 12, 18, 22, 32


def call(kernel, out_shapes, in_specs, scratch=(), flops=0, moved=0, limit=LIMIT):
    many = isinstance(out_shapes, (list, tuple))
    return pl.pallas_call(
        kernel,
        out_shape=out_shapes,
        in_specs=in_specs,
        out_specs=[VMEM] * len(out_shapes) if many else VMEM,
        scratch_shapes=list(scratch),
        compiler_params=pltpu.CompilerParams(vmem_limit_bytes=limit),
        cost_estimate=pl.CostEstimate(flops=flops, bytes_accessed=moved, transcendentals=0),
    )


def high_dot(a, b):
    return lax.dot_general(a, b, (((1,), (0,)), ((), ())), precision=HIGH, preferred_element_type=F32)


def lane_take(value, row):
    where = jnp.broadcast_to(row, value.shape)
    return jnp.take_along_axis(value, where, axis=1, mode="promise_in_bounds")


def pick_kernel(shape, *refs):
    slab, depth, block_cells, groups, count = shape
    out, arrivals = refs[5], refs[11]
    copies = [pltpu.make_async_copy(refs[i], refs[6 + i], arrivals.at[i]) for i in range(5)]
    for copy in copies:
        copy.start()
    for copy in copies:
        copy.wait()
    owner, weights, offsets, ancestors, prior = refs[6:11]
    width = groups * count
    per = LANES // count
    blocks = width // LANES
    level_of = lax.broadcasted_iota(jnp.int32, (slab, depth, LANES), 1)
    gains = []
    for c in range(blocks):
        gain = jnp.zeros((slab, depth, LANES), F32)
        for level in range(depth):
            row = jnp.concatenate(
                [
                    jnp.broadcast_to(weights[level : level + 1, g : g + 1], (1, count))
                    for g in range(c * per, (c + 1) * per)
                ],
                axis=1,
            )
            gain = jnp.where(level_of == level, row[None], gain)
        gains.append(gain.reshape(slab * depth, LANES))
    for b in range(NB):
        start = pl.multiple_of(owner[b] * block_cells, LANES)
        both = prior[:, :, pl.ds(start, block_cells)].reshape(slab * depth, block_cells)
        for c in range(blocks):
            cell = jnp.concatenate([offsets[b, g : g + 1, :] for g in range(c * per, (c + 1) * per)], axis=1)
            low, high = lax.rem(cell, LANES), lax.div(cell, LANES)
            found = jnp.zeros((slab * depth, LANES), F32)
            for h in range(block_cells // LANES):
                part = lane_take(both[:, h * LANES : (h + 1) * LANES], low)
                found = jnp.where(high == h, part, found)
            line = (b * blocks + c) * slab
            out[line : line + slab, :] = jnp.sum((found * gains[c]).reshape(slab, depth, LANES), axis=1)
    line = NB * width // LANES * slab
    out[line:, :] = jnp.zeros((out.shape[0] - line, LANES), F32)
    for b in range(NB):
        out[line + b : line + b + 1, :] = ancestors[b].astype(F32)


def retile_kernel(shape, prior, out):
    n, slab, depth, block_cells = shape
    for i in range(n):
        for level in range(depth):
            out[i, level] = prior[:, level, i * block_cells : (i + 1) * block_cells]


def prep_kernel(shape, owner, offsets, values, errors, ancestors, rows, steps):
    block_cells, count, scale, members = shape
    block, group = lax.axis_index("grid"), lax.axis_index("lev")
    index = lax.broadcasted_iota(jnp.int32, (8, 1), 0)
    region = jnp.full((8, 1), block, jnp.int32)
    for b in range(1, NB):
        region = jnp.where(index == b - 1, owner[b], region)
    centre = region.astype(F32) + 0.5
    rows[...] = jnp.zeros((SPARE, LANES), F32)
    row = lax.broadcasted_iota(jnp.int32, (members, members), 0)
    column = lax.broadcasted_iota(jnp.int32, (members, members), 1)
    turned = (row == column).astype(F32)
    for b in range(NB):
        cells = owner[b] * block_cells + offsets[b, pl.ds(group, 1), :]
        distance = (centre - cells.astype(F32) / block_cells) / scale
        taper = jnp.exp(-0.5 * distance * distance)
        alpha = 0.8 * (1.0 - jnp.exp(-jnp.sum(taper, axis=1, keepdims=True) / count))
        error = errors[b]
        part = (-0.5 / count) * (taper / (error * error))
        for later in range(b + 1, NB):
            i = PAIRS.index((b, later))
            rows[ALPHA + i : ALPHA + i + 1, :] = jnp.broadcast_to(alpha[later - 1 : later], (1, LANES))
            rows[LATER + i : LATER + i + 1, :count] = part[later - 1 : later]
        rows[VALUE + b : VALUE + b + 1, :count] = values[b]
        rows[OWN + b : OWN + b + 1, :count] = part[NB - 1 : NB]
        steps[b] = turned.T
        own = alpha[NB - 1 : NB]
        turned = own * lane_take(turned, ancestors[b]) + (1.0 - own) * turned
    steps[NB] = turned.T


def turn_kernel(shape, owner, rows, ahead, *refs):
    n, slab, width, count = shape
    pieces, out, slim, held = refs[:-3], refs[-3], refs[-2], refs[-1]
    members = n * slab
    block, group = lax.axis_index("grid"), lax.axis_index("lev")
    if len(pieces) == 1:
        held[...] = pieces[0][...]
    else:
        for distance, piece in zip(ORDER, pieces):
            held[lax.bitwise_xor(block, distance)] = piece[...]
    common = width // NB * (NB - 1)
    for i in range(width // LANES):
        value = held[:, i * slab : (i + 1) * slab, :].reshape(members, LANES).T
        out[i * LANES : (i + 1) * LANES, :] = value
        if (i + 1) * LANES <= common:
            slim[i * LANES : (i + 1) * LANES, :] = value
    for i in range(2):
        start = pl.multiple_of(common + lax.bitwise_xor(group, 2 + i) * count, count)
        slim[common + i * count : common + (i + 1) * count, :] = out[pl.ds(start, count), :]
    low = common + 2 * count
    out[width:, :] = rows[...]
    slim[low:, :] = rows[...]
    line = width // LANES * slab
    for i, (e, b) in enumerate(PAIRS):
        value = held[owner[b], line + e : line + e + 1, :]
        out[width + PARENT + i : width + PARENT + i + 1, :] = value
        slim[low + PARENT + i : low + PARENT + i + 1, :] = value


def mix_kernel(shape, steps, pull, fields, *refs):
    n, slab, depth, block_cells = shape
    outs, held = refs[:-1], refs[-1]
    members = n * slab
    held[...] = (steps[NB] + pull[0:1, :]).reshape(n, slab, members)
    block = lax.axis_index("grid")
    if len(outs) == 1:
        blend = held[...].reshape(members, members)
    else:
        blend = jnp.concatenate([held[lax.bitwise_xor(block, i)] for i in range(n)], axis=0)
    for level in range(depth):
        value = high_dot(blend, fields[:, level].reshape(members, block_cells)).reshape(n, slab, block_cells)
        if len(outs) == 1:
            outs[0][:, level] = value
        else:
            for out, part in zip(outs, PARTS):
                for i, distance in enumerate(part):
                    out[i, level] = value[distance]


def chain_kernel(shape, own, near, far, cross, steps, out):
    members, groups, count = shape
    width = groups * count
    group = lax.axis_index("lev")
    sources = [own, near, far, cross]
    bases = [NB * width, NB * width, (NB - 1) * width + 2 * count, (NB - 1) * width + 2 * count]
    columns = [source[base : base + SPARE, :].T for source, base in zip(sources, bases)]
    parents, alphas = [], []
    for source, base in zip(sources, bases):
        parents.append(source[base + PARENT : base + PARENT + 8, :].astype(jnp.int32))
        alphas.append(source[base + ALPHA : base + ALPHA + 6, :])
    tilts = {}
    pulled = []
    for b in range(NB):
        kinds = [(q, later) for q in range(groups) for later in range(b + 1, NB)] + [(0, None)]
        height = -(-len(kinds) // 8) * 8
        index = lax.broadcasted_iota(jnp.int32, (height, members), 0)
        logs = jnp.zeros((height, members), F32)
        for q in range(groups if b < NB - 1 else 1):
            start = pl.multiple_of(b * width + lax.bitwise_xor(group, q) * count, count)
            total = jnp.zeros((count, members), F32)
            tilted = jnp.zeros((count, members), F32)
            for p, source in enumerate(sources):
                if b == NB - 1 and p > 1:
                    value = source[b * width + (p - 2) * count : b * width + (p - 1) * count, :]
                else:
                    value = source[pl.ds(start, count), :]
                for e in range(b):
                    i = PAIRS.index((e, b))
                    tilted = tilted + value * tilts[e, p, b]
                    alpha = alphas[p][i : i + 1]
                    moved = lane_take(value, parents[p][i : i + 1])
                    value = alpha * moved + (1.0 - alpha) * value
                total = total + value
            if b > 0:
                total = total + jnp.sum(tilted, axis=1, keepdims=True)
            miss = columns[q][:count, VALUE + b : VALUE + b + 1] - total
            square = miss * miss
            for row, (owner_group, later) in enumerate(kinds):
                if owner_group != q:
                    continue
                at = OWN + b if later is None else LATER + PAIRS.index((b, later))
                log = jnp.sum(columns[q][:count, at : at + 1] * square, axis=0, keepdims=True)
                logs = jnp.where(index == row, log, logs)
        expo = jnp.exp(logs - jnp.max(logs, axis=1, keepdims=True))
        tilt = expo / jnp.sum(expo, axis=1, keepdims=True) - 1.0 / members
        for row, (q, later) in enumerate(kinds):
            if later is None:
                pulled.append(tilt[row : row + 1])
            else:
                tilts[b, q, later] = tilt[row : row + 1]
    pull = jnp.zeros((8, members), F32)
    for b in range(NB):
        pull = pull + high_dot(jnp.broadcast_to(pulled[b], (8, members)), steps[b])
    out[...] = pull


def final_kernel(shape, *refs):
    n, slab, depth, block_cells = shape
    pieces, out = refs[:-1], refs[-1]
    block = lax.axis_index("grid")
    for i in range(n):
        region = i if len(pieces) == 1 else lax.bitwise_xor(block, ORDER[i])
        cells = pl.ds(pl.multiple_of(region * block_cells, LANES), block_cells)
        for level in range(depth):
            out[:, level, cells] = pieces[0][i, level] if len(pieces) == 1 else pieces[i][0, level]


def hop(value, distance, n):
    return lax.ppermute(value, "grid", [(j, j ^ distance) for j in range(n)])


def gather_pieces(piece, n):
    if n != 8:
        return [lax.all_to_all(jnp.broadcast_to(piece[None], (n,) + piece.shape), "grid", 0, 0, tiled=True)]
    pieces = {0: piece}
    for i in (4, 2, 6, 7, 1):
        pieces[i] = hop(piece, i, n)
    for i in (4, 2):
        pieces[i + 1] = hop(pieces[i], 1, n)
    return [pieces[i] for i in ORDER]


def exchange_parts(parts, n):
    if len(parts) == 1:
        return [lax.all_to_all(parts[0], "grid", 0, 0, tiled=True)]
    pieces = {0: parts[0]}
    for part, distances in zip(parts[1:], PARTS[1:]):
        pieces[distances[0]] = hop(part, distances[0], n)
        if len(distances) == 2:
            pieces[distances[1]] = hop(pieces[distances[0]][1:], 1, n)
    return [pieces[i] for i in ORDER]


def body(prior, channel_weights, obs_owner, obs_offset, obs_value, obs_error, ancestors):
    n, lev = lax.axis_size("grid"), lax.axis_size("lev")
    slab, depth, cells = prior.shape
    members = slab * n
    block_cells = cells // n
    groups = channel_weights.shape[1]
    count = obs_offset.shape[2]
    width = NB * groups * count
    scale = n / 2.0
    shape = jax.ShapeDtypeStruct
    parents = ancestors[:, 0]
    tall = width // LANES * slab + 8

    piece = call(
        functools.partial(pick_kernel, (slab, depth, block_cells, groups, count)),
        shape((tall, LANES), F32),
        [PLACE] * 5,
        scratch=[
            pltpu.SMEM(obs_owner.shape, jnp.int32),
            pltpu.VMEM(channel_weights.shape, F32),
            pltpu.VMEM(obs_offset.shape, jnp.int32),
            pltpu.VMEM(parents.shape, jnp.int32),
            pltpu.VMEM(prior.shape, F32),
            pltpu.SemaphoreType.DMA((5,)),
        ],
        moved=10**6,
        limit=None,
    )(obs_owner, channel_weights, obs_offset, parents, prior)
    pieces = gather_pieces(piece, n)
    send = call(
        functools.partial(retile_kernel, (n, slab, depth, block_cells)),
        shape((n, depth, slab, block_cells), F32),
        [VMEM],
        moved=10**6,
    )(prior)
    fields = lax.all_to_all(send, "grid", 0, 0, tiled=True)

    rows, steps = call(
        functools.partial(prep_kernel, (block_cells, count, scale, members)),
        [shape((SPARE, LANES), F32), shape((NB + 1, members, members), F32)],
        [SMEM, VMEM, VMEM, VMEM, VMEM],
        moved=10**6,
    )(obs_owner, obs_offset, obs_value, obs_error, parents)

    slim_height = (NB - 1) * groups * count + 2 * count + SPARE
    own, slim = call(
        functools.partial(turn_kernel, (n, slab, width, count)),
        [shape((width + SPARE, members), F32), shape((slim_height, members), F32)],
        [SMEM, VMEM, PLACE] + [VMEM] * len(pieces),
        scratch=[pltpu.VMEM((n, tall, LANES), F32)],
        moved=10**6,
    )(obs_owner, rows, send, *pieces)
    far = lax.ppermute(slim, "lev", [(j, j ^ 2) for j in range(lev)])
    near = lax.ppermute(own, "lev", [(j, j ^ 1) for j in range(lev)])
    cross = lax.ppermute(far, "lev", [(j, j ^ 1) for j in range(lev)])

    pull = call(
        functools.partial(chain_kernel, (members, groups, count)),
        shape((8, members), F32),
        [VMEM] * 5,
        moved=10**5,
    )(own, near, far, cross, steps)

    if n == 8:
        layout = [shape((len(part), depth, slab, block_cells), F32) for part in PARTS]
    else:
        layout = [shape((n, depth, slab, block_cells), F32)]
    send = call(
        functools.partial(mix_kernel, (n, slab, depth, block_cells)),
        layout,
        [VMEM] * 3,
        scratch=[pltpu.VMEM((n, slab, members), F32)],
        flops=10**8,
        moved=10**6,
    )(steps, pull, fields)
    moved = exchange_parts(send, n)

    return call(
        functools.partial(final_kernel, (n, slab, depth, block_cells)),
        shape((slab, depth, cells), F32),
        [VMEM] * len(moved),
        moved=10**6,
    )(*moved)


def solution(mesh):
    in_specs = (
        P("grid", "lev", None),
        P("lev", None),
        P(),
        P(),
        P(None, "lev", None),
        P(None, "lev", None),
        P(None, "lev", "grid", None),
    )
    out_specs = P("grid", "lev", None)
    return jax.shard_map(body, mesh=mesh, in_specs=in_specs, out_specs=out_specs, check_vma=False)
```

```python
import functools

import jax
import jax.numpy as jnp
from jax import lax
from jax.experimental import pallas as pl
from jax.experimental.pallas import tpu as pltpu
from jax.sharding import PartitionSpec as P

NB = 4
HIGH = lax.Precision.HIGHEST
LANES = 128
F32 = jnp.float32
VMEM = pl.BlockSpec(memory_space=pltpu.VMEM)
SMEM = pl.BlockSpec(memory_space=pltpu.SMEM)
PLACE = pl.BlockSpec(memory_space=pl.ANY)
LIMIT = 48 * 1024 * 1024

PARTS = ((0,), (4,), (5,), (6,), (7,), (2, 3), (1,))
PAIRS = [(e, b) for b in range(1, NB) for e in range(b)]
PARENT, ALPHA, LATER, VALUE, OWN, SPARE = 0, 6, 12, 18, 22, 32


def call(kernel, out_shapes, in_specs, scratch=(), flops=0, moved=0, limit=LIMIT, out_specs=None, aliases={}):
    many = isinstance(out_shapes, (list, tuple))
    return pl.pallas_call(
        kernel,
        out_shape=out_shapes,
        in_specs=in_specs,
        out_specs=out_specs or ([VMEM] * len(out_shapes) if many else VMEM),
        input_output_aliases=aliases,
        scratch_shapes=list(scratch),
        compiler_params=pltpu.CompilerParams(vmem_limit_bytes=limit),
        cost_estimate=pl.CostEstimate(flops=flops, bytes_accessed=moved, transcendentals=0),
    )


def high_dot(a, b):
    return lax.dot_general(a, b, (((1,), (0,)), ((), ())), precision=HIGH, preferred_element_type=F32)


def lane_take(value, row):
    where = jnp.broadcast_to(row, value.shape)
    return jnp.take_along_axis(value, where, axis=1, mode="promise_in_bounds")


def pick_kernel(shape, *refs):
    slab, depth, block_cells, groups, count = shape
    out, arrivals = refs[5], refs[11]
    copies = [pltpu.make_async_copy(refs[i], refs[6 + i], arrivals.at[i]) for i in range(5)]
    for copy in copies:
        copy.start()
    for copy in copies:
        copy.wait()
    owner, weights, offsets, ancestors, prior = refs[6:11]
    width = groups * count
    per = LANES // count
    blocks = width // LANES
    level_of = lax.broadcasted_iota(jnp.int32, (slab, depth, LANES), 1)
    gains = []
    for c in range(blocks):
        gain = jnp.zeros((slab, depth, LANES), F32)
        for level in range(depth):
            row = jnp.concatenate(
                [
                    jnp.broadcast_to(weights[level : level + 1, g : g + 1], (1, count))
                    for g in range(c * per, (c + 1) * per)
                ],
                axis=1,
            )
            gain = jnp.where(level_of == level, row[None], gain)
        gains.append(gain.reshape(slab * depth, LANES))
    for b in range(NB):
        start = pl.multiple_of(owner[b] * block_cells, LANES)
        both = prior[:, :, pl.ds(start, block_cells)].reshape(slab * depth, block_cells)
        for c in range(blocks):
            cell = jnp.concatenate([offsets[b, g : g + 1, :] for g in range(c * per, (c + 1) * per)], axis=1)
            low, high = lax.rem(cell, LANES), lax.div(cell, LANES)
            found = jnp.zeros((slab * depth, LANES), F32)
            for h in range(block_cells // LANES):
                part = lane_take(both[:, h * LANES : (h + 1) * LANES], low)
                found = jnp.where(high == h, part, found)
            line = (b * blocks + c) * slab
            out[line : line + slab, :] = jnp.sum((found * gains[c]).reshape(slab, depth, LANES), axis=1)
    line = NB * width // LANES * slab
    out[line:, :] = jnp.zeros((out.shape[0] - line, LANES), F32)
    for b in range(NB):
        out[line + b : line + b + 1, :] = ancestors[b].astype(F32)


def retile_kernel(shape, prior, out):
    n, slab, depth, block_cells = shape
    for i in range(n):
        for level in range(depth):
            out[i, level] = prior[:, level, i * block_cells : (i + 1) * block_cells]


def prep_kernel(shape, owner, offsets, values, errors, ancestors, rows, steps):
    block_cells, count, scale, members = shape
    block, group = lax.axis_index("grid"), lax.axis_index("lev")
    index = lax.broadcasted_iota(jnp.int32, (8, 1), 0)
    region = jnp.full((8, 1), block, jnp.int32)
    for b in range(1, NB):
        region = jnp.where(index == b - 1, owner[b], region)
    centre = region.astype(F32) + 0.5
    rows[...] = jnp.zeros((SPARE, LANES), F32)
    row = lax.broadcasted_iota(jnp.int32, (members, members), 0)
    column = lax.broadcasted_iota(jnp.int32, (members, members), 1)
    turned = (row == column).astype(F32)
    for b in range(NB):
        cells = owner[b] * block_cells + offsets[b, pl.ds(group, 1), :]
        distance = (centre - cells.astype(F32) / block_cells) / scale
        taper = jnp.exp(-0.5 * distance * distance)
        alpha = 0.8 * (1.0 - jnp.exp(-jnp.sum(taper, axis=1, keepdims=True) / count))
        error = errors[b]
        part = (-0.5 / count) * (taper / (error * error))
        for later in range(b + 1, NB):
            i = PAIRS.index((b, later))
            rows[ALPHA + i : ALPHA + i + 1, :] = jnp.broadcast_to(alpha[later - 1 : later], (1, LANES))
            rows[LATER + i : LATER + i + 1, :count] = part[later - 1 : later]
        rows[VALUE + b : VALUE + b + 1, :count] = values[b]
        rows[OWN + b : OWN + b + 1, :count] = part[NB - 1 : NB]
        steps[b] = turned.T
        own = alpha[NB - 1 : NB]
        turned = own * lane_take(turned, ancestors[b]) + (1.0 - own) * turned
    steps[NB] = turned.T


def turn_kernel(shape, owner, rows, ahead, *refs):
    n, slab, width, count = shape
    pieces, out, slim, held = refs[:-3], refs[-3], refs[-2], refs[-1]
    members = n * slab
    block, group = lax.axis_index("grid"), lax.axis_index("lev")
    if len(pieces) == 1:
        held[...] = pieces[0][...]
    else:
        for i, piece in enumerate(pieces):
            held[lax.bitwise_xor(block, i)] = piece[...]
    common = width // NB * (NB - 1)
    for i in range(width // LANES):
        value = held[:, i * slab : (i + 1) * slab, :].reshape(members, LANES).T
        out[i * LANES : (i + 1) * LANES, :] = value
        if (i + 1) * LANES <= common:
            slim[i * LANES : (i + 1) * LANES, :] = value
    for i in range(2):
        start = pl.multiple_of(common + lax.bitwise_xor(group, 2 + i) * count, count)
        slim[common + i * count : common + (i + 1) * count, :] = out[pl.ds(start, count), :]
    low = common + 2 * count
    out[width:, :] = rows[...]
    slim[low:, :] = rows[...]
    line = width // LANES * slab
    for i, (e, b) in enumerate(PAIRS):
        value = held[owner[b], line + e : line + e + 1, :]
        out[width + PARENT + i : width + PARENT + i + 1, :] = value
        slim[low + PARENT + i : low + PARENT + i + 1, :] = value


def mix_kernel(shape, steps, pull, fields, *refs):
    n, slab, depth, block_cells = shape
    outs, held = refs[:-1], refs[-1]
    members = n * slab
    held[...] = (steps[NB] + pull[0:1, :]).reshape(n, slab, members)
    block = lax.axis_index("grid")
    if len(outs) == 1:
        blend = held[...].reshape(members, members)
    else:
        blend = jnp.concatenate([held[lax.bitwise_xor(block, i)] for i in range(n)], axis=0)
    for level in range(depth):
        value = high_dot(blend, fields[:, level].reshape(members, block_cells)).reshape(n, slab, block_cells)
        if len(outs) == 1:
            outs[0][:, level] = value
        else:
            for out, part in zip(outs, PARTS):
                for i, distance in enumerate(part):
                    out[i, level] = value[distance]


def chain_kernel(shape, own, near, far, cross, steps, out):
    members, groups, count = shape
    width = groups * count
    group = lax.axis_index("lev")
    sources = [own, near, far, cross]
    bases = [NB * width, NB * width, (NB - 1) * width + 2 * count, (NB - 1) * width + 2 * count]
    columns = [source[base : base + SPARE, :].T for source, base in zip(sources, bases)]
    parents, alphas = [], []
    for source, base in zip(sources, bases):
        parents.append(source[base + PARENT : base + PARENT + 8, :].astype(jnp.int32))
        alphas.append(source[base + ALPHA : base + ALPHA + 6, :])
    tilts = {}
    pulled = []
    for b in range(NB):
        kinds = [(q, later) for q in range(groups) for later in range(b + 1, NB)] + [(0, None)]
        height = -(-len(kinds) // 8) * 8
        index = lax.broadcasted_iota(jnp.int32, (height, members), 0)
        logs = jnp.zeros((height, members), F32)
        for q in range(groups if b < NB - 1 else 1):
            start = pl.multiple_of(b * width + lax.bitwise_xor(group, q) * count, count)
            total = jnp.zeros((count, members), F32)
            tilted = jnp.zeros((count, members), F32)
            for p, source in enumerate(sources):
                if b == NB - 1 and p > 1:
                    value = source[b * width + (p - 2) * count : b * width + (p - 1) * count, :]
                else:
                    value = source[pl.ds(start, count), :]
                for e in range(b):
                    i = PAIRS.index((e, b))
                    tilted = tilted + value * tilts[e, p, b]
                    alpha = alphas[p][i : i + 1]
                    moved = lane_take(value, parents[p][i : i + 1])
                    value = alpha * moved + (1.0 - alpha) * value
                total = total + value
            if b > 0:
                total = total + jnp.sum(tilted, axis=1, keepdims=True)
            miss = columns[q][:count, VALUE + b : VALUE + b + 1] - total
            square = miss * miss
            for row, (owner_group, later) in enumerate(kinds):
                if owner_group != q:
                    continue
                at = OWN + b if later is None else LATER + PAIRS.index((b, later))
                log = jnp.sum(columns[q][:count, at : at + 1] * square, axis=0, keepdims=True)
                logs = jnp.where(index == row, log, logs)
        expo = jnp.exp(logs - jnp.max(logs, axis=1, keepdims=True))
        tilt = expo / jnp.sum(expo, axis=1, keepdims=True) - 1.0 / members
        for row, (q, later) in enumerate(kinds):
            if later is None:
                pulled.append(tilt[row : row + 1])
            else:
                tilts[b, q, later] = tilt[row : row + 1]
    pull = jnp.zeros((8, members), F32)
    for b in range(NB):
        pull = pull + high_dot(jnp.broadcast_to(pulled[b], (8, members)), steps[b])
    out[...] = pull


def final_kernel(shape, arrived, out):
    n, slab, depth, block_cells = shape
    for i in range(n):
        for level in range(depth):
            out[:, level, i * block_cells : (i + 1) * block_cells] = arrived[i, level]


def place_kernel(shape, places, skip, *refs):
    slab, depth, block_cells = shape
    pieces, out, held, done = refs[skip:-3], refs[-3], refs[-2], refs[-1]
    block = lax.axis_index("grid")
    copies = []
    for k, (i, j, distance) in enumerate(places):
        for level in range(depth):
            held[k, :, level, :] = pieces[i][j, level]
        start = pl.multiple_of(lax.bitwise_xor(block, distance) * block_cells, LANES)
        copies.append(pltpu.make_async_copy(held.at[k], out.at[:, :, pl.ds(start, block_cells)], done.at[k]))
        copies[-1].start()
    for copy in copies:
        copy.wait()


def place(shape, whole, places, pieces, before=None, moved=0):
    slab, depth, block_cells = shape
    given = [] if before is None else [before]
    return call(
        functools.partial(place_kernel, shape, places, len(given)),
        whole,
        [PLACE] * len(given) + [VMEM] * len(pieces),
        scratch=[
            pltpu.VMEM((len(places), slab, depth, block_cells), F32),
            pltpu.SemaphoreType.DMA((len(places),)),
        ],
        moved=moved,
        out_specs=PLACE,
        aliases={0: 0} if given else {},
    )(*given, *pieces)


def hop(value, distance, n):
    return lax.ppermute(value, "grid", [(j, j ^ distance) for j in range(n)])


def gather_pieces(piece, n):
    if n != 8:
        return [lax.all_to_all(jnp.broadcast_to(piece[None], (n,) + piece.shape), "grid", 0, 0, tiled=True)]
    pieces = {0: piece}
    for i in (4, 2, 6, 7, 1):
        pieces[i] = hop(piece, i, n)
    for i in (4, 2):
        pieces[i + 1] = hop(pieces[i], 1, n)
    return [pieces[i] for i in range(n)]


def exchange_parts(parts, shape, whole, n):
    far = [parts[0]] + [hop(part, distances[0], n) for part, distances in zip(parts[1:5], PARTS[1:5])]
    near = hop(parts[5], PARTS[5][0], n)
    beside, onward = hop(parts[6], 1, n), hop(near[1:], 1, n)
    out = place(shape, whole, [(i, 0, PARTS[i][0]) for i in range(5)], far, moved=10**6)
    return place(shape, whole, [(0, 0, 2), (1, 0, 1), (2, 0, 3)], [near, beside, onward], out, moved=10**6)


def body(prior, channel_weights, obs_owner, obs_offset, obs_value, obs_error, ancestors):
    n, lev = lax.axis_size("grid"), lax.axis_size("lev")
    slab, depth, cells = prior.shape
    members = slab * n
    block_cells = cells // n
    groups = channel_weights.shape[1]
    count = obs_offset.shape[2]
    width = NB * groups * count
    scale = n / 2.0
    shape = jax.ShapeDtypeStruct
    parents = ancestors[:, 0]
    tall = width // LANES * slab + 8

    piece = call(
        functools.partial(pick_kernel, (slab, depth, block_cells, groups, count)),
        shape((tall, LANES), F32),
        [PLACE] * 5,
        scratch=[
            pltpu.SMEM(obs_owner.shape, jnp.int32),
            pltpu.VMEM(channel_weights.shape, F32),
            pltpu.VMEM(obs_offset.shape, jnp.int32),
            pltpu.VMEM(parents.shape, jnp.int32),
            pltpu.VMEM(prior.shape, F32),
            pltpu.SemaphoreType.DMA((5,)),
        ],
        moved=10**6,
        limit=None,
    )(obs_owner, channel_weights, obs_offset, parents, prior)
    pieces = gather_pieces(piece, n)
    send = call(
        functools.partial(retile_kernel, (n, slab, depth, block_cells)),
        shape((n, depth, slab, block_cells), F32),
        [VMEM],
        moved=10**6,
    )(prior)
    fields = lax.all_to_all(send, "grid", 0, 0, tiled=True)

    rows, steps = call(
        functools.partial(prep_kernel, (block_cells, count, scale, members)),
        [shape((SPARE, LANES), F32), shape((NB + 1, members, members), F32)],
        [SMEM, VMEM, VMEM, VMEM, VMEM],
        moved=10**6,
    )(obs_owner, obs_offset, obs_value, obs_error, parents)

    slim_height = (NB - 1) * groups * count + 2 * count + SPARE
    own, slim = call(
        functools.partial(turn_kernel, (n, slab, width, count)),
        [shape((width + SPARE, members), F32), shape((slim_height, members), F32)],
        [SMEM, VMEM, PLACE] + [VMEM] * len(pieces),
        scratch=[pltpu.VMEM((n, tall, LANES), F32)],
        moved=10**6,
    )(obs_owner, rows, send, *pieces)
    far = lax.ppermute(slim, "lev", [(j, j ^ 2) for j in range(lev)])
    near = lax.ppermute(own, "lev", [(j, j ^ 1) for j in range(lev)])
    cross = lax.ppermute(far, "lev", [(j, j ^ 1) for j in range(lev)])

    pull = call(
        functools.partial(chain_kernel, (members, groups, count)),
        shape((8, members), F32),
        [VMEM] * 5,
        moved=10**5,
    )(own, near, far, cross, steps)

    if n == 8:
        layout = [shape((len(part), depth, slab, block_cells), F32) for part in PARTS]
    else:
        layout = [shape((n, depth, slab, block_cells), F32)]
    send = call(
        functools.partial(mix_kernel, (n, slab, depth, block_cells)),
        layout,
        [VMEM] * 3,
        scratch=[pltpu.VMEM((n, slab, members), F32)],
        flops=10**8,
        moved=10**6,
    )(steps, pull, fields)
    whole = shape((slab, depth, cells), F32)
    if n == 8:
        return exchange_parts(send, (slab, depth, block_cells), whole, n)
    moved = lax.all_to_all(send[0], "grid", 0, 0, tiled=True)
    return call(functools.partial(final_kernel, (n, slab, depth, block_cells)), whole, [VMEM], moved=10**6)(moved)


def solution(mesh):
    in_specs = (
        P("grid", "lev", None),
        P("lev", None),
        P(),
        P(),
        P(None, "lev", None),
        P(None, "lev", None),
        P(None, "lev", "grid", None),
    )
    out_specs = P("grid", "lev", None)
    return jax.shard_map(body, mesh=mesh, in_specs=in_specs, out_specs=out_specs, check_vma=False)
```

```python
import functools

import jax
import jax.numpy as jnp
from jax import lax
from jax.experimental import pallas as pl
from jax.experimental.pallas import tpu as pltpu
from jax.sharding import PartitionSpec as P

NB = 4
HIGH = lax.Precision.HIGHEST
LANES = 128
F32 = jnp.float32
VMEM = pl.BlockSpec(memory_space=pltpu.VMEM)
SMEM = pl.BlockSpec(memory_space=pltpu.SMEM)
PLACE = pl.BlockSpec(memory_space=pl.ANY)
LIMIT = 48 * 1024 * 1024

GATHERED = (0, 4, 5, 2, 3, 1, 6, 7)
PARTS = ((0,), (4,), (5,), (6,), (7,), (2, 3), (1,))
PAIRS = [(e, b) for b in range(1, NB) for e in range(b)]
PARENT, ALPHA, LATER, VALUE, OWN, SPARE = 0, 6, 12, 18, 22, 32


def call(kernel, out_shapes, in_specs, scratch=(), flops=0, moved=0, limit=LIMIT, out_specs=None, aliases={}):
    many = isinstance(out_shapes, (list, tuple))
    return pl.pallas_call(
        kernel,
        out_shape=out_shapes,
        in_specs=in_specs,
        out_specs=out_specs or ([VMEM] * len(out_shapes) if many else VMEM),
        input_output_aliases=aliases,
        scratch_shapes=list(scratch),
        compiler_params=pltpu.CompilerParams(vmem_limit_bytes=limit),
        cost_estimate=pl.CostEstimate(flops=flops, bytes_accessed=moved, transcendentals=0),
    )


def high_dot(a, b):
    return lax.dot_general(a, b, (((1,), (0,)), ((), ())), precision=HIGH, preferred_element_type=F32)


def lane_take(value, row):
    where = jnp.broadcast_to(row, value.shape)
    return jnp.take_along_axis(value, where, axis=1, mode="promise_in_bounds")


def pick_kernel(shape, *refs):
    slab, depth, block_cells, groups, count = shape
    out, arrivals = refs[5], refs[11]
    copies = [pltpu.make_async_copy(refs[i], refs[6 + i], arrivals.at[i]) for i in range(5)]
    for copy in copies:
        copy.start()
    for copy in copies:
        copy.wait()
    owner, weights, offsets, ancestors, prior = refs[6:11]
    width = groups * count
    per = LANES // count
    blocks = width // LANES
    level_of = lax.broadcasted_iota(jnp.int32, (slab, depth, LANES), 1)
    gains = []
    for c in range(blocks):
        gain = jnp.zeros((slab, depth, LANES), F32)
        for level in range(depth):
            row = jnp.concatenate(
                [
                    jnp.broadcast_to(weights[level : level + 1, g : g + 1], (1, count))
                    for g in range(c * per, (c + 1) * per)
                ],
                axis=1,
            )
            gain = jnp.where(level_of == level, row[None], gain)
        gains.append(gain.reshape(slab * depth, LANES))
    for b in range(NB):
        start = pl.multiple_of(owner[b] * block_cells, LANES)
        both = prior[:, :, pl.ds(start, block_cells)].reshape(slab * depth, block_cells)
        for c in range(blocks):
            cell = jnp.concatenate([offsets[b, g : g + 1, :] for g in range(c * per, (c + 1) * per)], axis=1)
            low, high = lax.rem(cell, LANES), lax.div(cell, LANES)
            found = jnp.zeros((slab * depth, LANES), F32)
            for h in range(block_cells // LANES):
                part = lane_take(both[:, h * LANES : (h + 1) * LANES], low)
                found = jnp.where(high == h, part, found)
            line = (b * blocks + c) * slab
            out[line : line + slab, :] = jnp.sum((found * gains[c]).reshape(slab, depth, LANES), axis=1)
    line = NB * width // LANES * slab
    out[line:, :] = jnp.zeros((out.shape[0] - line, LANES), F32)
    for b in range(NB):
        out[line + b : line + b + 1, :] = ancestors[b].astype(F32)


def retile_kernel(shape, prior, out):
    n, slab, depth, block_cells = shape
    for i in range(n):
        for level in range(depth):
            out[i, level] = prior[:, level, i * block_cells : (i + 1) * block_cells]


def prep_kernel(shape, owner, offsets, values, errors, ancestors, rows, steps):
    block_cells, count, scale, members = shape
    block, group = lax.axis_index("grid"), lax.axis_index("lev")
    index = lax.broadcasted_iota(jnp.int32, (8, 1), 0)
    region = jnp.full((8, 1), block, jnp.int32)
    for b in range(1, NB):
        region = jnp.where(index == b - 1, owner[b], region)
    centre = region.astype(F32) + 0.5
    rows[...] = jnp.zeros((SPARE, LANES), F32)
    row = lax.broadcasted_iota(jnp.int32, (members, members), 0)
    column = lax.broadcasted_iota(jnp.int32, (members, members), 1)
    turned = (row == column).astype(F32)
    for b in range(NB):
        cells = owner[b] * block_cells + offsets[b, pl.ds(group, 1), :]
        distance = (centre - cells.astype(F32) / block_cells) / scale
        taper = jnp.exp(-0.5 * distance * distance)
        alpha = 0.8 * (1.0 - jnp.exp(-jnp.sum(taper, axis=1, keepdims=True) / count))
        error = errors[b]
        part = (-0.5 / count) * (taper / (error * error))
        for later in range(b + 1, NB):
            i = PAIRS.index((b, later))
            rows[ALPHA + i : ALPHA + i + 1, :] = jnp.broadcast_to(alpha[later - 1 : later], (1, LANES))
            rows[LATER + i : LATER + i + 1, :count] = part[later - 1 : later]
        rows[VALUE + b : VALUE + b + 1, :count] = values[b]
        rows[OWN + b : OWN + b + 1, :count] = part[NB - 1 : NB]
        steps[b] = turned.T
        own = alpha[NB - 1 : NB]
        turned = own * lane_take(turned, ancestors[b]) + (1.0 - own) * turned
    steps[NB] = turned.T


def turn_kernel(shape, owner, rows, ahead, *refs):
    n, slab, width, count = shape
    pieces, out, slim, held = refs[:-3], refs[-3], refs[-2], refs[-1]
    members = n * slab
    block, group = lax.axis_index("grid"), lax.axis_index("lev")
    if len(pieces) == 1:
        held[...] = pieces[0][...]
    else:
        for distance, piece in zip(GATHERED, pieces):
            held[lax.bitwise_xor(block, distance)] = piece[...]
    common = width // NB * (NB - 1)
    for i in range(width // LANES):
        value = held[:, i * slab : (i + 1) * slab, :].reshape(members, LANES).T
        out[i * LANES : (i + 1) * LANES, :] = value
        if (i + 1) * LANES <= common:
            slim[i * LANES : (i + 1) * LANES, :] = value
    for i in range(2):
        start = pl.multiple_of(common + lax.bitwise_xor(group, 2 + i) * count, count)
        slim[common + i * count : common + (i + 1) * count, :] = out[pl.ds(start, count), :]
    low = common + 2 * count
    out[width:, :] = rows[...]
    slim[low:, :] = rows[...]
    line = width // LANES * slab
    for i, (e, b) in enumerate(PAIRS):
        value = held[owner[b], line + e : line + e + 1, :]
        out[width + PARENT + i : width + PARENT + i + 1, :] = value
        slim[low + PARENT + i : low + PARENT + i + 1, :] = value


def mix_kernel(shape, steps, pull, fields, *refs):
    n, slab, depth, block_cells = shape
    outs, held = refs[:-1], refs[-1]
    members = n * slab
    held[...] = (steps[NB] + pull[0:1, :]).reshape(n, slab, members)
    block = lax.axis_index("grid")
    if len(outs) == 1:
        blend = held[...].reshape(members, members)
    else:
        blend = jnp.concatenate([held[lax.bitwise_xor(block, i)] for i in range(n)], axis=0)
    for level in range(depth):
        value = high_dot(blend, fields[:, level].reshape(members, block_cells)).reshape(n, slab, block_cells)
        if len(outs) == 1:
            outs[0][:, level] = value
        else:
            for out, part in zip(outs, PARTS):
                for i, distance in enumerate(part):
                    out[i, level] = value[distance]


def chain_kernel(shape, own, near, far, cross, steps, out):
    members, groups, count = shape
    width = groups * count
    group = lax.axis_index("lev")
    sources = [own, near, far, cross]
    bases = [NB * width, NB * width, (NB - 1) * width + 2 * count, (NB - 1) * width + 2 * count]
    columns = [source[base : base + SPARE, :].T for source, base in zip(sources, bases)]
    parents, alphas = [], []
    for source, base in zip(sources, bases):
        parents.append(source[base + PARENT : base + PARENT + 8, :].astype(jnp.int32))
        alphas.append(source[base + ALPHA : base + ALPHA + 6, :])
    tilts = {}
    pulled = []
    for b in range(NB):
        kinds = [(q, later) for q in range(groups) for later in range(b + 1, NB)] + [(0, None)]
        height = -(-len(kinds) // 8) * 8
        index = lax.broadcasted_iota(jnp.int32, (height, members), 0)
        logs = jnp.zeros((height, members), F32)
        for q in range(groups if b < NB - 1 else 1):
            start = pl.multiple_of(b * width + lax.bitwise_xor(group, q) * count, count)
            total = jnp.zeros((count, members), F32)
            tilted = jnp.zeros((count, members), F32)
            for p, source in enumerate(sources):
                if b == NB - 1 and p > 1:
                    value = source[b * width + (p - 2) * count : b * width + (p - 1) * count, :]
                else:
                    value = source[pl.ds(start, count), :]
                for e in range(b):
                    i = PAIRS.index((e, b))
                    tilted = tilted + value * tilts[e, p, b]
                    alpha = alphas[p][i : i + 1]
                    moved = lane_take(value, parents[p][i : i + 1])
                    value = alpha * moved + (1.0 - alpha) * value
                total = total + value
            if b > 0:
                total = total + jnp.sum(tilted, axis=1, keepdims=True)
            miss = columns[q][:count, VALUE + b : VALUE + b + 1] - total
            square = miss * miss
            for row, (owner_group, later) in enumerate(kinds):
                if owner_group != q:
                    continue
                at = OWN + b if later is None else LATER + PAIRS.index((b, later))
                log = jnp.sum(columns[q][:count, at : at + 1] * square, axis=0, keepdims=True)
                logs = jnp.where(index == row, log, logs)
        expo = jnp.exp(logs - jnp.max(logs, axis=1, keepdims=True))
        tilt = expo / jnp.sum(expo, axis=1, keepdims=True) - 1.0 / members
        for row, (q, later) in enumerate(kinds):
            if later is None:
                pulled.append(tilt[row : row + 1])
            else:
                tilts[b, q, later] = tilt[row : row + 1]
    pull = jnp.zeros((8, members), F32)
    for b in range(NB):
        pull = pull + high_dot(jnp.broadcast_to(pulled[b], (8, members)), steps[b])
    out[...] = pull


def final_kernel(shape, arrived, out):
    n, slab, depth, block_cells = shape
    for i in range(n):
        for level in range(depth):
            out[:, level, i * block_cells : (i + 1) * block_cells] = arrived[i, level]


def place_kernel(shape, places, skip, *refs):
    slab, depth, block_cells = shape
    pieces, out, held, done = refs[skip:-3], refs[-3], refs[-2], refs[-1]
    block = lax.axis_index("grid")
    copies = []
    for k, (i, j, distance) in enumerate(places):
        for level in range(depth):
            held[k, :, level, :] = pieces[i][j, level]
        start = pl.multiple_of(lax.bitwise_xor(block, distance) * block_cells, LANES)
        copies.append(pltpu.make_async_copy(held.at[k], out.at[:, :, pl.ds(start, block_cells)], done.at[k]))
        copies[-1].start()
    for copy in copies:
        copy.wait()


def place(shape, whole, places, pieces, before=None, moved=0):
    slab, depth, block_cells = shape
    given = [] if before is None else [before]
    return call(
        functools.partial(place_kernel, shape, places, len(given)),
        whole,
        [PLACE] * len(given) + [VMEM] * len(pieces),
        scratch=[
            pltpu.VMEM((len(places), slab, depth, block_cells), F32),
            pltpu.SemaphoreType.DMA((len(places),)),
        ],
        moved=moved,
        out_specs=PLACE,
        aliases={0: 0} if given else {},
    )(*given, *pieces)


def hop(value, distance, n):
    return lax.ppermute(value, "grid", [(j, j ^ distance) for j in range(n)])


def gather_pieces(piece, n):
    if n != 8:
        return [lax.all_to_all(jnp.broadcast_to(piece[None], (n,) + piece.shape), "grid", 0, 0, tiled=True)]
    pieces = {0: piece}
    for i in (4, 2, 6, 7, 1):
        pieces[i] = hop(piece, i, n)
    for i in (4, 2):
        pieces[i + 1] = hop(pieces[i], 1, n)
    return [pieces[i] for i in GATHERED]


def exchange_parts(parts, shape, whole, n):
    far = [parts[0]] + [hop(part, distances[0], n) for part, distances in zip(parts[1:5], PARTS[1:5])]
    near = hop(parts[5], PARTS[5][0], n)
    beside, onward = hop(parts[6], 1, n), hop(near[1:], 1, n)
    out = place(shape, whole, [(i, 0, PARTS[i][0]) for i in range(5)], far, moved=10**6)
    return place(shape, whole, [(0, 0, 2), (1, 0, 1), (2, 0, 3)], [near, beside, onward], out, moved=10**6)


def body(prior, channel_weights, obs_owner, obs_offset, obs_value, obs_error, ancestors):
    n, lev = lax.axis_size("grid"), lax.axis_size("lev")
    slab, depth, cells = prior.shape
    members = slab * n
    block_cells = cells // n
    groups = channel_weights.shape[1]
    count = obs_offset.shape[2]
    width = NB * groups * count
    scale = n / 2.0
    shape = jax.ShapeDtypeStruct
    parents = ancestors[:, 0]
    tall = width // LANES * slab + 8

    piece = call(
        functools.partial(pick_kernel, (slab, depth, block_cells, groups, count)),
        shape((tall, LANES), F32),
        [PLACE] * 5,
        scratch=[
            pltpu.SMEM(obs_owner.shape, jnp.int32),
            pltpu.VMEM(channel_weights.shape, F32),
            pltpu.VMEM(obs_offset.shape, jnp.int32),
            pltpu.VMEM(parents.shape, jnp.int32),
            pltpu.VMEM(prior.shape, F32),
            pltpu.SemaphoreType.DMA((5,)),
        ],
        moved=10**6,
        limit=None,
    )(obs_owner, channel_weights, obs_offset, parents, prior)
    pieces = gather_pieces(piece, n)
    send = call(
        functools.partial(retile_kernel, (n, slab, depth, block_cells)),
        shape((n, depth, slab, block_cells), F32),
        [VMEM],
        moved=10**6,
    )(prior)
    fields = lax.all_to_all(send, "grid", 0, 0, tiled=True)

    rows, steps = call(
        functools.partial(prep_kernel, (block_cells, count, scale, members)),
        [shape((SPARE, LANES), F32), shape((NB + 1, members, members), F32)],
        [SMEM, VMEM, VMEM, VMEM, VMEM],
        moved=10**6,
    )(obs_owner, obs_offset, obs_value, obs_error, parents)

    slim_height = (NB - 1) * groups * count + 2 * count + SPARE
    own, slim = call(
        functools.partial(turn_kernel, (n, slab, width, count)),
        [shape((width + SPARE, members), F32), shape((slim_height, members), F32)],
        [SMEM, VMEM, PLACE] + [VMEM] * len(pieces),
        scratch=[pltpu.VMEM((n, tall, LANES), F32)],
        moved=10**6,
    )(obs_owner, rows, send, *pieces)
    far = lax.ppermute(slim, "lev", [(j, j ^ 2) for j in range(lev)])
    near = lax.ppermute(own, "lev", [(j, j ^ 1) for j in range(lev)])
    cross = lax.ppermute(far, "lev", [(j, j ^ 1) for j in range(lev)])

    pull = call(
        functools.partial(chain_kernel, (members, groups, count)),
        shape((8, members), F32),
        [VMEM] * 5,
        moved=10**5,
    )(own, near, far, cross, steps)

    if n == 8:
        layout = [shape((len(part), depth, slab, block_cells), F32) for part in PARTS]
    else:
        layout = [shape((n, depth, slab, block_cells), F32)]
    send = call(
        functools.partial(mix_kernel, (n, slab, depth, block_cells)),
        layout,
        [VMEM] * 3,
        scratch=[pltpu.VMEM((n, slab, members), F32)],
        flops=10**8,
        moved=10**6,
    )(steps, pull, fields)
    whole = shape((slab, depth, cells), F32)
    if n == 8:
        return exchange_parts(send, (slab, depth, block_cells), whole, n)
    moved = lax.all_to_all(send[0], "grid", 0, 0, tiled=True)
    return call(functools.partial(final_kernel, (n, slab, depth, block_cells)), whole, [VMEM], moved=10**6)(moved)


def solution(mesh):
    in_specs = (
        P("grid", "lev", None),
        P("lev", None),
        P(),
        P(),
        P(None, "lev", None),
        P(None, "lev", None),
        P(None, "lev", "grid", None),
    )
    out_specs = P("grid", "lev", None)
    return jax.shard_map(body, mesh=mesh, in_specs=in_specs, out_specs=out_specs, check_vma=False)
```

```python
import functools

import jax
import jax.numpy as jnp
from jax import lax
from jax.experimental import pallas as pl
from jax.experimental.pallas import tpu as pltpu
from jax.sharding import PartitionSpec as P

NB = 4
HIGH = lax.Precision.HIGHEST
LANES = 128
F32 = jnp.float32
VMEM = pl.BlockSpec(memory_space=pltpu.VMEM)
SMEM = pl.BlockSpec(memory_space=pltpu.SMEM)
PLACE = pl.BlockSpec(memory_space=pl.ANY)
LIMIT = 48 * 1024 * 1024

PARTS = ((0,), (4,), (5,), (6,), (7,), (2, 3), (1,))
PAIRS = [(e, b) for b in range(1, NB) for e in range(b)]
PARENT, ALPHA, LATER, VALUE, OWN, SPARE = 0, 6, 12, 18, 22, 32


def call(kernel, out_shapes, in_specs, scratch=(), flops=0, moved=0, limit=LIMIT, out_specs=None, aliases={}):
    many = isinstance(out_shapes, (list, tuple))
    return pl.pallas_call(
        kernel,
        out_shape=out_shapes,
        in_specs=in_specs,
        out_specs=out_specs or ([VMEM] * len(out_shapes) if many else VMEM),
        input_output_aliases=aliases,
        scratch_shapes=list(scratch),
        compiler_params=pltpu.CompilerParams(vmem_limit_bytes=limit),
        cost_estimate=pl.CostEstimate(flops=flops, bytes_accessed=moved, transcendentals=0),
    )


def high_dot(a, b):
    return lax.dot_general(a, b, (((1,), (0,)), ((), ())), precision=HIGH, preferred_element_type=F32)


def lane_take(value, row):
    where = jnp.broadcast_to(row, value.shape)
    return jnp.take_along_axis(value, where, axis=1, mode="promise_in_bounds")


def pick_kernel(shape, *refs):
    slab, depth, block_cells, groups, count = shape
    out, arrivals = refs[5], refs[11]
    copies = [pltpu.make_async_copy(refs[i], refs[6 + i], arrivals.at[i]) for i in range(5)]
    for copy in copies:
        copy.start()
    for copy in copies:
        copy.wait()
    owner, weights, offsets, ancestors, prior = refs[6:11]
    width = groups * count
    per = LANES // count
    blocks = width // LANES
    level_of = lax.broadcasted_iota(jnp.int32, (slab, depth, LANES), 1)
    gains = []
    for c in range(blocks):
        gain = jnp.zeros((slab, depth, LANES), F32)
        for level in range(depth):
            row = jnp.concatenate(
                [
                    jnp.broadcast_to(weights[level : level + 1, g : g + 1], (1, count))
                    for g in range(c * per, (c + 1) * per)
                ],
                axis=1,
            )
            gain = jnp.where(level_of == level, row[None], gain)
        gains.append(gain.reshape(slab * depth, LANES))
    for b in range(NB):
        start = pl.multiple_of(owner[b] * block_cells, LANES)
        both = prior[:, :, pl.ds(start, block_cells)].reshape(slab * depth, block_cells)
        for c in range(blocks):
            cell = jnp.concatenate([offsets[b, g : g + 1, :] for g in range(c * per, (c + 1) * per)], axis=1)
            low, high = lax.rem(cell, LANES), lax.div(cell, LANES)
            found = jnp.zeros((slab * depth, LANES), F32)
            for h in range(block_cells // LANES):
                part = lane_take(both[:, h * LANES : (h + 1) * LANES], low)
                found = jnp.where(high == h, part, found)
            line = (b * blocks + c) * slab
            out[line : line + slab, :] = jnp.sum((found * gains[c]).reshape(slab, depth, LANES), axis=1)
    line = NB * width // LANES * slab
    out[line:, :] = jnp.zeros((out.shape[0] - line, LANES), F32)
    for b in range(NB):
        out[line + b : line + b + 1, :] = ancestors[b].astype(F32)


def retile_kernel(shape, source, out, prior, arrived):
    n, slab, depth, block_cells = shape
    copy = pltpu.make_async_copy(source, prior, arrived)
    copy.start()
    copy.wait()
    for i in range(n):
        for level in range(depth):
            out[i, level] = prior[:, level, i * block_cells : (i + 1) * block_cells]


def prep_kernel(shape, owner, offsets, values, errors, ancestors, rows, steps):
    block_cells, count, scale, members = shape
    block, group = lax.axis_index("grid"), lax.axis_index("lev")
    index = lax.broadcasted_iota(jnp.int32, (8, 1), 0)
    region = jnp.full((8, 1), block, jnp.int32)
    for b in range(1, NB):
        region = jnp.where(index == b - 1, owner[b], region)
    centre = region.astype(F32) + 0.5
    rows[...] = jnp.zeros((SPARE, LANES), F32)
    row = lax.broadcasted_iota(jnp.int32, (members, members), 0)
    column = lax.broadcasted_iota(jnp.int32, (members, members), 1)
    turned = (row == column).astype(F32)
    for b in range(NB):
        cells = owner[b] * block_cells + offsets[b, pl.ds(group, 1), :]
        distance = (centre - cells.astype(F32) / block_cells) / scale
        taper = jnp.exp(-0.5 * distance * distance)
        alpha = 0.8 * (1.0 - jnp.exp(-jnp.sum(taper, axis=1, keepdims=True) / count))
        error = errors[b]
        part = (-0.5 / count) * (taper / (error * error))
        for later in range(b + 1, NB):
            i = PAIRS.index((b, later))
            rows[ALPHA + i : ALPHA + i + 1, :] = jnp.broadcast_to(alpha[later - 1 : later], (1, LANES))
            rows[LATER + i : LATER + i + 1, :count] = part[later - 1 : later]
        rows[VALUE + b : VALUE + b + 1, :count] = values[b]
        rows[OWN + b : OWN + b + 1, :count] = part[NB - 1 : NB]
        steps[b] = turned.T
        own = alpha[NB - 1 : NB]
        turned = own * lane_take(turned, ancestors[b]) + (1.0 - own) * turned
    steps[NB] = turned.T


def turn_kernel(shape, owner, rows, ahead, *refs):
    n, slab, width, count = shape
    pieces, out, slim, held = refs[:-3], refs[-3], refs[-2], refs[-1]
    members = n * slab
    block, group = lax.axis_index("grid"), lax.axis_index("lev")
    if len(pieces) == 1:
        held[...] = pieces[0][...]
    else:
        for i, piece in enumerate(pieces):
            held[lax.bitwise_xor(block, i)] = piece[...]
    common = width // NB * (NB - 1)
    for i in range(width // LANES):
        value = held[:, i * slab : (i + 1) * slab, :].reshape(members, LANES).T
        out[i * LANES : (i + 1) * LANES, :] = value
        if (i + 1) * LANES <= common:
            slim[i * LANES : (i + 1) * LANES, :] = value
    for i in range(2):
        start = pl.multiple_of(common + lax.bitwise_xor(group, 2 + i) * count, count)
        slim[common + i * count : common + (i + 1) * count, :] = out[pl.ds(start, count), :]
    low = common + 2 * count
    out[width:, :] = rows[...]
    slim[low:, :] = rows[...]
    line = width // LANES * slab
    for i, (e, b) in enumerate(PAIRS):
        value = held[owner[b], line + e : line + e + 1, :]
        out[width + PARENT + i : width + PARENT + i + 1, :] = value
        slim[low + PARENT + i : low + PARENT + i + 1, :] = value


def mix_kernel(shape, steps, pull, fields, *refs):
    n, slab, depth, block_cells = shape
    outs, held = refs[:-1], refs[-1]
    members = n * slab
    held[...] = (steps[NB] + pull[0:1, :]).reshape(n, slab, members)
    block = lax.axis_index("grid")
    if len(outs) == 1:
        blend = held[...].reshape(members, members)
    else:
        blend = jnp.concatenate([held[lax.bitwise_xor(block, i)] for i in range(n)], axis=0)
    for level in range(depth):
        value = high_dot(blend, fields[:, level].reshape(members, block_cells)).reshape(n, slab, block_cells)
        if len(outs) == 1:
            outs[0][:, level] = value
        else:
            for out, part in zip(outs, PARTS):
                for i, distance in enumerate(part):
                    out[i, level] = value[distance]


def chain_kernel(shape, own, near, far, cross, steps, out):
    members, groups, count = shape
    width = groups * count
    group = lax.axis_index("lev")
    sources = [own, near, far, cross]
    bases = [NB * width, NB * width, (NB - 1) * width + 2 * count, (NB - 1) * width + 2 * count]
    columns = [source[base : base + SPARE, :].T for source, base in zip(sources, bases)]
    parents, alphas = [], []
    for source, base in zip(sources, bases):
        parents.append(source[base + PARENT : base + PARENT + 8, :].astype(jnp.int32))
        alphas.append(source[base + ALPHA : base + ALPHA + 6, :])
    tilts = {}
    pulled = []
    for b in range(NB):
        kinds = [(q, later) for q in range(groups) for later in range(b + 1, NB)] + [(0, None)]
        height = -(-len(kinds) // 8) * 8
        index = lax.broadcasted_iota(jnp.int32, (height, members), 0)
        logs = jnp.zeros((height, members), F32)
        for q in range(groups if b < NB - 1 else 1):
            start = pl.multiple_of(b * width + lax.bitwise_xor(group, q) * count, count)
            total = jnp.zeros((count, members), F32)
            tilted = jnp.zeros((count, members), F32)
            for p, source in enumerate(sources):
                if b == NB - 1 and p > 1:
                    value = source[b * width + (p - 2) * count : b * width + (p - 1) * count, :]
                else:
                    value = source[pl.ds(start, count), :]
                for e in range(b):
                    i = PAIRS.index((e, b))
                    tilted = tilted + value * tilts[e, p, b]
                    alpha = alphas[p][i : i + 1]
                    moved = lane_take(value, parents[p][i : i + 1])
                    value = alpha * moved + (1.0 - alpha) * value
                total = total + value
            if b > 0:
                total = total + jnp.sum(tilted, axis=1, keepdims=True)
            miss = columns[q][:count, VALUE + b : VALUE + b + 1] - total
            square = miss * miss
            for row, (owner_group, later) in enumerate(kinds):
                if owner_group != q:
                    continue
                at = OWN + b if later is None else LATER + PAIRS.index((b, later))
                log = jnp.sum(columns[q][:count, at : at + 1] * square, axis=0, keepdims=True)
                logs = jnp.where(index == row, log, logs)
        expo = jnp.exp(logs - jnp.max(logs, axis=1, keepdims=True))
        tilt = expo / jnp.sum(expo, axis=1, keepdims=True) - 1.0 / members
        for row, (q, later) in enumerate(kinds):
            if later is None:
                pulled.append(tilt[row : row + 1])
            else:
                tilts[b, q, later] = tilt[row : row + 1]
    pull = jnp.zeros((8, members), F32)
    for b in range(NB):
        pull = pull + high_dot(jnp.broadcast_to(pulled[b], (8, members)), steps[b])
    out[...] = pull


def final_kernel(shape, arrived, out):
    n, slab, depth, block_cells = shape
    for i in range(n):
        for level in range(depth):
            out[:, level, i * block_cells : (i + 1) * block_cells] = arrived[i, level]


def place_kernel(shape, places, skip, *refs):
    slab, depth, block_cells = shape
    pieces, out, held, done = refs[skip:-3], refs[-3], refs[-2], refs[-1]
    block = lax.axis_index("grid")
    copies = []
    for k, (i, j, distance) in enumerate(places):
        for level in range(depth):
            held[k, :, level, :] = pieces[i][j, level]
        start = pl.multiple_of(lax.bitwise_xor(block, distance) * block_cells, LANES)
        copies.append(pltpu.make_async_copy(held.at[k], out.at[:, :, pl.ds(start, block_cells)], done.at[k]))
        copies[-1].start()
    for copy in copies:
        copy.wait()


def place(shape, whole, places, pieces, before=None, moved=0):
    slab, depth, block_cells = shape
    given = [] if before is None else [before]
    return call(
        functools.partial(place_kernel, shape, places, len(given)),
        whole,
        [PLACE] * len(given) + [VMEM] * len(pieces),
        scratch=[
            pltpu.VMEM((len(places), slab, depth, block_cells), F32),
            pltpu.SemaphoreType.DMA((len(places),)),
        ],
        moved=moved,
        out_specs=PLACE,
        aliases={0: 0} if given else {},
    )(*given, *pieces)


def hop(value, distance, n):
    return lax.ppermute(value, "grid", [(j, j ^ distance) for j in range(n)])


def gather_pieces(piece, n):
    if n != 8:
        return [lax.all_to_all(jnp.broadcast_to(piece[None], (n,) + piece.shape), "grid", 0, 0, tiled=True)]
    pieces = {0: piece}
    for i in (4, 2, 6, 7, 1):
        pieces[i] = hop(piece, i, n)
    for i in (4, 2):
        pieces[i + 1] = hop(pieces[i], 1, n)
    return [pieces[i] for i in range(n)]


def exchange_parts(parts, shape, whole, n):
    far = [parts[0]] + [hop(part, distances[0], n) for part, distances in zip(parts[1:5], PARTS[1:5])]
    near = hop(parts[5], PARTS[5][0], n)
    beside, onward = hop(parts[6], 1, n), hop(near[1:], 1, n)
    out = place(shape, whole, [(i, 0, PARTS[i][0]) for i in range(5)], far, moved=10**6)
    return place(shape, whole, [(0, 0, 2), (1, 0, 1), (2, 0, 3)], [near, beside, onward], out, moved=10**6)


def body(prior, channel_weights, obs_owner, obs_offset, obs_value, obs_error, ancestors):
    n, lev = lax.axis_size("grid"), lax.axis_size("lev")
    slab, depth, cells = prior.shape
    members = slab * n
    block_cells = cells // n
    groups = channel_weights.shape[1]
    count = obs_offset.shape[2]
    width = NB * groups * count
    scale = n / 2.0
    shape = jax.ShapeDtypeStruct
    parents = ancestors[:, 0]
    tall = width // LANES * slab + 8

    piece = call(
        functools.partial(pick_kernel, (slab, depth, block_cells, groups, count)),
        shape((tall, LANES), F32),
        [PLACE] * 5,
        scratch=[
            pltpu.SMEM(obs_owner.shape, jnp.int32),
            pltpu.VMEM(channel_weights.shape, F32),
            pltpu.VMEM(obs_offset.shape, jnp.int32),
            pltpu.VMEM(parents.shape, jnp.int32),
            pltpu.VMEM(prior.shape, F32),
            pltpu.SemaphoreType.DMA((5,)),
        ],
        moved=10**6,
        limit=None,
    )(obs_owner, channel_weights, obs_offset, parents, prior)
    pieces = gather_pieces(piece, n)
    send = call(
        functools.partial(retile_kernel, (n, slab, depth, block_cells)),
        shape((n, depth, slab, block_cells), F32),
        [PLACE],
        scratch=[pltpu.VMEM(prior.shape, F32), pltpu.SemaphoreType.DMA],
        moved=10**6,
        limit=None,
    )(prior)
    fields = lax.all_to_all(send, "grid", 0, 0, tiled=True)

    rows, steps = call(
        functools.partial(prep_kernel, (block_cells, count, scale, members)),
        [shape((SPARE, LANES), F32), shape((NB + 1, members, members), F32)],
        [SMEM, VMEM, VMEM, VMEM, VMEM],
        moved=10**6,
    )(obs_owner, obs_offset, obs_value, obs_error, parents)

    slim_height = (NB - 1) * groups * count + 2 * count + SPARE
    own, slim = call(
        functools.partial(turn_kernel, (n, slab, width, count)),
        [shape((width + SPARE, members), F32), shape((slim_height, members), F32)],
        [SMEM, VMEM, PLACE] + [VMEM] * len(pieces),
        scratch=[pltpu.VMEM((n, tall, LANES), F32)],
        moved=10**6,
    )(obs_owner, rows, send, *pieces)
    far = lax.ppermute(slim, "lev", [(j, j ^ 2) for j in range(lev)])
    near = lax.ppermute(own, "lev", [(j, j ^ 1) for j in range(lev)])
    cross = lax.ppermute(far, "lev", [(j, j ^ 1) for j in range(lev)])

    pull = call(
        functools.partial(chain_kernel, (members, groups, count)),
        shape((8, members), F32),
        [VMEM] * 5,
        moved=10**5,
    )(own, near, far, cross, steps)

    if n == 8:
        layout = [shape((len(part), depth, slab, block_cells), F32) for part in PARTS]
    else:
        layout = [shape((n, depth, slab, block_cells), F32)]
    send = call(
        functools.partial(mix_kernel, (n, slab, depth, block_cells)),
        layout,
        [VMEM] * 3,
        scratch=[pltpu.VMEM((n, slab, members), F32)],
        flops=10**8,
        moved=10**6,
    )(steps, pull, fields)
    whole = shape((slab, depth, cells), F32)
    if n == 8:
        return exchange_parts(send, (slab, depth, block_cells), whole, n)
    moved = lax.all_to_all(send[0], "grid", 0, 0, tiled=True)
    return call(functools.partial(final_kernel, (n, slab, depth, block_cells)), whole, [VMEM], moved=10**6)(moved)


def solution(mesh):
    in_specs = (
        P("grid", "lev", None),
        P("lev", None),
        P(),
        P(),
        P(None, "lev", None),
        P(None, "lev", None),
        P(None, "lev", "grid", None),
    )
    out_specs = P("grid", "lev", None)
    return jax.shard_map(body, mesh=mesh, in_specs=in_specs, out_specs=out_specs, check_vma=False)
```

```python
import functools

import jax
import jax.numpy as jnp
from jax import lax
from jax.experimental import pallas as pl
from jax.experimental.pallas import tpu as pltpu
from jax.sharding import PartitionSpec as P

NB = 4
HIGH = lax.Precision.HIGHEST
LANES = 128
F32 = jnp.float32
VMEM = pl.BlockSpec(memory_space=pltpu.VMEM)
SMEM = pl.BlockSpec(memory_space=pltpu.SMEM)
PLACE = pl.BlockSpec(memory_space=pl.ANY)
LIMIT = 48 * 1024 * 1024

PARTS = ((0,), (4,), (5,), (6,), (7,), (2, 3), (1,))
PAIRS = [(e, b) for b in range(1, NB) for e in range(b)]
PARENT, ALPHA, LATER, VALUE, OWN, SPARE = 0, 6, 12, 18, 22, 32


def call(kernel, out_shapes, in_specs, scratch=(), flops=0, moved=0, limit=LIMIT, out_specs=None, aliases={}):
    many = isinstance(out_shapes, (list, tuple))
    return pl.pallas_call(
        kernel,
        out_shape=out_shapes,
        in_specs=in_specs,
        out_specs=out_specs or ([VMEM] * len(out_shapes) if many else VMEM),
        input_output_aliases=aliases,
        scratch_shapes=list(scratch),
        compiler_params=pltpu.CompilerParams(vmem_limit_bytes=limit),
        cost_estimate=pl.CostEstimate(flops=flops, bytes_accessed=moved, transcendentals=0),
    )


def high_dot(a, b):
    return lax.dot_general(a, b, (((1,), (0,)), ((), ())), precision=HIGH, preferred_element_type=F32)


def lane_take(value, row):
    where = jnp.broadcast_to(row, value.shape)
    return jnp.take_along_axis(value, where, axis=1, mode="promise_in_bounds")


def pick_kernel(shape, *refs):
    slab, depth, block_cells, groups, count = shape
    out, arrivals = refs[5], refs[11]
    copies = [pltpu.make_async_copy(refs[i], refs[6 + i], arrivals.at[i]) for i in range(5)]
    for copy in copies:
        copy.start()
    for copy in copies:
        copy.wait()
    owner, weights, offsets, ancestors, prior = refs[6:11]
    width = groups * count
    per = LANES // count
    blocks = width // LANES
    level_of = lax.broadcasted_iota(jnp.int32, (slab, depth, LANES), 1)
    gains = []
    for c in range(blocks):
        gain = jnp.zeros((slab, depth, LANES), F32)
        for level in range(depth):
            row = jnp.concatenate(
                [
                    jnp.broadcast_to(weights[level : level + 1, g : g + 1], (1, count))
                    for g in range(c * per, (c + 1) * per)
                ],
                axis=1,
            )
            gain = jnp.where(level_of == level, row[None], gain)
        gains.append(gain.reshape(slab * depth, LANES))
    for b in range(NB):
        start = pl.multiple_of(owner[b] * block_cells, LANES)
        both = prior[:, :, pl.ds(start, block_cells)].reshape(slab * depth, block_cells)
        for c in range(blocks):
            cell = jnp.concatenate([offsets[b, g : g + 1, :] for g in range(c * per, (c + 1) * per)], axis=1)
            low, high = lax.rem(cell, LANES), lax.div(cell, LANES)
            found = jnp.zeros((slab * depth, LANES), F32)
            for h in range(block_cells // LANES):
                part = lane_take(both[:, h * LANES : (h + 1) * LANES], low)
                found = jnp.where(high == h, part, found)
            line = (b * blocks + c) * slab
            out[line : line + slab, :] = jnp.sum((found * gains[c]).reshape(slab, depth, LANES), axis=1)
    line = NB * width // LANES * slab
    out[line:, :] = jnp.zeros((out.shape[0] - line, LANES), F32)
    for b in range(NB):
        out[line + b : line + b + 1, :] = ancestors[b].astype(F32)


def retile_kernel(shape, prior, out):
    n, slab, depth, block_cells = shape
    for i in range(n):
        for level in range(depth):
            out[i, level] = prior[:, level, i * block_cells : (i + 1) * block_cells]


def prep_kernel(shape, owner, offsets, values, errors, ancestors, rows, steps):
    block_cells, count, scale, members = shape
    block, group = lax.axis_index("grid"), lax.axis_index("lev")
    index = lax.broadcasted_iota(jnp.int32, (8, 1), 0)
    region = jnp.full((8, 1), block, jnp.int32)
    for b in range(1, NB):
        region = jnp.where(index == b - 1, owner[b], region)
    centre = region.astype(F32) + 0.5
    rows[...] = jnp.zeros((SPARE, LANES), F32)
    row = lax.broadcasted_iota(jnp.int32, (members, members), 0)
    column = lax.broadcasted_iota(jnp.int32, (members, members), 1)
    turned = (row == column).astype(F32)
    for b in range(NB):
        cells = owner[b] * block_cells + offsets[b, pl.ds(group, 1), :]
        distance = (centre - cells.astype(F32) / block_cells) / scale
        taper = jnp.exp(-0.5 * distance * distance)
        alpha = 0.8 * (1.0 - jnp.exp(-jnp.sum(taper, axis=1, keepdims=True) / count))
        error = errors[b]
        part = (-0.5 / count) * (taper / (error * error))
        for later in range(b + 1, NB):
            i = PAIRS.index((b, later))
            rows[ALPHA + i : ALPHA + i + 1, :] = jnp.broadcast_to(alpha[later - 1 : later], (1, LANES))
            rows[LATER + i : LATER + i + 1, :count] = part[later - 1 : later]
        rows[VALUE + b : VALUE + b + 1, :count] = values[b]
        rows[OWN + b : OWN + b + 1, :count] = part[NB - 1 : NB]
        steps[b] = turned.T
        own = alpha[NB - 1 : NB]
        turned = own * lane_take(turned, ancestors[b]) + (1.0 - own) * turned
    steps[NB] = turned.T


def turn_kernel(shape, owner, rows, ahead, *refs):
    n, slab, width, count = shape
    pieces, out, slim, held = refs[:-3], refs[-3], refs[-2], refs[-1]
    members = n * slab
    block, group = lax.axis_index("grid"), lax.axis_index("lev")
    if len(pieces) == 1:
        held[...] = pieces[0][...]
    else:
        for i, piece in enumerate(pieces):
            held[lax.bitwise_xor(block, i)] = piece[...]
    common = width // NB * (NB - 1)
    for i in range(width // LANES):
        value = held[:, i * slab : (i + 1) * slab, :].reshape(members, LANES).T
        out[i * LANES : (i + 1) * LANES, :] = value
        if (i + 1) * LANES <= common:
            slim[i * LANES : (i + 1) * LANES, :] = value
    for i in range(2):
        start = pl.multiple_of(common + lax.bitwise_xor(group, 2 + i) * count, count)
        slim[common + i * count : common + (i + 1) * count, :] = out[pl.ds(start, count), :]
    low = common + 2 * count
    out[width:, :] = rows[...]
    slim[low:, :] = rows[...]
    line = width // LANES * slab
    for i, (e, b) in enumerate(PAIRS):
        value = held[owner[b], line + e : line + e + 1, :]
        out[width + PARENT + i : width + PARENT + i + 1, :] = value
        slim[low + PARENT + i : low + PARENT + i + 1, :] = value


def mix_kernel(shape, steps, pull, fields, *refs):
    n, slab, depth, block_cells = shape
    outs, held = refs[:-1], refs[-1]
    members = n * slab
    held[...] = (steps[NB] + pull[0:1, :]).reshape(n, slab, members)
    block = lax.axis_index("grid")
    if len(outs) == 1:
        blend = held[...].reshape(members, members)
    else:
        blend = jnp.concatenate([held[lax.bitwise_xor(block, i)] for i in range(n)], axis=0)
    for level in range(depth):
        value = high_dot(blend, fields[:, level].reshape(members, block_cells)).reshape(n, slab, block_cells)
        if len(outs) == 1:
            outs[0][:, level] = value
        else:
            for out, part in zip(outs, PARTS):
                for i, distance in enumerate(part):
                    out[i, level] = value[distance]


def chain_kernel(shape, own, near, far, cross, steps, out):
    members, groups, count = shape
    width = groups * count
    group = lax.axis_index("lev")
    sources = [own, near, far, cross]
    bases = [NB * width, NB * width, (NB - 1) * width + 2 * count, (NB - 1) * width + 2 * count]
    columns = [source[base : base + SPARE, :].T for source, base in zip(sources, bases)]
    parents, alphas = [], []
    for source, base in zip(sources, bases):
        parents.append(source[base + PARENT : base + PARENT + 8, :].astype(jnp.int32))
        alphas.append(source[base + ALPHA : base + ALPHA + 6, :])
    tilts = {}
    pulled = []
    for b in range(NB):
        kinds = [(q, later) for q in range(groups) for later in range(b + 1, NB)] + [(0, None)]
        height = -(-len(kinds) // 8) * 8
        index = lax.broadcasted_iota(jnp.int32, (height, members), 0)
        logs = jnp.zeros((height, members), F32)
        for q in range(groups if b < NB - 1 else 1):
            start = pl.multiple_of(b * width + lax.bitwise_xor(group, q) * count, count)
            total = jnp.zeros((count, members), F32)
            tilted = jnp.zeros((count, members), F32)
            for p, source in enumerate(sources):
                if b == NB - 1 and p > 1:
                    value = source[b * width + (p - 2) * count : b * width + (p - 1) * count, :]
                else:
                    value = source[pl.ds(start, count), :]
                for e in range(b):
                    i = PAIRS.index((e, b))
                    tilted = tilted + value * tilts[e, p, b]
                    alpha = alphas[p][i : i + 1]
                    moved = lane_take(value, parents[p][i : i + 1])
                    value = alpha * moved + (1.0 - alpha) * value
                total = total + value
            if b > 0:
                total = total + jnp.sum(tilted, axis=1, keepdims=True)
            miss = columns[q][:count, VALUE + b : VALUE + b + 1] - total
            square = miss * miss
            for row, (owner_group, later) in enumerate(kinds):
                if owner_group != q:
                    continue
                at = OWN + b if later is None else LATER + PAIRS.index((b, later))
                log = jnp.sum(columns[q][:count, at : at + 1] * square, axis=0, keepdims=True)
                logs = jnp.where(index == row, log, logs)
        expo = jnp.exp(logs - jnp.max(logs, axis=1, keepdims=True))
        tilt = expo / jnp.sum(expo, axis=1, keepdims=True) - 1.0 / members
        for row, (q, later) in enumerate(kinds):
            if later is None:
                pulled.append(tilt[row : row + 1])
            else:
                tilts[b, q, later] = tilt[row : row + 1]
    pull = jnp.zeros((8, members), F32)
    for b in range(NB):
        pull = pull + high_dot(jnp.broadcast_to(pulled[b], (8, members)), steps[b])
    out[...] = pull


def final_kernel(shape, arrived, out):
    n, slab, depth, block_cells = shape
    for i in range(n):
        for level in range(depth):
            out[:, level, i * block_cells : (i + 1) * block_cells] = arrived[i, level]


def place_kernel(shape, places, skip, *refs):
    slab, depth, block_cells = shape
    pieces, out, held, done = refs[skip:-3], refs[-3], refs[-2], refs[-1]
    block = lax.axis_index("grid")
    copies = []
    for k, (i, j, distance) in enumerate(places):
        for level in range(depth):
            held[k, :, level, :] = pieces[i][j, level]
        start = pl.multiple_of(lax.bitwise_xor(block, distance) * block_cells, LANES)
        copies.append(pltpu.make_async_copy(held.at[k], out.at[:, :, pl.ds(start, block_cells)], done.at[k]))
        copies[-1].start()
    for copy in copies:
        copy.wait()


def place(shape, whole, places, pieces, before=None, moved=0):
    slab, depth, block_cells = shape
    given = [] if before is None else [before]
    return call(
        functools.partial(place_kernel, shape, places, len(given)),
        whole,
        [PLACE] * len(given) + [VMEM] * len(pieces),
        scratch=[
            pltpu.VMEM((len(places), slab, depth, block_cells), F32),
            pltpu.SemaphoreType.DMA((len(places),)),
        ],
        moved=moved,
        out_specs=PLACE,
        aliases={0: 0} if given else {},
    )(*given, *pieces)


def hop(value, distance, n):
    return lax.ppermute(value, "grid", [(j, j ^ distance) for j in range(n)])


def gather_pieces(piece, n):
    if n != 8:
        return [lax.all_to_all(jnp.broadcast_to(piece[None], (n,) + piece.shape), "grid", 0, 0, tiled=True)]
    pieces = {0: piece}
    for i in (4, 2, 6, 7, 1):
        pieces[i] = hop(piece, i, n)
    for i in (4, 2):
        pieces[i + 1] = hop(pieces[i], 1, n)
    return [pieces[i] for i in range(n)]


def exchange_parts(parts, shape, whole, n):
    far = [parts[0]] + [hop(part, distances[0], n) for part, distances in zip(parts[1:5], PARTS[1:5])]
    near = hop(parts[5], PARTS[5][0], n)
    beside, onward = hop(parts[6], 1, n), hop(near[1:], 1, n)
    out = place(shape, whole, [(i, 0, PARTS[i][0]) for i in range(6)], far + [near], moved=10**6)
    return place(shape, whole, [(0, 0, 1), (1, 0, 3)], [beside, onward], out, moved=10**6)


def body(prior, channel_weights, obs_owner, obs_offset, obs_value, obs_error, ancestors):
    n, lev = lax.axis_size("grid"), lax.axis_size("lev")
    slab, depth, cells = prior.shape
    members = slab * n
    block_cells = cells // n
    groups = channel_weights.shape[1]
    count = obs_offset.shape[2]
    width = NB * groups * count
    scale = n / 2.0
    shape = jax.ShapeDtypeStruct
    parents = ancestors[:, 0]
    tall = width // LANES * slab + 8

    piece = call(
        functools.partial(pick_kernel, (slab, depth, block_cells, groups, count)),
        shape((tall, LANES), F32),
        [PLACE] * 5,
        scratch=[
            pltpu.SMEM(obs_owner.shape, jnp.int32),
            pltpu.VMEM(channel_weights.shape, F32),
            pltpu.VMEM(obs_offset.shape, jnp.int32),
            pltpu.VMEM(parents.shape, jnp.int32),
            pltpu.VMEM(prior.shape, F32),
            pltpu.SemaphoreType.DMA((5,)),
        ],
        moved=10**6,
        limit=None,
    )(obs_owner, channel_weights, obs_offset, parents, prior)
    pieces = gather_pieces(piece, n)
    send = call(
        functools.partial(retile_kernel, (n, slab, depth, block_cells)),
        shape((n, depth, slab, block_cells), F32),
        [VMEM],
        moved=10**6,
    )(prior)
    fields = lax.all_to_all(send, "grid", 0, 0, tiled=True)

    rows, steps = call(
        functools.partial(prep_kernel, (block_cells, count, scale, members)),
        [shape((SPARE, LANES), F32), shape((NB + 1, members, members), F32)],
        [SMEM, VMEM, VMEM, VMEM, VMEM],
        moved=10**6,
    )(obs_owner, obs_offset, obs_value, obs_error, parents)

    slim_height = (NB - 1) * groups * count + 2 * count + SPARE
    own, slim = call(
        functools.partial(turn_kernel, (n, slab, width, count)),
        [shape((width + SPARE, members), F32), shape((slim_height, members), F32)],
        [SMEM, VMEM, PLACE] + [VMEM] * len(pieces),
        scratch=[pltpu.VMEM((n, tall, LANES), F32)],
        moved=10**6,
    )(obs_owner, rows, send, *pieces)
    far = lax.ppermute(slim, "lev", [(j, j ^ 2) for j in range(lev)])
    near = lax.ppermute(own, "lev", [(j, j ^ 1) for j in range(lev)])
    cross = lax.ppermute(far, "lev", [(j, j ^ 1) for j in range(lev)])

    pull = call(
        functools.partial(chain_kernel, (members, groups, count)),
        shape((8, members), F32),
        [VMEM] * 5,
        moved=10**5,
    )(own, near, far, cross, steps)

    if n == 8:
        layout = [shape((len(part), depth, slab, block_cells), F32) for part in PARTS]
    else:
        layout = [shape((n, depth, slab, block_cells), F32)]
    send = call(
        functools.partial(mix_kernel, (n, slab, depth, block_cells)),
        layout,
        [VMEM] * 3,
        scratch=[pltpu.VMEM((n, slab, members), F32)],
        flops=10**8,
        moved=10**6,
    )(steps, pull, fields)
    whole = shape((slab, depth, cells), F32)
    if n == 8:
        return exchange_parts(send, (slab, depth, block_cells), whole, n)
    moved = lax.all_to_all(send[0], "grid", 0, 0, tiled=True)
    return call(functools.partial(final_kernel, (n, slab, depth, block_cells)), whole, [VMEM], moved=10**6)(moved)


def solution(mesh):
    in_specs = (
        P("grid", "lev", None),
        P("lev", None),
        P(),
        P(),
        P(None, "lev", None),
        P(None, "lev", None),
        P(None, "lev", "grid", None),
    )
    out_specs = P("grid", "lev", None)
    return jax.shard_map(body, mesh=mesh, in_specs=in_specs, out_specs=out_specs, check_vma=False)
```

```python
import functools

import jax
import jax.numpy as jnp
from jax import lax
from jax.experimental import pallas as pl
from jax.experimental.pallas import tpu as pltpu
from jax.sharding import PartitionSpec as P

NB = 4
HIGH = lax.Precision.HIGHEST
LANES = 128
F32 = jnp.float32
VMEM = pl.BlockSpec(memory_space=pltpu.VMEM)
SMEM = pl.BlockSpec(memory_space=pltpu.SMEM)
PLACE = pl.BlockSpec(memory_space=pl.ANY)
LIMIT = 48 * 1024 * 1024

PARTS = ((0,), (4,), (5,), (6,), (7,), (2, 3), (1,))
PAIRS = [(e, b) for b in range(1, NB) for e in range(b)]
PARENT, ALPHA, LATER, VALUE, OWN, SPARE = 0, 6, 12, 18, 22, 32


def call(kernel, out_shapes, in_specs, scratch=(), flops=0, moved=0, limit=LIMIT, out_specs=None, aliases={}):
    many = isinstance(out_shapes, (list, tuple))
    return pl.pallas_call(
        kernel,
        out_shape=out_shapes,
        in_specs=in_specs,
        out_specs=out_specs or ([VMEM] * len(out_shapes) if many else VMEM),
        input_output_aliases=aliases,
        scratch_shapes=list(scratch),
        compiler_params=pltpu.CompilerParams(vmem_limit_bytes=limit),
        cost_estimate=pl.CostEstimate(flops=flops, bytes_accessed=moved, transcendentals=0),
    )


def high_dot(a, b):
    return lax.dot_general(a, b, (((1,), (0,)), ((), ())), precision=HIGH, preferred_element_type=F32)


def lane_take(value, row):
    where = jnp.broadcast_to(row, value.shape)
    return jnp.take_along_axis(value, where, axis=1, mode="promise_in_bounds")


def pick_kernel(shape, *refs):
    slab, depth, block_cells, groups, count = shape
    out, arrivals = refs[5], refs[11]
    copies = [pltpu.make_async_copy(refs[i], refs[6 + i], arrivals.at[i]) for i in range(5)]
    for copy in copies:
        copy.start()
    for copy in copies:
        copy.wait()
    owner, weights, offsets, ancestors, prior = refs[6:11]
    width = groups * count
    per = LANES // count
    blocks = width // LANES
    level_of = lax.broadcasted_iota(jnp.int32, (slab, depth, LANES), 1)
    gains = []
    for c in range(blocks):
        gain = jnp.zeros((slab, depth, LANES), F32)
        for level in range(depth):
            row = jnp.concatenate(
                [
                    jnp.broadcast_to(weights[level : level + 1, g : g + 1], (1, count))
                    for g in range(c * per, (c + 1) * per)
                ],
                axis=1,
            )
            gain = jnp.where(level_of == level, row[None], gain)
        gains.append(gain.reshape(slab * depth, LANES))
    for b in range(NB):
        start = pl.multiple_of(owner[b] * block_cells, LANES)
        both = prior[:, :, pl.ds(start, block_cells)].reshape(slab * depth, block_cells)
        for c in range(blocks):
            cell = jnp.concatenate([offsets[b, g : g + 1, :] for g in range(c * per, (c + 1) * per)], axis=1)
            low, high = lax.rem(cell, LANES), lax.div(cell, LANES)
            found = jnp.zeros((slab * depth, LANES), F32)
            for h in range(block_cells // LANES):
                part = lane_take(both[:, h * LANES : (h + 1) * LANES], low)
                found = jnp.where(high == h, part, found)
            line = (b * blocks + c) * slab
            out[line : line + slab, :] = jnp.sum((found * gains[c]).reshape(slab, depth, LANES), axis=1)
    line = NB * width // LANES * slab
    out[line:, :] = jnp.zeros((out.shape[0] - line, LANES), F32)
    for b in range(NB):
        out[line + b : line + b + 1, :] = ancestors[b].astype(F32)


def retile_kernel(shape, prior, out):
    n, slab, depth, block_cells = shape
    for i in range(n):
        for level in range(depth):
            out[i, level] = prior[:, level, i * block_cells : (i + 1) * block_cells]


def prep_kernel(shape, owner, offsets, values, errors, ancestors, rows, steps):
    block_cells, count, scale, members = shape
    block, group = lax.axis_index("grid"), lax.axis_index("lev")
    index = lax.broadcasted_iota(jnp.int32, (8, 1), 0)
    region = jnp.full((8, 1), block, jnp.int32)
    for b in range(1, NB):
        region = jnp.where(index == b - 1, owner[b], region)
    centre = region.astype(F32) + 0.5
    rows[...] = jnp.zeros((SPARE, LANES), F32)
    row = lax.broadcasted_iota(jnp.int32, (members, members), 0)
    column = lax.broadcasted_iota(jnp.int32, (members, members), 1)
    turned = (row == column).astype(F32)
    for b in range(NB):
        cells = owner[b] * block_cells + offsets[b, pl.ds(group, 1), :]
        distance = (centre - cells.astype(F32) / block_cells) / scale
        taper = jnp.exp(-0.5 * distance * distance)
        alpha = 0.8 * (1.0 - jnp.exp(-jnp.sum(taper, axis=1, keepdims=True) / count))
        error = errors[b]
        part = (-0.5 / count) * (taper / (error * error))
        for later in range(b + 1, NB):
            i = PAIRS.index((b, later))
            rows[ALPHA + i : ALPHA + i + 1, :] = jnp.broadcast_to(alpha[later - 1 : later], (1, LANES))
            rows[LATER + i : LATER + i + 1, :count] = part[later - 1 : later]
        rows[VALUE + b : VALUE + b + 1, :count] = values[b]
        rows[OWN + b : OWN + b + 1, :count] = part[NB - 1 : NB]
        steps[b] = turned.T
        own = alpha[NB - 1 : NB]
        turned = own * lane_take(turned, ancestors[b]) + (1.0 - own) * turned
    steps[NB] = turned.T


def turn_kernel(shape, owner, rows, ahead, *refs):
    n, slab, width, count = shape
    pieces, out, slim, held = refs[:-3], refs[-3], refs[-2], refs[-1]
    members = n * slab
    block, group = lax.axis_index("grid"), lax.axis_index("lev")
    if len(pieces) == 1:
        held[...] = pieces[0][...]
    else:
        for i, piece in enumerate(pieces):
            held[lax.bitwise_xor(block, i)] = piece[...]
    common = width // NB * (NB - 1)
    for i in range(width // LANES):
        value = held[:, i * slab : (i + 1) * slab, :].reshape(members, LANES).T
        out[i * LANES : (i + 1) * LANES, :] = value
        if (i + 1) * LANES <= common:
            slim[i * LANES : (i + 1) * LANES, :] = value
    for i in range(2):
        start = pl.multiple_of(common + lax.bitwise_xor(group, 2 + i) * count, count)
        slim[common + i * count : common + (i + 1) * count, :] = out[pl.ds(start, count), :]
    low = common + 2 * count
    out[width:, :] = rows[...]
    slim[low:, :] = rows[...]
    line = width // LANES * slab
    for i, (e, b) in enumerate(PAIRS):
        value = held[owner[b], line + e : line + e + 1, :]
        out[width + PARENT + i : width + PARENT + i + 1, :] = value
        slim[low + PARENT + i : low + PARENT + i + 1, :] = value


def mix_kernel(shape, steps, pull, fields, *refs):
    n, slab, depth, block_cells = shape
    outs, held = refs[:-1], refs[-1]
    members = n * slab
    held[...] = (steps[NB] + pull[0:1, :]).reshape(n, slab, members)
    block = lax.axis_index("grid")
    if len(outs) == 1:
        blend = held[...].reshape(members, members)
    else:
        blend = jnp.concatenate([held[lax.bitwise_xor(block, i)] for i in range(n)], axis=0)
    for level in range(depth):
        value = high_dot(blend, fields[:, level].reshape(members, block_cells)).reshape(n, slab, block_cells)
        if len(outs) == 1:
            outs[0][:, level] = value
        else:
            for out, part in zip(outs, PARTS):
                for i, distance in enumerate(part):
                    out[i, level] = value[distance]


def chain_kernel(shape, own, near, far, cross, steps, out):
    members, groups, count = shape
    width = groups * count
    group = lax.axis_index("lev")
    sources = [own, near, far, cross]
    bases = [NB * width, NB * width, (NB - 1) * width + 2 * count, (NB - 1) * width + 2 * count]
    columns = [source[base : base + SPARE, :].T for source, base in zip(sources, bases)]
    parents, alphas = [], []
    for source, base in zip(sources, bases):
        parents.append(source[base + PARENT : base + PARENT + 8, :].astype(jnp.int32))
        alphas.append(source[base + ALPHA : base + ALPHA + 6, :])
    tilts = {}
    pulled = []
    for b in range(NB):
        kinds = [(q, later) for q in range(groups) for later in range(b + 1, NB)] + [(0, None)]
        height = -(-len(kinds) // 8) * 8
        index = lax.broadcasted_iota(jnp.int32, (height, members), 0)
        logs = jnp.zeros((height, members), F32)
        for q in range(groups if b < NB - 1 else 1):
            start = pl.multiple_of(b * width + lax.bitwise_xor(group, q) * count, count)
            total = jnp.zeros((count, members), F32)
            tilted = jnp.zeros((count, members), F32)
            for p, source in enumerate(sources):
                if b == NB - 1 and p > 1:
                    value = source[b * width + (p - 2) * count : b * width + (p - 1) * count, :]
                else:
                    value = source[pl.ds(start, count), :]
                for e in range(b):
                    i = PAIRS.index((e, b))
                    tilted = tilted + value * tilts[e, p, b]
                    alpha = alphas[p][i : i + 1]
                    moved = lane_take(value, parents[p][i : i + 1])
                    value = alpha * moved + (1.0 - alpha) * value
                total = total + value
            if b > 0:
                total = total + jnp.sum(tilted, axis=1, keepdims=True)
            miss = columns[q][:count, VALUE + b : VALUE + b + 1] - total
            square = miss * miss
            for row, (owner_group, later) in enumerate(kinds):
                if owner_group != q:
                    continue
                at = OWN + b if later is None else LATER + PAIRS.index((b, later))
                log = jnp.sum(columns[q][:count, at : at + 1] * square, axis=0, keepdims=True)
                logs = jnp.where(index == row, log, logs)
        expo = jnp.exp(logs - jnp.max(logs, axis=1, keepdims=True))
        tilt = expo / jnp.sum(expo, axis=1, keepdims=True) - 1.0 / members
        for row, (q, later) in enumerate(kinds):
            if later is None:
                pulled.append(tilt[row : row + 1])
            else:
                tilts[b, q, later] = tilt[row : row + 1]
    pull = jnp.zeros((8, members), F32)
    for b in range(NB):
        pull = pull + high_dot(jnp.broadcast_to(pulled[b], (8, members)), steps[b])
    out[...] = pull


def final_kernel(shape, arrived, out):
    n, slab, depth, block_cells = shape
    for i in range(n):
        for level in range(depth):
            out[:, level, i * block_cells : (i + 1) * block_cells] = arrived[i, level]


def place_kernel(shape, places, skip, *refs):
    slab, depth, block_cells = shape
    pieces, out, held, done = refs[skip:-3], refs[-3], refs[-2], refs[-1]
    block = lax.axis_index("grid")
    copies = []
    for k, (i, j, distance) in enumerate(places):
        for level in range(depth):
            held[k, :, level, :] = pieces[i][j, level]
        start = pl.multiple_of(lax.bitwise_xor(block, distance) * block_cells, LANES)
        copies.append(pltpu.make_async_copy(held.at[k], out.at[:, :, pl.ds(start, block_cells)], done.at[k]))
        copies[-1].start()
    for copy in copies:
        copy.wait()


def place(shape, whole, places, pieces, before=None, moved=0):
    slab, depth, block_cells = shape
    given = [] if before is None else [before]
    return call(
        functools.partial(place_kernel, shape, places, len(given)),
        whole,
        [PLACE] * len(given) + [VMEM] * len(pieces),
        scratch=[
            pltpu.VMEM((len(places), slab, depth, block_cells), F32),
            pltpu.SemaphoreType.DMA((len(places),)),
        ],
        moved=moved,
        out_specs=PLACE,
        aliases={0: 0} if given else {},
    )(*given, *pieces)


def hop(value, distance, n):
    return lax.ppermute(value, "grid", [(j, j ^ distance) for j in range(n)])


def gather_pieces(piece, n):
    if n != 8:
        return [lax.all_to_all(jnp.broadcast_to(piece[None], (n,) + piece.shape), "grid", 0, 0, tiled=True)]
    pieces = {0: piece}
    for i in (4, 2, 6, 7, 1):
        pieces[i] = hop(piece, i, n)
    for i in (4, 2):
        pieces[i + 1] = hop(pieces[i], 1, n)
    return [pieces[i] for i in range(n)]


def exchange_parts(parts, shape, whole, n):
    far = [parts[0]] + [hop(part, distances[0], n) for part, distances in zip(parts[1:5], PARTS[1:5])]
    near = hop(parts[5], PARTS[5][0], n)
    beside, onward = hop(parts[6], 1, n), hop(near[1:], 1, n)
    out = place(shape, whole, [(i, 0, PARTS[i][0]) for i in range(5)], far, moved=10**6)
    return place(shape, whole, [(0, 0, 2), (1, 0, 3), (2, 0, 1)], [near, onward, beside], out, moved=10**6)


def body(prior, channel_weights, obs_owner, obs_offset, obs_value, obs_error, ancestors):
    n, lev = lax.axis_size("grid"), lax.axis_size("lev")
    slab, depth, cells = prior.shape
    members = slab * n
    block_cells = cells // n
    groups = channel_weights.shape[1]
    count = obs_offset.shape[2]
    width = NB * groups * count
    scale = n / 2.0
    shape = jax.ShapeDtypeStruct
    parents = ancestors[:, 0]
    tall = width // LANES * slab + 8

    piece = call(
        functools.partial(pick_kernel, (slab, depth, block_cells, groups, count)),
        shape((tall, LANES), F32),
        [PLACE] * 5,
        scratch=[
            pltpu.SMEM(obs_owner.shape, jnp.int32),
            pltpu.VMEM(channel_weights.shape, F32),
            pltpu.VMEM(obs_offset.shape, jnp.int32),
            pltpu.VMEM(parents.shape, jnp.int32),
            pltpu.VMEM(prior.shape, F32),
            pltpu.SemaphoreType.DMA((5,)),
        ],
        moved=10**6,
        limit=None,
    )(obs_owner, channel_weights, obs_offset, parents, prior)
    pieces = gather_pieces(piece, n)
    send = call(
        functools.partial(retile_kernel, (n, slab, depth, block_cells)),
        shape((n, depth, slab, block_cells), F32),
        [VMEM],
        moved=10**6,
    )(prior)
    fields = lax.all_to_all(send, "grid", 0, 0, tiled=True)

    rows, steps = call(
        functools.partial(prep_kernel, (block_cells, count, scale, members)),
        [shape((SPARE, LANES), F32), shape((NB + 1, members, members), F32)],
        [SMEM, VMEM, VMEM, VMEM, VMEM],
        moved=10**6,
    )(obs_owner, obs_offset, obs_value, obs_error, parents)

    slim_height = (NB - 1) * groups * count + 2 * count + SPARE
    own, slim = call(
        functools.partial(turn_kernel, (n, slab, width, count)),
        [shape((width + SPARE, members), F32), shape((slim_height, members), F32)],
        [SMEM, VMEM, PLACE] + [VMEM] * len(pieces),
        scratch=[pltpu.VMEM((n, tall, LANES), F32)],
        moved=10**6,
    )(obs_owner, rows, send, *pieces)
    far = lax.ppermute(slim, "lev", [(j, j ^ 2) for j in range(lev)])
    near = lax.ppermute(own, "lev", [(j, j ^ 1) for j in range(lev)])
    cross = lax.ppermute(far, "lev", [(j, j ^ 1) for j in range(lev)])

    pull = call(
        functools.partial(chain_kernel, (members, groups, count)),
        shape((8, members), F32),
        [VMEM] * 5,
        moved=10**5,
    )(own, near, far, cross, steps)

    if n == 8:
        layout = [shape((len(part), depth, slab, block_cells), F32) for part in PARTS]
    else:
        layout = [shape((n, depth, slab, block_cells), F32)]
    send = call(
        functools.partial(mix_kernel, (n, slab, depth, block_cells)),
        layout,
        [VMEM] * 3,
        scratch=[pltpu.VMEM((n, slab, members), F32)],
        flops=10**8,
        moved=10**6,
    )(steps, pull, fields)
    whole = shape((slab, depth, cells), F32)
    if n == 8:
        return exchange_parts(send, (slab, depth, block_cells), whole, n)
    moved = lax.all_to_all(send[0], "grid", 0, 0, tiled=True)
    return call(functools.partial(final_kernel, (n, slab, depth, block_cells)), whole, [VMEM], moved=10**6)(moved)


def solution(mesh):
    in_specs = (
        P("grid", "lev", None),
        P("lev", None),
        P(),
        P(),
        P(None, "lev", None),
        P(None, "lev", None),
        P(None, "lev", "grid", None),
    )
    out_specs = P("grid", "lev", None)
    return jax.shard_map(body, mesh=mesh, in_specs=in_specs, out_specs=out_specs, check_vma=False)
```
